32 devices in a mesh: groups: 2 (over x), seq: 16 (over z, y, core).
Axes of the slice: x: 2, y: 2, z: 4, core: 2. Of those that a mesh axis runs over, the one named last changes fastest.
Arguments:
- clip: bfloat16 [16, 32, 32, 128], P('groups', 'seq'), parts along dimension 0, may hold values from -6 to 6
- frame_counts: int32 [6], P('groups'), parts along dimension 0, may hold values from 1 to 4, 8 in all
- conv_first: bfloat16 [3, 3, 3, 128, 128], replicated, may hold values from -0.109375 to 0.109375
- conv_second: bfloat16 [3, 3, 3, 128, 128], replicated, may hold values from -0.109375 to 0.109375
- patch_weight: bfloat16 [512, 1152], replicated, may hold values from -0.25 to 0.25
- qkv_weight: bfloat16 [1152, 3456], replicated, may hold values from -1 to 1
- query_gain: float32 [72], replicated, may hold values from 1.4 to 4
- key_gain: float32 [72], replicated, may hold values from 1.4 to 4
- out_weight: bfloat16 [1152, 1152], P('seq'), may hold values from -0.1875 to 0.1875
- window_lengths: int32 [2, 3], P('groups'), parts along dimension 0, may hold values from 1 to 1024, 2048 in all within a row
Outputs:
- attended: bfloat16 [4096, 1152], P(('groups', 'seq')), parts along dimension 0
The draws below stay inside these ranges and needn't reach their ends.
There are 2 independent parts, one for each index of `groups`. The reference program is written for one: setup_inputs(seed, part) draws one part's arguments, and reference() takes and returns one part's arrays. A program takes and returns all parts, laid end to end along the dimension named above; an argument that names none is the same for every part. Nothing has to cross between parts.
Inputs may be any that keep to these rules, and one draw needn't show every extreme that they name: `frame_counts`: the clips' frame counts sum to 8; one clip has exactly 4. `window_lengths`: each row sums to 2048; in each row one window has exactly 1024 tokens.
All inputs are finite; a program needn't handle non-finite values.
Results may differ from the reference program's by a relative error of at most 0.039.
Values may be sent and summed in bfloat16 or wider, within the bound.
No kernel may reach another device: no remote copies, remote signals or barrier semaphores. Data moves between devices by JAX's collectives and lax.ppermute only.
A program may use at most 64 MiB of HBM per device.

```python
import math
import jax
import jax.numpy as jnp
import numpy as np
from jax import lax

CH = 128
D = 1152
HEADS = 16
FRAMES = 8
ROWS_DEV = 2
COLS = 32
CLIPS = 3
NWIN = 3
SPAN = 2048
WGROUPS = 1
HEIGHT = 32
N_SEQ = 16


def draw_qkv_weight(key, part):
    key = jax.random.fold_in(key, 11)
    first_key, second_key, third_key = jax.random.split(key, 3)
    query_part = jnp.clip(jax.random.normal(first_key, (D, D), jnp.float32), -6.0, 6.0) / D ** 0.5
    noise_part = jnp.clip(jax.random.normal(second_key, (D, D), jnp.float32), -6.0, 6.0) / D ** 0.5
    value_part = jnp.clip(jax.random.normal(third_key, (D, D), jnp.float32), -6.0, 6.0) / D ** 0.5
    key_part = noise_part
    return jnp.concatenate([query_part, key_part, value_part], axis=1).astype(jnp.bfloat16)


def draw_query_gain(key, part):
    key = jax.random.fold_in(key, 21)
    return jax.random.uniform(key, (D // HEADS,), jnp.float32, 1.4, 2.2)


def draw_key_gain(key, part):
    key = jax.random.fold_in(key, 22)
    return jax.random.uniform(key, (D // HEADS,), jnp.float32, 1.4, 2.2)


def block_scale(own_key, dims, cuts, least, largest):
    loudness = 1.0
    for axis_at, blocks in cuts:
        steps = jax.random.uniform(jax.random.fold_in(jax.random.fold_in(own_key, 6), axis_at), (blocks,), jnp.float32, least / len(cuts), largest / len(cuts))
        loudness = loudness * jnp.repeat(jnp.exp(steps), dims[axis_at] // blocks).reshape((-1,) + (1,) * (len(dims) - 1 - axis_at))
    return loudness


def profile(count, total, most, lean):
    portions = [(1 << 20) // math.isqrt(standing ** lean) + 1 for standing in range(2, count + 1)]
    surplus, counts = total - most - (count - 1), [1] * (count - 1)
    while surplus > 0:
        movable = [i for i in range(count - 1) if counts[i] < most]
        whole, left = sum([portions[i] for i in movable]), surplus
        for i in movable:
            extra = min(most - counts[i], max(1, left * portions[i] // whole), surplus)
            counts[i] = counts[i] + extra
            surplus = surplus - extra
    return np.array([most] + counts)


def ragged_sizes(rng, number_of, total, bound, skew):
    if number_of == 2:
        one = jax.random.randint(rng, (), max(1, total - bound), min(bound, total - 1) + 1)
        return jnp.stack([one, total - one])
    sizes = jnp.asarray(profile(number_of, total, bound, skew), jnp.int32)
    couples = (number_of - 1) // 2
    source_of, taker = sizes[1:1 + 2 * couples:2], sizes[2:2 + 2 * couples:2]
    margin = jnp.minimum(source_of - 1, bound - taker)
    moved = jax.random.randint(jax.random.fold_in(rng, 1), (couples,), 0, 1 << 20) % (margin + 1)
    sizes = sizes.at[1:1 + 2 * couples:2].set(source_of - moved).at[2:2 + 2 * couples:2].set(taker + moved)
    return sizes[jax.random.permutation(jax.random.fold_in(rng, 2), number_of)]


def normal_values(own_key, shape, deviation, most, pieces=(), kind=jnp.bfloat16):
    result = deviation * jax.random.normal(own_key, shape, jnp.float32)
    if pieces:
        result = result * block_scale(own_key, shape, pieces, -0.22, 0.18)
    return jnp.clip(result, -most, most).astype(kind)


def setup_inputs(seed: int = 0, part: int = 0) -> dict:
    seeds = jax.random.split(jax.random.key(seed), 11)
    part_keys = jax.random.split(jax.random.fold_in(seeds[10], part), 11)
    clip = normal_values(part_keys[0], (FRAMES, HEIGHT, COLS, CH), 1.0, 6.0, ((1, 16),))
    frame_counts = ragged_sizes(part_keys[1], CLIPS, FRAMES, FRAMES // 2, 1).astype(jnp.int32)
    conv_first = normal_values(seeds[2], (3, 3, 3, CH, CH), (27 * CH) ** -0.5, 0.109375)
    conv_second = normal_values(seeds[3], (3, 3, 3, CH, CH), (27 * CH) ** -0.5, 0.109375)
    patch_weight = normal_values(seeds[4], (4 * CH, D), (4 * CH) ** -0.5, 0.25)
    qkv_weight = draw_qkv_weight(jax.random.fold_in(seeds[10], 71), part)
    query_gain = draw_query_gain(jax.random.fold_in(seeds[10], 71), part)
    key_gain = draw_key_gain(jax.random.fold_in(seeds[10], 71), part)
    out_weight = normal_values(seeds[8], (D, D), D ** -0.5, 0.1875, ((0, 16),))
    window_lengths = jax.vmap(lambda own: ragged_sizes(own, NWIN, SPAN, SPAN // 2, 1))(jax.random.split(part_keys[9], WGROUPS)).reshape((WGROUPS, NWIN)).astype(jnp.int32)
    return dict(clip=clip, frame_counts=frame_counts, conv_first=conv_first, conv_second=conv_second, patch_weight=patch_weight, qkv_weight=qkv_weight, query_gain=query_gain, key_gain=key_gain, out_weight=out_weight, window_lengths=window_lengths)


def frame_weights(frame_counts, frames):
    position = jnp.arange(frames, dtype=jnp.int32)
    clip_ends = jnp.cumsum(frame_counts).astype(jnp.int32)

    def clip_of(index):
        return lax.optimization_barrier(jnp.sum((index[:, None] >= clip_ends[None, :]).astype(jnp.int32), axis=1))
    own_clip = clip_of(position)
    columns = []
    for offset in (-1, 0, 1):
        neighbor = position + offset
        inside = (neighbor >= 0) & (neighbor < frames)
        same_clip = clip_of(jnp.clip(neighbor, 0, frames - 1)) == own_clip
        columns.append((inside & same_clip).astype(jnp.float32))
    return jnp.stack(columns, axis=1)

def convolve(activation, kernel, tap_weights):
    source = activation.astype(jnp.float32)
    empty_frame = jnp.zeros_like(source[:1])
    shifted = (jnp.concatenate([empty_frame, source[:-1]], 0), source, jnp.concatenate([source[1:], empty_frame], 0))
    summed = jnp.zeros(source.shape[:3] + (kernel.shape[-1],), jnp.float32)
    for offset in range(3):
        response = lax.conv_general_dilated(shifted[offset], kernel[offset].astype(jnp.float32), (1, 1), ((1, 1), (1, 1)), dimension_numbers=('NHWC', 'HWIO', 'NHWC'), precision=lax.Precision.HIGHEST)
        summed = summed + tap_weights[:, offset][:, None, None, None] * response
    return summed

def rms_scale(part, gain):
    factor = lax.rsqrt(lax.optimization_barrier(jnp.mean(part * part, axis=-1, keepdims=True)) + 1e-06)
    return (part * factor * gain.astype(jnp.float32)).astype(jnp.bfloat16)

def reference(clip, frame_counts, conv_first, conv_second, patch_weight, qkv_weight, query_gain, key_gain, out_weight, window_lengths):
    frames, height, tile_cols, channels = clip.shape
    head_dim = D // HEADS
    score_scale = 1.0 / math.sqrt(head_dim)
    tap_weights = frame_weights(frame_counts, frames)
    first_in = jax.nn.silu(clip.astype(jnp.float32)).astype(jnp.bfloat16)
    hidden_one = convolve(first_in, conv_first, tap_weights).astype(jnp.bfloat16)
    second_in = jax.nn.silu(hidden_one.astype(jnp.float32)).astype(jnp.bfloat16)
    latent = (clip.astype(jnp.float32) + convolve(second_in, conv_second, tap_weights)).astype(jnp.bfloat16)
    patches = latent.reshape(frames, height // 2, 2, tile_cols // 2, 2, channels).transpose(0, 1, 3, 2, 4, 5).reshape(-1, 4 * channels)
    embedded = jnp.dot(patches, patch_weight, preferred_element_type=jnp.float32).astype(jnp.bfloat16)
    group_tokens = embedded.reshape(-1, SPAN, D)

    def attend_group(inputs):
        tokens_group, lengths = inputs
        values_f = tokens_group.astype(jnp.float32)
        row_mean = lax.optimization_barrier(jnp.mean(values_f, axis=-1, keepdims=True))
        centered = values_f - row_mean
        variance = lax.optimization_barrier(jnp.mean(centered * centered, axis=-1, keepdims=True))
        normed = (centered / jnp.sqrt(variance + 1e-06)).astype(jnp.bfloat16)
        projected = jnp.dot(normed, qkv_weight, preferred_element_type=jnp.float32).reshape(SPAN, 3, HEADS, head_dim)
        queries = rms_scale(projected[:, 0], query_gain).transpose(1, 0, 2)
        keys_all = rms_scale(projected[:, 1], key_gain).transpose(1, 0, 2)
        values_all = projected[:, 2].astype(jnp.bfloat16).transpose(1, 0, 2)
        window_ends = jnp.cumsum(lengths).astype(jnp.int32)
        token_index = jnp.arange(SPAN, dtype=jnp.int32)
        segment = lax.optimization_barrier(jnp.sum((token_index[:, None] >= window_ends[None, :]).astype(jnp.int32), axis=1))
        allowed = segment[:, None] == segment[None, :]

        def one_head(triple):
            query_rows, key_rows, value_rows = triple
            scores = jnp.dot(query_rows, key_rows.T, preferred_element_type=jnp.float32) * score_scale
            scores = jnp.where(allowed, scores, -1e+30)
            row_peak = lax.optimization_barrier(jnp.max(scores, axis=-1, keepdims=True))
            weights = jnp.exp(scores - row_peak)
            row_mass = lax.optimization_barrier(jnp.sum(weights, axis=-1, keepdims=True))
            mixed = jnp.dot(weights.astype(jnp.bfloat16), value_rows, preferred_element_type=jnp.float32) / row_mass
            return mixed.astype(jnp.bfloat16)
        heads_result = lax.map(one_head, (queries, keys_all, values_all))
        merged = heads_result.transpose(1, 0, 2).reshape(SPAN, D)
        return jnp.dot(merged, out_weight, preferred_element_type=jnp.float32).astype(jnp.bfloat16)
    attended = lax.map(attend_group, (group_tokens, window_lengths))
    attended = attended.reshape(frames, N_SEQ, ROWS_DEV // 2, tile_cols // 2, D).transpose(1, 0, 2, 3, 4).reshape(-1, D)
    return attended
```

```python
import functools
import math

import jax
import jax.numpy as jnp
from jax import lax
from jax.experimental import pallas as pl
from jax.experimental.pallas import tpu as pltpu
from jax.sharding import PartitionSpec as P

D = 1152
HEADS = 16


def extended(array, sides, width):
    for axis, dim in sides:
        size, length = (lax.axis_size(axis), array.shape[dim])
        up = [(i, (i + 1) % size) for i in range(size - 1)]
        down = [(j, i) for i, j in up]
        last = lax.slice_in_dim(array, length - width, length, axis=dim)
        first = lax.slice_in_dim(array, 0, width, axis=dim)
        before = lax.ppermute(last, axis, up)
        after = lax.ppermute(first, axis, down)
        array = jnp.concatenate([before, array, after], axis=dim)
    return array


def frame_weights(frame_counts, frames):
    position = jnp.arange(frames, dtype=jnp.int32)
    clip_ends = jnp.cumsum(frame_counts)

    def clip_of(index):
        return jnp.sum((index[:, None] >= clip_ends[None, :]).astype(jnp.int32), axis=1)

    own_clip = clip_of(position)
    columns = []
    for offset in (-1, 0, 1):
        neighbor = position + offset
        inside = (neighbor >= 0) & (neighbor < frames)
        same_clip = clip_of(jnp.clip(neighbor, 0, frames - 1)) == own_clip
        columns.append((inside & same_clip).astype(jnp.float32))
    return jnp.stack(columns, axis=1)


def convolve_rows(activation, kernel, tap_weights):
    empty_frame = jnp.zeros_like(activation[:1])
    shifted = (
        jnp.concatenate([empty_frame, activation[:-1]], 0),
        activation,
        jnp.concatenate([activation[1:], empty_frame], 0),
    )
    summed = None
    for offset in range(3):
        response = lax.conv_general_dilated(
            shifted[offset],
            kernel[offset],
            (1, 1),
            ((0, 0), (1, 1)),
            dimension_numbers=("NHWC", "HWIO", "NHWC"),
            preferred_element_type=jnp.float32,
        )
        tap_term = tap_weights[:, offset][:, None, None, None] * response
        summed = tap_term if offset == 0 else summed + tap_term
    return summed


def rms_scale(part, gain):
    factor = lax.rsqrt(jnp.mean(part * part, axis=-1, keepdims=True) + 1e-06)
    return (part * factor * gain).astype(jnp.bfloat16)


def general_shards(
    clip,
    frame_counts,
    conv_first,
    conv_second,
    patch_weight,
    qkv_weight,
    query_gain,
    key_gain,
    out_weight,
    window_lengths,
):
    frames, tile_rows, tile_cols, channels = clip.shape
    devices = lax.axis_size("seq")
    position = lax.axis_index("seq")
    head_dim = D // HEADS
    score_scale = 1.0 / math.sqrt(head_dim)
    tap_weights = frame_weights(frame_counts, frames)
    source = clip.astype(jnp.float32)
    padded_clip = extended(clip, (("seq", 1),), 2)
    first_in = jax.nn.silu(padded_clip.astype(jnp.float32)).astype(jnp.bfloat16)
    hidden_wide = convolve_rows(first_in, conv_first, tap_weights)
    global_row = position * tile_rows - 1 + jnp.arange(tile_rows + 2, dtype=jnp.int32)
    inside = ((global_row >= 0) & (global_row < tile_rows * devices)).astype(jnp.float32)
    hidden_one = (hidden_wide * inside[None, :, None, None]).astype(jnp.bfloat16)
    padded_second = jax.nn.silu(hidden_one.astype(jnp.float32)).astype(jnp.bfloat16)
    latent = (source + convolve_rows(padded_second, conv_second, tap_weights)).astype(jnp.bfloat16)
    token_rows = tile_rows // 2
    token_cols = tile_cols // 2
    patches = (
        latent.reshape(frames, token_rows, 2, token_cols, 2, channels)
        .transpose(0, 1, 3, 2, 4, 5)
        .reshape(-1, 4 * channels)
    )
    tok_count = patches.shape[0]
    embedded = jnp.dot(patches, patch_weight, preferred_element_type=jnp.float32).astype(
        jnp.bfloat16
    )
    values_f = embedded.astype(jnp.float32)
    row_mean = jnp.mean(values_f, axis=-1, keepdims=True)
    centered = values_f - row_mean
    variance = jnp.mean(centered * centered, axis=-1, keepdims=True)
    normed = (centered / jnp.sqrt(variance + 1e-06)).astype(jnp.bfloat16)
    projected = jnp.dot(normed, qkv_weight, preferred_element_type=jnp.float32).reshape(
        tok_count, 3, HEADS, head_dim
    )
    stacked = jnp.stack(
        [
            rms_scale(projected[:, 0], query_gain),
            rms_scale(projected[:, 1], key_gain),
            projected[:, 2].astype(jnp.bfloat16),
        ],
        axis=1,
    )
    groups = devices // HEADS
    frame_share = frames // groups
    local_share = tok_count // groups
    span_rows = devices * local_share
    outgoing = (
        stacked.reshape(groups, local_share, 3, HEADS, head_dim)
        .transpose(0, 3, 1, 2, 4)
        .reshape(devices, local_share, 3 * head_dim)
    )
    incoming = lax.all_to_all(outgoing, "seq", split_axis=0, concat_axis=0, tiled=True)
    arranged = (
        incoming.reshape(devices, frame_share, token_rows * token_cols, 3, head_dim)
        .transpose(3, 1, 0, 2, 4)
        .reshape(3, span_rows, head_dim)
    )
    my_group = position // HEADS
    lengths = lax.dynamic_index_in_dim(window_lengths, my_group, 0, keepdims=False)
    window_ends = jnp.cumsum(lengths)
    token_index = jnp.arange(span_rows, dtype=jnp.int32)
    segment = jnp.sum((token_index[:, None] >= window_ends[None, :]).astype(jnp.int32), axis=1)
    key_rows = arranged[1]
    value_rows = arranged[2]
    block_rows = min(512, span_rows)
    block_count = span_rows // block_rows

    def attend_block(inputs):
        query_block, segment_block = inputs
        scores = jnp.dot(query_block, key_rows.T, preferred_element_type=jnp.float32) * score_scale
        allowed = segment_block[:, None] == segment[None, :]
        scores = jnp.where(allowed, scores, -1e30)
        row_peak = jnp.max(scores, axis=-1, keepdims=True)
        weights = jnp.exp(scores - row_peak)
        row_mass = jnp.sum(weights, axis=-1, keepdims=True)
        mixed = (
            jnp.dot(weights.astype(jnp.bfloat16), value_rows, preferred_element_type=jnp.float32)
            / row_mass
        )
        return mixed.astype(jnp.bfloat16)

    mixed_rows = lax.map(
        attend_block,
        (
            arranged[0].reshape(block_count, block_rows, head_dim),
            segment.reshape(block_count, block_rows),
        ),
    ).reshape(span_rows, head_dim)
    outgoing_back = (
        mixed_rows.reshape(frame_share, devices, token_rows * token_cols, head_dim)
        .transpose(1, 0, 2, 3)
        .reshape(devices, local_share, head_dim)
    )
    returned = lax.all_to_all(outgoing_back, "seq", split_axis=0, concat_axis=0, tiled=True)
    merged = (
        returned.reshape(groups, HEADS, local_share, head_dim)
        .transpose(0, 2, 1, 3)
        .reshape(tok_count, D)
    )
    projected_out = jnp.dot(
        merged,
        lax.all_gather(out_weight, "seq", axis=0, tiled=True),
        preferred_element_type=jnp.float32,
    )
    return projected_out.astype(jnp.bfloat16)


HD = D // HEADS
SLOT = 80
MASK = 1024.0
F32 = jnp.float32
BF16 = jnp.bfloat16
VMEM = pl.BlockSpec(memory_space=pltpu.VMEM)
SMEM = pl.BlockSpec(memory_space=pltpu.SMEM)
NT = (((1,), (1,)), ((), ()))


def params(mib=40):
    return pltpu.CompilerParams(vmem_limit_bytes=mib << 20)


def silu(v):
    return v / (1.0 + jnp.exp(-v))


def long_window(lengths):
    first, second = lengths[0, 0], lengths[0, 1]
    half = 1024
    start = jnp.where(first == half, 0, jnp.where(second == half, first, first + second))
    bound = jnp.where(first == half, half + second, first)
    return start, bound


def fold_kernel(patch_ref, qkv_ref, folded_ref):
    patch = patch_ref[...].astype(F32)
    centered = (patch - jnp.mean(patch, axis=1, keepdims=True)).astype(BF16)
    product = jnp.dot(centered, qkv_ref[...], preferred_element_type=F32)
    folded_ref[...] = product.T.astype(BF16)


def fold(patch_weight, qkv_weight):
    inner = patch_weight.shape[0]
    return pl.pallas_call(
        fold_kernel,
        grid=(3,),
        out_shape=jax.ShapeDtypeStruct((3 * D, inner), BF16),
        in_specs=[
            pl.BlockSpec((inner, D), lambda i: (0, 0)),
            pl.BlockSpec((D, D), lambda i: (0, i)),
        ],
        out_specs=pl.BlockSpec((D, inner), lambda i: (i, 0)),
        compiler_params=params(),
        name="fold",
        cost_estimate=pl.CostEstimate(flops=2 * inner * D * 3 * D, bytes_accessed=12 << 20, transcendentals=0),
    )(patch_weight, qkv_weight)


def frame_taps(counts_ref, frames):
    def clip_of(frame):
        end = 0
        index = 0
        for c in range(counts_ref.shape[0]):
            end = end + counts_ref[c]
            index = index + jnp.where(frame >= end, 1, 0)
        return index

    own = [clip_of(f) for f in range(frames)]
    joined = [jnp.where(own[f] == own[f + 1], 1.0, 0.0) for f in range(frames - 1)]
    return [0.0] + joined, joined + [0.0]


def conv_kernel(
    counts_ref, lengths_ref, own_ref, before_ref, after_ref, first_ref, second_ref, patch_ref,
    keep_ref, send_ref, grid_one, grid_two, pairs_one, pairs_two, pixels,
):
    frames, _, cols, ch = own_ref.shape
    wide = 12 * ch
    position = lax.axis_index("seq")
    before_tap, after_tap = frame_taps(counts_ref, frames)
    for weights, pairs in ((first_ref, pairs_one), (second_ref, pairs_two)):
        for o in range(3):
            for four in range(4):
                for out_row in range(2):
                    for j in range(3):
                        rows = pl.ds((four * 3 + j) * ch, ch)
                        columns = pl.ds(out_row * ch, ch)
                        tap = four - out_row
                        if 0 <= tap < 3:
                            pairs[o, rows, columns] = weights[o, tap, j]
                        else:
                            pairs[o, rows, columns] = jnp.zeros((ch, ch), BF16)
    column = lax.broadcasted_iota(jnp.int32, (frames, cols, ch), 1)

    def shifted(row):
        left = jnp.where(column == 0, 0.0, pltpu.roll(row, 1, 1))
        right = jnp.where(column == cols - 1, 0.0, pltpu.roll(row, cols - 1, 1))
        return [part.astype(BF16) for part in (left, row, right)]

    blank = jnp.zeros((cols, wide), BF16)
    for g in range(2):
        grid_one[g, 0] = blank
        grid_one[g, frames + 1] = blank
    grid_two[0] = blank
    grid_two[frames + 1] = blank
    sources = [before_ref, before_ref, own_ref, own_ref, after_ref, after_ref]
    for r in range(6):
        row = silu(sources[r][:, r % 2].astype(F32))
        parts = shifted(row)
        for g in range(2):
            four = r - 2 * g
            if 0 <= four < 4:
                for j in range(3):
                    grid_one[g, 1 : frames + 1, :, (four * 3 + j) * ch : (four * 3 + j + 1) * ch] = parts[j]

    def summed(terms):
        rows = []
        for f in range(frames):
            total = terms[1][f]
            if f > 0:
                total = total + before_tap[f] * terms[0][f]
            if f < frames - 1:
                total = total + after_tap[f] * terms[2][f]
            rows.append(total)
        return jnp.stack(rows)

    for g in range(2):
        terms = []
        for o in range(3):
            left = grid_one[g, o : o + frames].reshape(frames * cols, wide)
            terms.append(
                jnp.dot(left, pairs_one[o], preferred_element_type=F32).reshape(frames, cols, 2 * ch)
            )
        hidden = summed(terms)
        for out_row in range(2):
            four = 2 * g + out_row
            row = hidden[:, :, out_row * ch : (out_row + 1) * ch]
            if four == 0:
                row = row * jnp.where(position == 0, 0.0, 1.0)
            if four == 3:
                row = row * jnp.where(position == lax.axis_size("seq") - 1, 0.0, 1.0)
            row = silu(row.astype(BF16).astype(F32))
            parts = shifted(row)
            for j in range(3):
                grid_two[1 : frames + 1, :, (four * 3 + j) * ch : (four * 3 + j + 1) * ch] = parts[j]
    terms = []
    for o in range(3):
        left = grid_two[o : o + frames].reshape(frames * cols, wide)
        terms.append(
            jnp.dot(left, pairs_two[o], preferred_element_type=F32).reshape(frames, cols, 2 * ch)
        )
    residual = summed(terms)
    for out_row in range(2):
        block = own_ref[:, out_row].astype(F32) + residual[:, :, out_row * ch : (out_row + 1) * ch]
        pixels[out_row] = block.astype(BF16).astype(F32).reshape(frames * cols, ch)
    tokens = frames * cols // 2
    patches = jnp.concatenate(
        [pixels[a, pl.ds(b, tokens, 2), :] for a in range(2) for b in range(2)], axis=1
    )
    embedded = jnp.dot(patches.astype(BF16), patch_ref[...], preferred_element_type=F32)
    centered = embedded - jnp.mean(embedded, axis=1, keepdims=True)
    variance = jnp.mean(centered * centered, axis=1, keepdims=True)
    scaled = patches * (1.0 / jnp.sqrt(variance + 1e-06))
    half = tokens // 2
    low, high = scaled[:half], scaled[half:]
    start, _ = long_window(lengths_ref)
    q_cols = cols // 2
    slot = lax.broadcasted_iota(jnp.int32, low.shape, 0)
    token = (slot // q_cols) * (lax.axis_size("seq") * q_cols) + position * q_cols + slot % q_cols
    inside = jnp.where(token >= start, 1, 0)
    mine = inside == jnp.where(position % 2 == 0, 1, 0)
    keep = jnp.where(mine, low, high).astype(BF16)
    send = jnp.where(mine, high, low).astype(BF16)
    for tile in range(4):
        keep_ref[tile * half : (tile + 1) * half] = keep[:, tile * ch : (tile + 1) * ch]
        send_ref[tile * half : (tile + 1) * half] = send[:, tile * ch : (tile + 1) * ch]


def convolve(counts, lengths, clip, before, after, conv_first, conv_second, patch_weight):
    frames, _, cols, ch = clip.shape
    tokens = frames * cols // 2
    out = jax.ShapeDtypeStruct((2 * tokens, ch), BF16)
    return pl.pallas_call(
        conv_kernel,
        out_shape=(out, out),
        in_specs=[SMEM, SMEM] + [VMEM] * 6,
        out_specs=(VMEM, VMEM),
        scratch_shapes=[
            pltpu.VMEM((2, frames + 2, cols, 12 * ch), BF16),
            pltpu.VMEM((frames + 2, cols, 12 * ch), BF16),
            pltpu.VMEM((3, 12 * ch, 2 * ch), BF16),
            pltpu.VMEM((3, 12 * ch, 2 * ch), BF16),
            pltpu.VMEM((2, frames * cols, ch), F32),
        ],
        compiler_params=params(),
        name="convolve",
        cost_estimate=pl.CostEstimate(flops=2 << 30, bytes_accessed=4 << 20, transcendentals=1 << 18),
    )(counts, lengths, clip, before, after, conv_first, conv_second, patch_weight)


def chip_at(place):
    chips = lax.axis_size("seq") // 2
    place = lax.rem(place + 2 * chips, chips)
    return jnp.where(place < chips // 2, 2 * place, 2 * (chips - 1 - place) + 1)


def ring_place():
    chips = lax.axis_size("seq") // 2
    chip = lax.axis_index("seq") // 2
    return jnp.where(chip % 2 == 0, chip // 2, chips - 1 - chip // 2)


def ring_pairs():
    size = lax.axis_size("seq")
    chips = size // 2
    order = [2 * i for i in range(chips // 2)] + [2 * i + 1 for i in reversed(range(chips // 2))]
    return [
        (2 * order[i] + core, 2 * order[(i + 1) % chips] + core) for i in range(chips) for core in range(2)
    ]


def window_sides(lengths_ref, chip, count):
    size = lax.axis_size("seq")
    core = lax.axis_index("seq") % 2
    start, bound = long_window(lengths_ref)
    lane = lax.broadcasted_iota(jnp.int32, (8, count), 1)
    half = count // 2
    slot = lane % half
    row = 2 * chip + jnp.where(lane < half, core, 1 - core)
    q_cols = 16
    token = (slot // q_cols) * (size * q_cols) + row * q_cols + slot % q_cols
    inside = jnp.where(token >= start, 1, 0)
    upper = inside != jnp.where(core == 0, 1, 0)
    token = jnp.where(upper, token + 4 * size * q_cols, token)
    return jnp.where(token < bound, 1.0, -1.0)


def block_tokens(ref, ch=128, half=64):
    second = 4 * half + 5 * SLOT
    parts = []
    for base in (0, second):
        parts.append(
            jnp.concatenate([ref[base + t * half : base + (t + 1) * half] for t in range(4)], axis=1)
        )
    return jnp.concatenate(parts, axis=0)


def half_tokens(ref, half=64):
    return jnp.concatenate([ref[t * half : (t + 1) * half] for t in range(4)], axis=1)


def normed_heads(part, gain):
    count = part.shape[1]
    heads = part.reshape(HEADS, HD, count)
    factor = lax.rsqrt(jnp.mean(heads * heads, axis=1, keepdims=True) + 1e-06)
    return heads * factor * gain[None, :, :count]


def attend(tokens, sides, folded, key_gain, queries, acc_ref):
    count = tokens.shape[0]
    both = lax.dot_general(folded, tokens, NT, preferred_element_type=F32)
    keys = normed_heads(both[:D], key_gain)
    values = both[D:].reshape(HEADS, HD, count)
    row = lax.broadcasted_iota(jnp.int32, (8, count), 0)
    key_tail = jnp.where(row == 0, sides, jnp.where(row == 1, 1.0, 0.0))
    value_tail = jnp.where(row == 0, 1.0, 0.0)
    tail_row = lax.broadcasted_iota(jnp.int32, (8, 128), 0)
    for h in range(HEADS):
        key = jnp.concatenate([keys[h], key_tail], axis=0).T.astype(BF16)
        value = jnp.concatenate([values[h], value_tail], axis=0).astype(BF16)
        scores = jnp.dot(key, queries[h], preferred_element_type=F32)
        peak = jnp.max(scores, axis=0, keepdims=True)
        weights = jnp.exp2(scores - peak).astype(BF16)
        mixed = jnp.dot(value, weights, preferred_element_type=F32)
        acc_ref[h, :HD] = mixed[:HD]
        acc_ref[h, HD:] = jnp.where(tail_row == 1, peak, mixed[HD:])


def own_kernel(lengths_ref, block_ref, folded_ref, query_gain_ref, key_gain_ref, queries_ref, acc_ref):
    tokens = block_tokens(block_ref)
    count = tokens.shape[0]
    sides = window_sides(lengths_ref, lax.axis_index("seq") // 2, count)
    part = lax.dot_general(folded_ref[:D], tokens, NT, preferred_element_type=F32)
    queries = normed_heads(part, query_gain_ref[...])
    row = lax.broadcasted_iota(jnp.int32, (8, count), 0)
    tail = jnp.where(row == 0, MASK * sides, jnp.where(row == 1, -MASK, 0.0))
    for h in range(HEADS):
        queries_ref[h] = jnp.concatenate([queries[h], tail], axis=0).astype(BF16)
    attend(tokens, sides, folded_ref[D:], key_gain_ref[...], queries_ref, acc_ref)


def step_kernel(step, lengths_ref, ahead_ref, behind_ref, folded_ref, key_gain_ref, queries_ref, acc_ref):
    place = ring_place()
    if step < 4:
        tokens = jnp.concatenate([block_tokens(ahead_ref), block_tokens(behind_ref)], axis=0)
        sides = jnp.concatenate(
            [
                window_sides(lengths_ref, chip_at(place - step), 128),
                window_sides(lengths_ref, chip_at(place + step), 128),
            ],
            axis=1,
        )
    else:
        tokens = jnp.concatenate([half_tokens(ahead_ref), half_tokens(behind_ref)], axis=0)
        sides = window_sides(lengths_ref, chip_at(place + step), 128)
    attend(tokens, sides, folded_ref[D:], key_gain_ref[...], queries_ref, acc_ref)


ACC = jax.ShapeDtypeStruct((HEADS, SLOT, 128), F32)


def cost(count):
    flops = 2 * count * 2 * D * 512 + 4 * HEADS * 128 * 128 * count
    return pl.CostEstimate(flops=2 * flops, bytes_accessed=5 << 20, transcendentals=HEADS * 128 * count)


def own_attention(lengths, block, folded, query_gain, key_gain):
    return pl.pallas_call(
        own_kernel,
        out_shape=(jax.ShapeDtypeStruct((HEADS, SLOT, 128), BF16), ACC),
        in_specs=[SMEM] + [VMEM] * 4,
        out_specs=(VMEM, VMEM),
        compiler_params=params(),
        name="own_attention",
        cost_estimate=cost(192),
    )(lengths, block, folded, query_gain, key_gain)


def step_attention(step, lengths, ahead, behind, folded, key_gain, queries):
    return pl.pallas_call(
        functools.partial(step_kernel, step),
        out_shape=ACC,
        in_specs=[SMEM] + [VMEM] * 5,
        out_specs=VMEM,
        compiler_params=params(),
        name="step_attention",
        cost_estimate=cost(256 if step < 4 else 128),
    )(lengths, ahead, behind, folded, key_gain, queries)


def out_kernel(parts, *refs):
    acc_refs = refs[:parts]
    block_refs = refs[parts:-3]
    keep_ref, send_ref, mixed_ref = refs[-3:]
    zeros = jnp.zeros((SLOT - HD, 128), F32)
    for h in range(HEADS):
        peaks = [acc[h, HD + 1 : HD + 2] for acc in acc_refs]
        peak = functools.reduce(jnp.maximum, peaks)
        total = None
        for acc, own in zip(acc_refs, peaks):
            term = acc[h] * jnp.exp2(own - peak)
            total = term if total is None else total + term
        mixed = total[:HD] / total[HD : HD + 1]
        mixed_ref[h] = jnp.concatenate([mixed, zeros], axis=0)
    place = ring_place()
    core = lax.axis_index("seq") % 2
    offsets = [0, -1, 1, -2, 2, -3, 3, 4]
    per_core = len(block_refs) // 2
    slots, tiles = [], []
    for side in range(2):
        refs_here = block_refs[side * per_core : (side + 1) * per_core]
        for index, offset in enumerate(offsets):
            head = 2 * chip_at(place + offset) + jnp.where(core == side, 0, 1)
            slots.append(mixed_ref[head])
            if index < 7:
                low, high, base = refs_here[index], refs_here[index], 256 + 5 * SLOT + 256
            else:
                low, high, base = refs_here[7], refs_here[8], 256
            tiles.append(
                [low[256 + t * SLOT : 256 + (t + 1) * SLOT] for t in range(5)]
                + [high[base + t * SLOT : base + (t + 1) * SLOT] for t in range(4)]
            )
    left = jnp.concatenate(slots, axis=0).T.astype(BF16)
    half = keep_ref.shape[0]
    for first in range(0, 9, 2):
        group = range(first, min(first + 2, 9))
        right = jnp.concatenate(
            [jnp.concatenate([block[t] for block in tiles], axis=0) for t in group], axis=1
        )
        result = jnp.dot(left, right, preferred_element_type=F32).astype(BF16)
        columns = slice(first * 128, (group[-1] + 1) * 128)
        keep_ref[:, columns] = result[:half]
        send_ref[:, columns] = result[half:]


def project_out(accs, blocks):
    out = jax.ShapeDtypeStruct((64, D), BF16)
    return pl.pallas_call(
        functools.partial(out_kernel, len(accs)),
        out_shape=(out, out),
        in_specs=[VMEM] * (len(accs) + len(blocks)),
        out_specs=(VMEM, VMEM),
        scratch_shapes=[pltpu.VMEM((HEADS, SLOT, 128), F32)],
        compiler_params=params(),
        name="project_out",
        cost_estimate=pl.CostEstimate(flops=2 * 128 * 1280 * D, bytes_accessed=4 << 20, transcendentals=0),
    )(*accs, *blocks)


def merge_kernel(lengths_ref, keep_ref, got_ref, out_ref):
    position = lax.axis_index("seq")
    keep = keep_ref[...].astype(F32)
    got = got_ref[...].astype(F32)
    start, _ = long_window(lengths_ref)
    q_cols = 16
    slot = lax.broadcasted_iota(jnp.int32, keep.shape, 0)
    token = (slot // q_cols) * (lax.axis_size("seq") * q_cols) + position * q_cols + slot % q_cols
    inside = jnp.where(token >= start, 1, 0)
    mine = inside == jnp.where(position % 2 == 0, 1, 0)
    half = keep.shape[0]
    out_ref[:half] = jnp.where(mine, keep, got).astype(BF16)
    out_ref[half:] = jnp.where(mine, got, keep).astype(BF16)


def merge(lengths, keep, got):
    return pl.pallas_call(
        merge_kernel,
        out_shape=jax.ShapeDtypeStruct((128, D), BF16),
        in_specs=[SMEM, VMEM, VMEM],
        out_specs=VMEM,
        compiler_params=params(),
        name="merge",
    )(lengths, keep, got)


def weight_tiles(out_weight):
    padded = jnp.pad(out_weight, ((0, SLOT - HD), (0, 0)))
    return padded.reshape(SLOT, 9, 128).transpose(1, 0, 2).reshape(9 * SLOT, 128)


def shards(
    clip, frame_counts, conv_first, conv_second, patch_weight, qkv_weight, query_gain, key_gain,
    out_weight, window_lengths,
):
    size = lax.axis_size("seq")
    up = [(i, i + 1) for i in range(size - 1)]
    down = [(j, i) for i, j in up]
    cores = [(i, i ^ 1) for i in range(size)]
    forward = ring_pairs()
    backward = [(j, i) for i, j in forward]

    def send(array, pairs):
        return lax.ppermute(array, "seq", pairs)

    before = send(clip, up)
    after = send(clip, down)
    score_scale = math.log2(math.e) / math.sqrt(HD)
    query_rows = jnp.broadcast_to((query_gain * score_scale)[:, None], (HD, 256))
    key_rows = jnp.broadcast_to(key_gain[:, None], (HD, 256))
    folded = fold(patch_weight, qkv_weight)
    weight = weight_tiles(out_weight)
    keep, other = convolve(
        frame_counts, window_lengths, clip, before, after, conv_first, conv_second, patch_weight
    )
    got = send(other, cores)
    cut = 256 + 5 * SLOT
    block = jnp.concatenate([keep, weight[: 5 * SLOT], got, weight[5 * SLOT :]], axis=0)
    ahead, behind = block, block
    accs, blocks = [], [block]
    for step in range(1, 4):
        ahead_next = send(ahead, forward)
        behind_next = send(behind, backward)
        if step == 1:
            queries, acc = own_attention(window_lengths, block, folded, query_rows, key_rows)
        else:
            acc = step_attention(step - 1, window_lengths, ahead, behind, folded, key_rows, queries)
        accs.append(acc)
        ahead, behind = ahead_next, behind_next
        blocks += [ahead, behind]
    ahead_last = send(ahead[:cut], forward)
    behind_last = send(behind[cut:], backward)
    accs.append(step_attention(3, window_lengths, ahead, behind, folded, key_rows, queries))
    accs.append(step_attention(4, window_lengths, ahead_last, behind_last, folded, key_rows, queries))
    blocks += [ahead_last, behind_last]
    sibling = [send(array, cores) for array in blocks]
    keep_rows, send_rows = project_out(accs, blocks + sibling)
    return merge(window_lengths, keep_rows, send(send_rows, cores))


def solution(mesh):
    own = mesh.shape["seq"] == HEADS
    return jax.shard_map(
        shards if own else general_shards,
        mesh=mesh,
        in_specs=(
            P("groups", "seq", None, None),
            P("groups"),
            P(),
            P(),
            P(),
            P(),
            P(),
            P(),
            P("seq", None),
            P("groups", None),
        ),
        out_specs=P(("groups", "seq"), None),
        check_vma=False,
    )
```

```python
import functools
import math

import jax
import jax.numpy as jnp
from jax import lax
from jax.experimental import pallas as pl
from jax.experimental.pallas import tpu as pltpu
from jax.sharding import PartitionSpec as P

D = 1152
HEADS = 16


def extended(array, sides, width):
    for axis, dim in sides:
        size, length = (lax.axis_size(axis), array.shape[dim])
        up = [(i, (i + 1) % size) for i in range(size - 1)]
        down = [(j, i) for i, j in up]
        last = lax.slice_in_dim(array, length - width, length, axis=dim)
        first = lax.slice_in_dim(array, 0, width, axis=dim)
        before = lax.ppermute(last, axis, up)
        after = lax.ppermute(first, axis, down)
        array = jnp.concatenate([before, array, after], axis=dim)
    return array


def frame_weights(frame_counts, frames):
    position = jnp.arange(frames, dtype=jnp.int32)
    clip_ends = jnp.cumsum(frame_counts)

    def clip_of(index):
        return jnp.sum((index[:, None] >= clip_ends[None, :]).astype(jnp.int32), axis=1)

    own_clip = clip_of(position)
    columns = []
    for offset in (-1, 0, 1):
        neighbor = position + offset
        inside = (neighbor >= 0) & (neighbor < frames)
        same_clip = clip_of(jnp.clip(neighbor, 0, frames - 1)) == own_clip
        columns.append((inside & same_clip).astype(jnp.float32))
    return jnp.stack(columns, axis=1)


def convolve_rows(activation, kernel, tap_weights):
    empty_frame = jnp.zeros_like(activation[:1])
    shifted = (
        jnp.concatenate([empty_frame, activation[:-1]], 0),
        activation,
        jnp.concatenate([activation[1:], empty_frame], 0),
    )
    summed = None
    for offset in range(3):
        response = lax.conv_general_dilated(
            shifted[offset],
            kernel[offset],
            (1, 1),
            ((0, 0), (1, 1)),
            dimension_numbers=("NHWC", "HWIO", "NHWC"),
            preferred_element_type=jnp.float32,
        )
        tap_term = tap_weights[:, offset][:, None, None, None] * response
        summed = tap_term if offset == 0 else summed + tap_term
    return summed


def rms_scale(part, gain):
    factor = lax.rsqrt(jnp.mean(part * part, axis=-1, keepdims=True) + 1e-06)
    return (part * factor * gain).astype(jnp.bfloat16)


def general_shards(
    clip,
    frame_counts,
    conv_first,
    conv_second,
    patch_weight,
    qkv_weight,
    query_gain,
    key_gain,
    out_weight,
    window_lengths,
):
    frames, tile_rows, tile_cols, channels = clip.shape
    devices = lax.axis_size("seq")
    position = lax.axis_index("seq")
    head_dim = D // HEADS
    score_scale = 1.0 / math.sqrt(head_dim)
    tap_weights = frame_weights(frame_counts, frames)
    source = clip.astype(jnp.float32)
    padded_clip = extended(clip, (("seq", 1),), 2)
    first_in = jax.nn.silu(padded_clip.astype(jnp.float32)).astype(jnp.bfloat16)
    hidden_wide = convolve_rows(first_in, conv_first, tap_weights)
    global_row = position * tile_rows - 1 + jnp.arange(tile_rows + 2, dtype=jnp.int32)
    inside = ((global_row >= 0) & (global_row < tile_rows * devices)).astype(jnp.float32)
    hidden_one = (hidden_wide * inside[None, :, None, None]).astype(jnp.bfloat16)
    padded_second = jax.nn.silu(hidden_one.astype(jnp.float32)).astype(jnp.bfloat16)
    latent = (source + convolve_rows(padded_second, conv_second, tap_weights)).astype(jnp.bfloat16)
    token_rows = tile_rows // 2
    token_cols = tile_cols // 2
    patches = (
        latent.reshape(frames, token_rows, 2, token_cols, 2, channels)
        .transpose(0, 1, 3, 2, 4, 5)
        .reshape(-1, 4 * channels)
    )
    tok_count = patches.shape[0]
    embedded = jnp.dot(patches, patch_weight, preferred_element_type=jnp.float32).astype(
        jnp.bfloat16
    )
    values_f = embedded.astype(jnp.float32)
    row_mean = jnp.mean(values_f, axis=-1, keepdims=True)
    centered = values_f - row_mean
    variance = jnp.mean(centered * centered, axis=-1, keepdims=True)
    normed = (centered / jnp.sqrt(variance + 1e-06)).astype(jnp.bfloat16)
    projected = jnp.dot(normed, qkv_weight, preferred_element_type=jnp.float32).reshape(
        tok_count, 3, HEADS, head_dim
    )
    stacked = jnp.stack(
        [
            rms_scale(projected[:, 0], query_gain),
            rms_scale(projected[:, 1], key_gain),
            projected[:, 2].astype(jnp.bfloat16),
        ],
        axis=1,
    )
    groups = devices // HEADS
    frame_share = frames // groups
    local_share = tok_count // groups
    span_rows = devices * local_share
    outgoing = (
        stacked.reshape(groups, local_share, 3, HEADS, head_dim)
        .transpose(0, 3, 1, 2, 4)
        .reshape(devices, local_share, 3 * head_dim)
    )
    incoming = lax.all_to_all(outgoing, "seq", split_axis=0, concat_axis=0, tiled=True)
    arranged = (
        incoming.reshape(devices, frame_share, token_rows * token_cols, 3, head_dim)
        .transpose(3, 1, 0, 2, 4)
        .reshape(3, span_rows, head_dim)
    )
    my_group = position // HEADS
    lengths = lax.dynamic_index_in_dim(window_lengths, my_group, 0, keepdims=False)
    window_ends = jnp.cumsum(lengths)
    token_index = jnp.arange(span_rows, dtype=jnp.int32)
    segment = jnp.sum((token_index[:, None] >= window_ends[None, :]).astype(jnp.int32), axis=1)
    key_rows = arranged[1]
    value_rows = arranged[2]
    block_rows = min(512, span_rows)
    block_count = span_rows // block_rows

    def attend_block(inputs):
        query_block, segment_block = inputs
        scores = jnp.dot(query_block, key_rows.T, preferred_element_type=jnp.float32) * score_scale
        allowed = segment_block[:, None] == segment[None, :]
        scores = jnp.where(allowed, scores, -1e30)
        row_peak = jnp.max(scores, axis=-1, keepdims=True)
        weights = jnp.exp(scores - row_peak)
        row_mass = jnp.sum(weights, axis=-1, keepdims=True)
        mixed = (
            jnp.dot(weights.astype(jnp.bfloat16), value_rows, preferred_element_type=jnp.float32)
            / row_mass
        )
        return mixed.astype(jnp.bfloat16)

    mixed_rows = lax.map(
        attend_block,
        (
            arranged[0].reshape(block_count, block_rows, head_dim),
            segment.reshape(block_count, block_rows),
        ),
    ).reshape(span_rows, head_dim)
    outgoing_back = (
        mixed_rows.reshape(frame_share, devices, token_rows * token_cols, head_dim)
        .transpose(1, 0, 2, 3)
        .reshape(devices, local_share, head_dim)
    )
    returned = lax.all_to_all(outgoing_back, "seq", split_axis=0, concat_axis=0, tiled=True)
    merged = (
        returned.reshape(groups, HEADS, local_share, head_dim)
        .transpose(0, 2, 1, 3)
        .reshape(tok_count, D)
    )
    projected_out = jnp.dot(
        merged,
        lax.all_gather(out_weight, "seq", axis=0, tiled=True),
        preferred_element_type=jnp.float32,
    )
    return projected_out.astype(jnp.bfloat16)


HD = D // HEADS
SLOT = 80
MASK = 1024.0
F32 = jnp.float32
BF16 = jnp.bfloat16
VMEM = pl.BlockSpec(memory_space=pltpu.VMEM)
SMEM = pl.BlockSpec(memory_space=pltpu.SMEM)
NT = (((1,), (1,)), ((), ()))


def params(mib=40):
    return pltpu.CompilerParams(vmem_limit_bytes=mib << 20)


def silu(v):
    return v / (1.0 + jnp.exp(-v))


def long_window(lengths):
    first, second = lengths[0, 0], lengths[0, 1]
    half = 1024
    start = jnp.where(first == half, 0, jnp.where(second == half, first, first + second))
    bound = jnp.where(first == half, half + second, first)
    return start, bound


ANY = pl.BlockSpec(memory_space=pl.ANY)
TN = (((0,), (1,)), ((), ()))


def pair_weights(weights, pairs, ch=128):
    for o in range(3):
        for four in range(4):
            for out_row in range(2):
                columns = slice(out_row * ch, (out_row + 1) * ch)
                tap = four - out_row
                for j in range(3):
                    rows = slice((four * 3 + j) * ch, (four * 3 + j + 1) * ch)
                    if 0 <= tap < 3:
                        pairs[o, rows, columns] = weights[o, tap, j]
                    else:
                        pairs[o, rows, columns] = jnp.zeros((ch, ch), BF16)


def prepare_kernel(
    patch_any, qkv_any, first_any, second_any, folded_ref, pairs_one, pairs_two, patch_ref,
    qkv_ref, first_ref, second_ref, sems,
):
    copies = [
        pltpu.make_async_copy(patch_any, patch_ref, sems.at[0]),
        pltpu.make_async_copy(qkv_any.at[:, pl.ds(0, D)], qkv_ref.at[0], sems.at[1]),
        pltpu.make_async_copy(first_any, first_ref, sems.at[2]),
        pltpu.make_async_copy(second_any, second_ref, sems.at[3]),
        pltpu.make_async_copy(qkv_any.at[:, pl.ds(D, D)], qkv_ref.at[1], sems.at[4]),
        pltpu.make_async_copy(qkv_any.at[:, pl.ds(2 * D, D)], qkv_ref.at[2], sems.at[5]),
    ]
    for copy in copies:
        copy.start()
    copies[0].wait()
    patch = patch_ref[...].astype(F32)
    centered = (patch - jnp.mean(patch, axis=1, keepdims=True)).astype(BF16)

    def fold(part):
        product = lax.dot_general(qkv_ref[part], centered, TN, preferred_element_type=F32)
        folded_ref[part * D : (part + 1) * D] = product.astype(BF16)

    copies[1].wait()
    copies[2].wait()
    fold(0)
    pair_weights(first_ref, pairs_one)
    copies[3].wait()
    copies[4].wait()
    fold(1)
    pair_weights(second_ref, pairs_two)
    copies[5].wait()
    fold(2)


def prepare(patch_weight, qkv_weight, conv_first, conv_second):
    inner = patch_weight.shape[0]
    ch = conv_first.shape[-1]
    pairs = jax.ShapeDtypeStruct((3, 12 * ch, 2 * ch), BF16)
    return pl.pallas_call(
        prepare_kernel,
        out_shape=(
            jax.ShapeDtypeStruct((3 * D, inner), BF16),
            pairs,
            pairs,
            jax.ShapeDtypeStruct(patch_weight.shape, BF16),
        ),
        in_specs=[ANY] * 4,
        out_specs=(VMEM,) * 4,
        scratch_shapes=[
            pltpu.VMEM((3, D, D), BF16),
            pltpu.VMEM(conv_first.shape, BF16),
            pltpu.VMEM(conv_first.shape, BF16),
            pltpu.SemaphoreType.DMA((6,)),
        ],
        compiler_params=params(),
        name="prepare",
        cost_estimate=pl.CostEstimate(flops=2 * inner * D * 3 * D, bytes_accessed=12 << 20, transcendentals=0),
    )(patch_weight, qkv_weight, conv_first, conv_second)


def frame_taps(counts_ref, frames):
    def clip_of(frame):
        end = 0
        index = 0
        for c in range(counts_ref.shape[0]):
            end = end + counts_ref[c]
            index = index + jnp.where(frame >= end, 1, 0)
        return index

    own = [clip_of(f) for f in range(frames)]
    joined = [jnp.where(own[f] == own[f + 1], 1.0, 0.0) for f in range(frames - 1)]
    return [0.0] + joined, joined + [0.0]


def conv_kernel(
    counts_any, lengths_any, own_any, before_ref, after_ref, pairs_one, pairs_two, patch_ref,
    keep_ref, send_ref, grid_one, grid_two, pixels, own_ref, counts_ref, lengths_ref, sems,
):
    copies = [
        pltpu.make_async_copy(own_any, own_ref, sems.at[0]),
        pltpu.make_async_copy(counts_any, counts_ref, sems.at[1]),
        pltpu.make_async_copy(lengths_any, lengths_ref, sems.at[2]),
    ]
    for copy in copies:
        copy.start()
    frames, _, cols, ch = own_ref.shape
    wide = 12 * ch
    position = lax.axis_index("seq")
    column = lax.broadcasted_iota(jnp.int32, (frames, cols, ch), 1)

    def shifted(row):
        left = jnp.where(column == 0, 0.0, pltpu.roll(row, 1, 1))
        right = jnp.where(column == cols - 1, 0.0, pltpu.roll(row, cols - 1, 1))
        return [part.astype(BF16) for part in (left, row, right)]

    blank = jnp.zeros((cols, wide), BF16)
    for g in range(2):
        grid_one[g, 0] = blank
        grid_one[g, frames + 1] = blank
    grid_two[0] = blank
    grid_two[frames + 1] = blank
    sources = [before_ref, before_ref, own_ref, own_ref, after_ref, after_ref]
    for r in (0, 1, 4, 5, 2, 3):
        if r == 2:
            copies[0].wait()
        row = silu(sources[r][:, r % 2].astype(F32))
        parts = shifted(row)
        for g in range(2):
            four = r - 2 * g
            if 0 <= four < 4:
                for j in range(3):
                    grid_one[g, 1 : frames + 1, :, (four * 3 + j) * ch : (four * 3 + j + 1) * ch] = parts[j]

    copies[1].wait()
    copies[2].wait()
    before_tap, after_tap = frame_taps(counts_ref, frames)

    def summed(terms):
        rows = []
        for f in range(frames):
            total = terms[1][f]
            if f > 0:
                total = total + before_tap[f] * terms[0][f]
            if f < frames - 1:
                total = total + after_tap[f] * terms[2][f]
            rows.append(total)
        return jnp.stack(rows)

    for g in range(2):
        terms = []
        for o in range(3):
            left = grid_one[g, o : o + frames].reshape(frames * cols, wide)
            terms.append(
                jnp.dot(left, pairs_one[o], preferred_element_type=F32).reshape(frames, cols, 2 * ch)
            )
        hidden = summed(terms)
        for out_row in range(2):
            four = 2 * g + out_row
            row = hidden[:, :, out_row * ch : (out_row + 1) * ch]
            if four == 0:
                row = row * jnp.where(position == 0, 0.0, 1.0)
            if four == 3:
                row = row * jnp.where(position == lax.axis_size("seq") - 1, 0.0, 1.0)
            row = silu(row.astype(BF16).astype(F32))
            parts = shifted(row)
            for j in range(3):
                grid_two[1 : frames + 1, :, (four * 3 + j) * ch : (four * 3 + j + 1) * ch] = parts[j]
    terms = []
    for o in range(3):
        left = grid_two[o : o + frames].reshape(frames * cols, wide)
        terms.append(
            jnp.dot(left, pairs_two[o], preferred_element_type=F32).reshape(frames, cols, 2 * ch)
        )
    residual = summed(terms)
    for out_row in range(2):
        block = own_ref[:, out_row].astype(F32) + residual[:, :, out_row * ch : (out_row + 1) * ch]
        pixels[out_row] = block.astype(BF16).astype(F32).reshape(frames * cols, ch)
    tokens = frames * cols // 2
    patches = jnp.concatenate(
        [pixels[a, pl.ds(b, tokens, 2), :] for a in range(2) for b in range(2)], axis=1
    )
    embedded = jnp.dot(patches.astype(BF16), patch_ref[...], preferred_element_type=F32)
    centered = embedded - jnp.mean(embedded, axis=1, keepdims=True)
    variance = jnp.mean(centered * centered, axis=1, keepdims=True)
    scaled = patches * (1.0 / jnp.sqrt(variance + 1e-06))
    half = tokens // 2
    low, high = scaled[:half], scaled[half:]
    start, _ = long_window(lengths_ref)
    q_cols = cols // 2
    slot = lax.broadcasted_iota(jnp.int32, low.shape, 0)
    token = (slot // q_cols) * (lax.axis_size("seq") * q_cols) + position * q_cols + slot % q_cols
    inside = jnp.where(token >= start, 1, 0)
    mine = inside == jnp.where(position % 2 == 0, 1, 0)
    keep = jnp.where(mine, low, high).astype(BF16)
    send = jnp.where(mine, high, low).astype(BF16)
    for tile in range(4):
        keep_ref[tile * half : (tile + 1) * half] = keep[:, tile * ch : (tile + 1) * ch]
        send_ref[tile * half : (tile + 1) * half] = send[:, tile * ch : (tile + 1) * ch]


def convolve(counts, lengths, clip, before, after, pairs_one, pairs_two, patch_weight):
    frames, _, cols, ch = clip.shape
    tokens = frames * cols // 2
    out = jax.ShapeDtypeStruct((2 * tokens, ch), BF16)
    return pl.pallas_call(
        conv_kernel,
        out_shape=(out, out),
        in_specs=[ANY] * 3 + [VMEM] * 5,
        out_specs=(VMEM, VMEM),
        scratch_shapes=[
            pltpu.VMEM((2, frames + 2, cols, 12 * ch), BF16),
            pltpu.VMEM((frames + 2, cols, 12 * ch), BF16),
            pltpu.VMEM((2, frames * cols, ch), F32),
            pltpu.VMEM(clip.shape, BF16),
            pltpu.SMEM(counts.shape, jnp.int32),
            pltpu.SMEM(lengths.shape, jnp.int32),
            pltpu.SemaphoreType.DMA((3,)),
        ],
        compiler_params=params(),
        name="convolve",
        cost_estimate=pl.CostEstimate(flops=2 << 30, bytes_accessed=4 << 20, transcendentals=1 << 18),
    )(counts, lengths, clip, before, after, pairs_one, pairs_two, patch_weight)


def chip_at(place):
    chips = lax.axis_size("seq") // 2
    place = lax.rem(place + 2 * chips, chips)
    return jnp.where(place < chips // 2, 2 * place, 2 * (chips - 1 - place) + 1)


def ring_place():
    chips = lax.axis_size("seq") // 2
    chip = lax.axis_index("seq") // 2
    return jnp.where(chip % 2 == 0, chip // 2, chips - 1 - chip // 2)


def ring_pairs():
    size = lax.axis_size("seq")
    chips = size // 2
    order = [2 * i for i in range(chips // 2)] + [2 * i + 1 for i in reversed(range(chips // 2))]
    return [
        (2 * order[i] + core, 2 * order[(i + 1) % chips] + core) for i in range(chips) for core in range(2)
    ]


def window_sides(lengths_ref, chip, count):
    size = lax.axis_size("seq")
    core = lax.axis_index("seq") % 2
    start, bound = long_window(lengths_ref)
    lane = lax.broadcasted_iota(jnp.int32, (8, count), 1)
    half = count // 2
    slot = lane % half
    row = 2 * chip + jnp.where(lane < half, core, 1 - core)
    q_cols = 16
    token = (slot // q_cols) * (size * q_cols) + row * q_cols + slot % q_cols
    inside = jnp.where(token >= start, 1, 0)
    upper = inside != jnp.where(core == 0, 1, 0)
    token = jnp.where(upper, token + 4 * size * q_cols, token)
    return jnp.where(token < bound, 1.0, -1.0)


def block_tokens(ref, ch=128, half=64):
    second = 4 * half + 5 * SLOT
    parts = []
    for base in (0, second):
        parts.append(
            jnp.concatenate([ref[base + t * half : base + (t + 1) * half] for t in range(4)], axis=1)
        )
    return jnp.concatenate(parts, axis=0)


def half_tokens(ref, half=64):
    return jnp.concatenate([ref[t * half : (t + 1) * half] for t in range(4)], axis=1)


def normed_heads(part, gain):
    count = part.shape[1]
    heads = part.reshape(-1, HD, count)
    factor = lax.rsqrt(jnp.mean(heads * heads, axis=1, keepdims=True) + 1e-06)
    return heads * factor * gain[None, :, :count]


def attend(tokens, sides, folded, key_gain, queries, acc_ref, keys_ref, values_ref, scores_ref, weights_ref):
    count = tokens.shape[0]
    row = lax.broadcasted_iota(jnp.int32, (8, count), 0)
    key_tail = jnp.where(row == 0, sides, jnp.where(row == 1, 1.0, 0.0))
    value_tail = jnp.where(row == 0, 1.0, 0.0)
    heads_at_once = 4
    for first in range(0, HEADS, heads_at_once):
        rows = slice(first * HD, (first + heads_at_once) * HD)
        part = lax.dot_general(folded[rows], tokens, NT, preferred_element_type=F32)
        keys = normed_heads(part, key_gain)
        for h in range(heads_at_once):
            keys_ref[first + h] = jnp.concatenate([keys[h], key_tail], axis=0).astype(BF16)
            scores_ref[first + h] = jnp.dot(queries[first + h], keys_ref[first + h], preferred_element_type=F32)
    for first in range(0, HEADS, heads_at_once):
        rows = slice(D + first * HD, D + (first + heads_at_once) * HD)
        part = lax.dot_general(folded[rows], tokens, NT, preferred_element_type=F32)
        values = part.reshape(heads_at_once, HD, count)
        for h in range(heads_at_once):
            values_ref[first + h] = jnp.concatenate([values[h], value_tail], axis=0).astype(BF16)
    lane = lax.broadcasted_iota(jnp.int32, (128, 128), 1)
    peaks = jnp.zeros((128, 128), F32)
    for h in range(HEADS):
        scores = scores_ref[h]
        peak = jnp.max(scores, axis=1, keepdims=True)
        weights_ref[h] = jnp.exp2(scores - peak).astype(BF16)
        peaks = jnp.where(lane == h, peak, peaks)
    peaks = peaks.T
    tail_row = lax.broadcasted_iota(jnp.int32, (8, 128), 0)
    for h in range(HEADS):
        mixed = lax.dot_general(values_ref[h], weights_ref[h], NT, preferred_element_type=F32)
        acc_ref[h, :HD] = mixed[:HD]
        acc_ref[h, HD:] = jnp.where(tail_row == 1, peaks[h : h + 1], mixed[HD:])


def attend_scratch(count):
    return [
        pltpu.VMEM((HEADS, SLOT, count), BF16),
        pltpu.VMEM((HEADS, SLOT, count), BF16),
        pltpu.VMEM((HEADS, 128, count), F32),
        pltpu.VMEM((HEADS, 128, count), BF16),
    ]


def own_kernel(lengths_ref, block_ref, folded_ref, query_gain_ref, key_gain_ref, queries_ref, acc_ref, *scratch):
    tokens = block_tokens(block_ref)
    count = tokens.shape[0]
    sides = window_sides(lengths_ref, lax.axis_index("seq") // 2, count)
    part = lax.dot_general(folded_ref[:D], tokens, NT, preferred_element_type=F32)
    queries = normed_heads(part, query_gain_ref[...])
    row = lax.broadcasted_iota(jnp.int32, (8, count), 0)
    tail = jnp.where(row == 0, MASK * sides, jnp.where(row == 1, -MASK, 0.0))
    for h in range(HEADS):
        queries_ref[h] = jnp.concatenate([queries[h], tail], axis=0).T.astype(BF16)
    attend(tokens, sides, folded_ref.at[D:], key_gain_ref[...], queries_ref, acc_ref, *scratch)


def step_kernel(step, lengths_ref, ahead_ref, behind_ref, folded_ref, key_gain_ref, queries_ref, acc_ref, *scratch):
    place = ring_place()
    if step < 4:
        tokens = jnp.concatenate([block_tokens(ahead_ref), block_tokens(behind_ref)], axis=0)
        sides = jnp.concatenate(
            [
                window_sides(lengths_ref, chip_at(place - step), 128),
                window_sides(lengths_ref, chip_at(place + step), 128),
            ],
            axis=1,
        )
    else:
        tokens = jnp.concatenate([half_tokens(ahead_ref), half_tokens(behind_ref)], axis=0)
        sides = window_sides(lengths_ref, chip_at(place + step), 128)
    attend(tokens, sides, folded_ref.at[D:], key_gain_ref[...], queries_ref, acc_ref, *scratch)


ACC = jax.ShapeDtypeStruct((HEADS, SLOT, 128), F32)


def cost(count):
    flops = 2 * count * 2 * D * 512 + 4 * HEADS * 128 * 128 * count
    return pl.CostEstimate(flops=2 * flops, bytes_accessed=5 << 20, transcendentals=HEADS * 128 * count)


def own_attention(lengths, block, folded, query_gain, key_gain):
    return pl.pallas_call(
        own_kernel,
        out_shape=(jax.ShapeDtypeStruct((HEADS, 128, SLOT), BF16), ACC),
        in_specs=[SMEM] + [VMEM] * 4,
        out_specs=(VMEM, VMEM),
        scratch_shapes=attend_scratch(128),
        compiler_params=params(),
        name="own_attention",
        cost_estimate=cost(192),
    )(lengths, block, folded, query_gain, key_gain)


def step_attention(step, lengths, ahead, behind, folded, key_gain, queries):
    return pl.pallas_call(
        functools.partial(step_kernel, step),
        out_shape=ACC,
        in_specs=[SMEM] + [VMEM] * 5,
        out_specs=VMEM,
        scratch_shapes=attend_scratch(256 if step < 4 else 128),
        compiler_params=params(),
        name="step_attention",
        cost_estimate=cost(256 if step < 4 else 128),
    )(lengths, ahead, behind, folded, key_gain, queries)


def out_kernel(parts, *refs):
    acc_refs = refs[:parts]
    block_refs = refs[parts:-3]
    keep_ref, send_ref, mixed_ref = refs[-3:]
    zeros = jnp.zeros((SLOT - HD, 128), F32)
    for h in range(HEADS):
        peaks = [acc[h, HD + 1 : HD + 2] for acc in acc_refs]
        peak = functools.reduce(jnp.maximum, peaks)
        total = None
        for acc, own in zip(acc_refs, peaks):
            term = acc[h] * jnp.exp2(own - peak)
            total = term if total is None else total + term
        mixed = total[:HD] / total[HD : HD + 1]
        mixed_ref[h] = jnp.concatenate([mixed, zeros], axis=0)
    place = ring_place()
    core = lax.axis_index("seq") % 2
    offsets = [0, -1, 1, -2, 2, -3, 3, 4]
    per_core = len(block_refs) // 2
    slots, tiles = [], []
    for side in range(2):
        refs_here = block_refs[side * per_core : (side + 1) * per_core]
        for index, offset in enumerate(offsets):
            head = 2 * chip_at(place + offset) + jnp.where(core == side, 0, 1)
            slots.append(mixed_ref[head])
            if index < 7:
                low, high, base = refs_here[index], refs_here[index], 256 + 5 * SLOT + 256
            else:
                low, high, base = refs_here[7], refs_here[8], 256
            tiles.append(
                [low[256 + t * SLOT : 256 + (t + 1) * SLOT] for t in range(5)]
                + [high[base + t * SLOT : base + (t + 1) * SLOT] for t in range(4)]
            )
    left = jnp.concatenate(slots, axis=0).T.astype(BF16)
    half = keep_ref.shape[0]
    for first in range(0, 9, 2):
        group = range(first, min(first + 2, 9))
        right = jnp.concatenate(
            [jnp.concatenate([block[t] for block in tiles], axis=0) for t in group], axis=1
        )
        result = jnp.dot(left, right, preferred_element_type=F32).astype(BF16)
        columns = slice(first * 128, (group[-1] + 1) * 128)
        keep_ref[:, columns] = result[:half]
        send_ref[:, columns] = result[half:]


def project_out(accs, blocks):
    out = jax.ShapeDtypeStruct((64, D), BF16)
    return pl.pallas_call(
        functools.partial(out_kernel, len(accs)),
        out_shape=(out, out),
        in_specs=[VMEM] * (len(accs) + len(blocks)),
        out_specs=(VMEM, VMEM),
        scratch_shapes=[pltpu.VMEM((HEADS, SLOT, 128), F32)],
        compiler_params=params(),
        name="project_out",
        cost_estimate=pl.CostEstimate(flops=2 * 128 * 1280 * D, bytes_accessed=4 << 20, transcendentals=0),
    )(*accs, *blocks)


def merge_kernel(lengths_ref, keep_ref, got_ref, out_ref):
    position = lax.axis_index("seq")
    keep = keep_ref[...].astype(F32)
    got = got_ref[...].astype(F32)
    start, _ = long_window(lengths_ref)
    q_cols = 16
    slot = lax.broadcasted_iota(jnp.int32, keep.shape, 0)
    token = (slot // q_cols) * (lax.axis_size("seq") * q_cols) + position * q_cols + slot % q_cols
    inside = jnp.where(token >= start, 1, 0)
    mine = inside == jnp.where(position % 2 == 0, 1, 0)
    half = keep.shape[0]
    out_ref[:half] = jnp.where(mine, keep, got).astype(BF16)
    out_ref[half:] = jnp.where(mine, got, keep).astype(BF16)


def merge(lengths, keep, got):
    return pl.pallas_call(
        merge_kernel,
        out_shape=jax.ShapeDtypeStruct((128, D), BF16),
        in_specs=[SMEM, VMEM, VMEM],
        out_specs=VMEM,
        compiler_params=params(),
        name="merge",
    )(lengths, keep, got)


def weight_tiles(out_weight):
    padded = jnp.pad(out_weight, ((0, SLOT - HD), (0, 0)))
    return padded.reshape(SLOT, 9, 128).transpose(1, 0, 2).reshape(9 * SLOT, 128)


def shards(
    clip, frame_counts, conv_first, conv_second, patch_weight, qkv_weight, query_gain, key_gain,
    out_weight, window_lengths,
):
    size = lax.axis_size("seq")
    up = [(i, i + 1) for i in range(size - 1)]
    down = [(j, i) for i, j in up]
    cores = [(i, i ^ 1) for i in range(size)]
    forward = ring_pairs()
    backward = [(j, i) for i, j in forward]

    def send(array, pairs):
        return lax.ppermute(array, "seq", pairs)

    def tied(*arrays):
        return lax.optimization_barrier(arrays)

    before = send(clip, up)
    after = send(clip, down)
    score_scale = math.log2(math.e) / math.sqrt(HD)
    query_rows = jnp.broadcast_to((query_gain * score_scale)[:, None], (HD, 256))
    key_rows = jnp.broadcast_to(key_gain[:, None], (HD, 256))
    weight = weight_tiles(out_weight)
    folded, pairs_one, pairs_two, patch = prepare(patch_weight, qkv_weight, conv_first, conv_second)
    before, after, pairs_one, weight, query_rows, key_rows = tied(
        before, after, pairs_one, weight, query_rows, key_rows
    )
    keep, other = convolve(
        frame_counts, window_lengths, clip, before, after, pairs_one, pairs_two, patch
    )
    got = send(other, cores)
    cut = 256 + 5 * SLOT
    block = jnp.concatenate([keep, weight[: 5 * SLOT], got, weight[5 * SLOT :]], axis=0)
    ahead, behind = block, block
    accs, blocks, sibling = [], [block], []
    for step in range(1, 5):
        if step < 4:
            ahead_next, behind_next = send(ahead, forward), send(behind, backward)
        else:
            ahead_next, behind_next = send(ahead[:cut], forward), send(behind[cut:], backward)
        if step == 1:
            sibling.append(send(block, cores))
            queries, acc = own_attention(window_lengths, block, folded, query_rows, key_rows)
        else:
            sibling += [send(ahead, cores), send(behind, cores)]
            acc = step_attention(step - 1, window_lengths, ahead, behind, folded, key_rows, queries)
        ahead, behind, acc = tied(ahead_next, behind_next, acc)
        accs.append(acc)
        blocks += [ahead, behind]
    sibling += [send(ahead, cores), send(behind, cores)]
    accs.append(step_attention(4, window_lengths, ahead, behind, folded, key_rows, queries))
    keep_rows, send_rows = project_out(accs, blocks + sibling)
    return merge(window_lengths, keep_rows, send(send_rows, cores))


def solution(mesh):
    own = mesh.shape["seq"] == HEADS
    return jax.shard_map(
        shards if own else general_shards,
        mesh=mesh,
        in_specs=(
            P("groups", "seq", None, None),
            P("groups"),
            P(),
            P(),
            P(),
            P(),
            P(),
            P(),
            P("seq", None),
            P("groups", None),
        ),
        out_specs=P(("groups", "seq"), None),
        check_vma=False,
    )
```

```python
import functools
import math

import jax
import jax.numpy as jnp
from jax import lax
from jax.experimental import pallas as pl
from jax.experimental.pallas import tpu as pltpu
from jax.sharding import PartitionSpec as P

D = 1152
HEADS = 16


def extended(array, sides, width):
    for axis, dim in sides:
        size, length = (lax.axis_size(axis), array.shape[dim])
        up = [(i, (i + 1) % size) for i in range(size - 1)]
        down = [(j, i) for i, j in up]
        last = lax.slice_in_dim(array, length - width, length, axis=dim)
        first = lax.slice_in_dim(array, 0, width, axis=dim)
        before = lax.ppermute(last, axis, up)
        after = lax.ppermute(first, axis, down)
        array = jnp.concatenate([before, array, after], axis=dim)
    return array


def frame_weights(frame_counts, frames):
    position = jnp.arange(frames, dtype=jnp.int32)
    clip_ends = jnp.cumsum(frame_counts)

    def clip_of(index):
        return jnp.sum((index[:, None] >= clip_ends[None, :]).astype(jnp.int32), axis=1)

    own_clip = clip_of(position)
    columns = []
    for offset in (-1, 0, 1):
        neighbor = position + offset
        inside = (neighbor >= 0) & (neighbor < frames)
        same_clip = clip_of(jnp.clip(neighbor, 0, frames - 1)) == own_clip
        columns.append((inside & same_clip).astype(jnp.float32))
    return jnp.stack(columns, axis=1)


def convolve_rows(activation, kernel, tap_weights):
    empty_frame = jnp.zeros_like(activation[:1])
    shifted = (
        jnp.concatenate([empty_frame, activation[:-1]], 0),
        activation,
        jnp.concatenate([activation[1:], empty_frame], 0),
    )
    summed = None
    for offset in range(3):
        response = lax.conv_general_dilated(
            shifted[offset],
            kernel[offset],
            (1, 1),
            ((0, 0), (1, 1)),
            dimension_numbers=("NHWC", "HWIO", "NHWC"),
            preferred_element_type=jnp.float32,
        )
        tap_term = tap_weights[:, offset][:, None, None, None] * response
        summed = tap_term if offset == 0 else summed + tap_term
    return summed


def rms_scale(part, gain):
    factor = lax.rsqrt(jnp.mean(part * part, axis=-1, keepdims=True) + 1e-06)
    return (part * factor * gain).astype(jnp.bfloat16)


def general_shards(
    clip,
    frame_counts,
    conv_first,
    conv_second,
    patch_weight,
    qkv_weight,
    query_gain,
    key_gain,
    out_weight,
    window_lengths,
):
    frames, tile_rows, tile_cols, channels = clip.shape
    devices = lax.axis_size("seq")
    position = lax.axis_index("seq")
    head_dim = D // HEADS
    score_scale = 1.0 / math.sqrt(head_dim)
    tap_weights = frame_weights(frame_counts, frames)
    source = clip.astype(jnp.float32)
    padded_clip = extended(clip, (("seq", 1),), 2)
    first_in = jax.nn.silu(padded_clip.astype(jnp.float32)).astype(jnp.bfloat16)
    hidden_wide = convolve_rows(first_in, conv_first, tap_weights)
    global_row = position * tile_rows - 1 + jnp.arange(tile_rows + 2, dtype=jnp.int32)
    inside = ((global_row >= 0) & (global_row < tile_rows * devices)).astype(jnp.float32)
    hidden_one = (hidden_wide * inside[None, :, None, None]).astype(jnp.bfloat16)
    padded_second = jax.nn.silu(hidden_one.astype(jnp.float32)).astype(jnp.bfloat16)
    latent = (source + convolve_rows(padded_second, conv_second, tap_weights)).astype(jnp.bfloat16)
    token_rows = tile_rows // 2
    token_cols = tile_cols // 2
    patches = (
        latent.reshape(frames, token_rows, 2, token_cols, 2, channels)
        .transpose(0, 1, 3, 2, 4, 5)
        .reshape(-1, 4 * channels)
    )
    tok_count = patches.shape[0]
    embedded = jnp.dot(patches, patch_weight, preferred_element_type=jnp.float32).astype(
        jnp.bfloat16
    )
    values_f = embedded.astype(jnp.float32)
    row_mean = jnp.mean(values_f, axis=-1, keepdims=True)
    centered = values_f - row_mean
    variance = jnp.mean(centered * centered, axis=-1, keepdims=True)
    normed = (centered / jnp.sqrt(variance + 1e-06)).astype(jnp.bfloat16)
    projected = jnp.dot(normed, qkv_weight, preferred_element_type=jnp.float32).reshape(
        tok_count, 3, HEADS, head_dim
    )
    stacked = jnp.stack(
        [
            rms_scale(projected[:, 0], query_gain),
            rms_scale(projected[:, 1], key_gain),
            projected[:, 2].astype(jnp.bfloat16),
        ],
        axis=1,
    )
    groups = devices // HEADS
    frame_share = frames // groups
    local_share = tok_count // groups
    span_rows = devices * local_share
    outgoing = (
        stacked.reshape(groups, local_share, 3, HEADS, head_dim)
        .transpose(0, 3, 1, 2, 4)
        .reshape(devices, local_share, 3 * head_dim)
    )
    incoming = lax.all_to_all(outgoing, "seq", split_axis=0, concat_axis=0, tiled=True)
    arranged = (
        incoming.reshape(devices, frame_share, token_rows * token_cols, 3, head_dim)
        .transpose(3, 1, 0, 2, 4)
        .reshape(3, span_rows, head_dim)
    )
    my_group = position // HEADS
    lengths = lax.dynamic_index_in_dim(window_lengths, my_group, 0, keepdims=False)
    window_ends = jnp.cumsum(lengths)
    token_index = jnp.arange(span_rows, dtype=jnp.int32)
    segment = jnp.sum((token_index[:, None] >= window_ends[None, :]).astype(jnp.int32), axis=1)
    key_rows = arranged[1]
    value_rows = arranged[2]
    block_rows = min(512, span_rows)
    block_count = span_rows // block_rows

    def attend_block(inputs):
        query_block, segment_block = inputs
        scores = jnp.dot(query_block, key_rows.T, preferred_element_type=jnp.float32) * score_scale
        allowed = segment_block[:, None] == segment[None, :]
        scores = jnp.where(allowed, scores, -1e30)
        row_peak = jnp.max(scores, axis=-1, keepdims=True)
        weights = jnp.exp(scores - row_peak)
        row_mass = jnp.sum(weights, axis=-1, keepdims=True)
        mixed = (
            jnp.dot(weights.astype(jnp.bfloat16), value_rows, preferred_element_type=jnp.float32)
            / row_mass
        )
        return mixed.astype(jnp.bfloat16)

    mixed_rows = lax.map(
        attend_block,
        (
            arranged[0].reshape(block_count, block_rows, head_dim),
            segment.reshape(block_count, block_rows),
        ),
    ).reshape(span_rows, head_dim)
    outgoing_back = (
        mixed_rows.reshape(frame_share, devices, token_rows * token_cols, head_dim)
        .transpose(1, 0, 2, 3)
        .reshape(devices, local_share, head_dim)
    )
    returned = lax.all_to_all(outgoing_back, "seq", split_axis=0, concat_axis=0, tiled=True)
    merged = (
        returned.reshape(groups, HEADS, local_share, head_dim)
        .transpose(0, 2, 1, 3)
        .reshape(tok_count, D)
    )
    projected_out = jnp.dot(
        merged,
        lax.all_gather(out_weight, "seq", axis=0, tiled=True),
        preferred_element_type=jnp.float32,
    )
    return projected_out.astype(jnp.bfloat16)


HD = D // HEADS
SLOT = 80
MASK = 1024.0
F32 = jnp.float32
BF16 = jnp.bfloat16
VMEM = pl.BlockSpec(memory_space=pltpu.VMEM)
SMEM = pl.BlockSpec(memory_space=pltpu.SMEM)
NT = (((1,), (1,)), ((), ()))


def params(mib=40):
    return pltpu.CompilerParams(vmem_limit_bytes=mib << 20)


def silu(v):
    return v / (1.0 + jnp.exp(-v))


def long_window(lengths):
    first, second = lengths[0, 0], lengths[0, 1]
    half = 1024
    start = jnp.where(first == half, 0, jnp.where(second == half, first, first + second))
    bound = jnp.where(first == half, half + second, first)
    return start, bound


ANY = pl.BlockSpec(memory_space=pl.ANY)
TN = (((0,), (1,)), ((), ()))


def pair_weights(weights, pairs, ch=128):
    for o in range(3):
        for four in range(4):
            for out_row in range(2):
                columns = slice(out_row * ch, (out_row + 1) * ch)
                tap = four - out_row
                for j in range(3):
                    rows = slice((four * 3 + j) * ch, (four * 3 + j + 1) * ch)
                    if 0 <= tap < 3:
                        pairs[o, rows, columns] = weights[o, tap, j]
                    else:
                        pairs[o, rows, columns] = jnp.zeros((ch, ch), BF16)


def prepare_kernel(patch_any, first_any, second_any, pairs_one, pairs_two, patch_ref, centered_ref, first_ref, second_ref, sems):
    copies = [
        pltpu.make_async_copy(first_any, first_ref, sems.at[0]),
        pltpu.make_async_copy(second_any, second_ref, sems.at[1]),
        pltpu.make_async_copy(patch_any, patch_ref, sems.at[2]),
    ]
    for copy in copies:
        copy.start()
    copies[0].wait()
    pair_weights(first_ref, pairs_one)
    copies[1].wait()
    pair_weights(second_ref, pairs_two)
    copies[2].wait()
    patch = patch_ref[...].astype(F32)
    centered_ref[...] = (patch - jnp.mean(patch, axis=1, keepdims=True)).astype(BF16)


def prepare(patch_weight, conv_first, conv_second):
    ch = conv_first.shape[-1]
    pairs = jax.ShapeDtypeStruct((3, 12 * ch, 2 * ch), BF16)
    patch = jax.ShapeDtypeStruct(patch_weight.shape, BF16)
    return pl.pallas_call(
        prepare_kernel,
        out_shape=(pairs, pairs, patch, patch),
        in_specs=[ANY] * 3,
        out_specs=(VMEM,) * 4,
        scratch_shapes=[
            pltpu.VMEM(conv_first.shape, BF16),
            pltpu.VMEM(conv_first.shape, BF16),
            pltpu.SemaphoreType.DMA((3,)),
        ],
        compiler_params=params(),
        name="prepare",
        cost_estimate=pl.CostEstimate(flops=1 << 31, bytes_accessed=6 << 20, transcendentals=0),
    )(patch_weight, conv_first, conv_second)


def fold_kernel(centered_ref, qkv_any, folded_ref, query_ref, qkv_ref, sems):
    copies = [
        pltpu.make_async_copy(qkv_any.at[:, pl.ds(D * (i + 1), D)], qkv_ref.at[i], sems.at[i]) for i in range(2)
    ]
    copies.append(pltpu.make_async_copy(qkv_any.at[:, pl.ds(0, D)], query_ref, sems.at[2]))
    for copy in copies:
        copy.start()
    for part in range(2):
        copies[part].wait()
        product = lax.dot_general(qkv_ref[part], centered_ref[...], TN, preferred_element_type=F32)
        folded_ref[part * D : (part + 1) * D] = product.astype(BF16)
    copies[2].wait()


def fold(centered, qkv_weight):
    inner = centered.shape[0]
    return pl.pallas_call(
        fold_kernel,
        out_shape=(jax.ShapeDtypeStruct((2 * D, inner), BF16), jax.ShapeDtypeStruct((D, D), BF16)),
        in_specs=[VMEM, ANY],
        out_specs=(VMEM, VMEM),
        scratch_shapes=[pltpu.VMEM((2, D, D), BF16), pltpu.SemaphoreType.DMA((3,))],
        compiler_params=params(),
        name="fold",
        cost_estimate=pl.CostEstimate(flops=2 * inner * D * 2 * D, bytes_accessed=12 << 20, transcendentals=0),
    )(centered, qkv_weight)


def frame_taps(counts_ref, frames):
    def clip_of(frame):
        end = 0
        index = 0
        for c in range(counts_ref.shape[0]):
            end = end + counts_ref[c]
            index = index + jnp.where(frame >= end, 1, 0)
        return index

    own = [clip_of(f) for f in range(frames)]
    joined = [jnp.where(own[f] == own[f + 1], 1.0, 0.0) for f in range(frames - 1)]
    return [0.0] + joined, joined + [0.0]


def conv_kernel(
    counts_any, lengths_any, own_any, before_ref, after_ref, pairs_one, pairs_two, patch_ref,
    keep_ref, send_ref, grid_one, grid_two, pixels, own_ref, counts_ref, lengths_ref, sems,
):
    copies = [
        pltpu.make_async_copy(own_any, own_ref, sems.at[0]),
        pltpu.make_async_copy(counts_any, counts_ref, sems.at[1]),
        pltpu.make_async_copy(lengths_any, lengths_ref, sems.at[2]),
    ]
    for copy in copies:
        copy.start()
    frames, _, cols, ch = own_ref.shape
    wide = 12 * ch
    position = lax.axis_index("seq")
    column = lax.broadcasted_iota(jnp.int32, (frames, cols, ch), 1)

    def shifted(row):
        left = jnp.where(column == 0, 0.0, pltpu.roll(row, 1, 1))
        right = jnp.where(column == cols - 1, 0.0, pltpu.roll(row, cols - 1, 1))
        return [part.astype(BF16) for part in (left, row, right)]

    blank = jnp.zeros((cols, wide), BF16)
    for g in range(2):
        grid_one[g, 0] = blank
        grid_one[g, frames + 1] = blank
    grid_two[0] = blank
    grid_two[frames + 1] = blank
    sources = [before_ref, before_ref, own_ref, own_ref, after_ref, after_ref]
    for r in (0, 1, 4, 5, 2, 3):
        if r == 2:
            copies[0].wait()
        row = silu(sources[r][:, r % 2].astype(F32))
        parts = shifted(row)
        for g in range(2):
            four = r - 2 * g
            if 0 <= four < 4:
                for j in range(3):
                    grid_one[g, 1 : frames + 1, :, (four * 3 + j) * ch : (four * 3 + j + 1) * ch] = parts[j]

    copies[1].wait()
    copies[2].wait()
    before_tap, after_tap = frame_taps(counts_ref, frames)

    def summed(terms):
        rows = []
        for f in range(frames):
            total = terms[1][f]
            if f > 0:
                total = total + before_tap[f] * terms[0][f]
            if f < frames - 1:
                total = total + after_tap[f] * terms[2][f]
            rows.append(total)
        return jnp.stack(rows)

    for g in range(2):
        terms = []
        for o in range(3):
            left = grid_one[g, o : o + frames].reshape(frames * cols, wide)
            terms.append(
                jnp.dot(left, pairs_one[o], preferred_element_type=F32).reshape(frames, cols, 2 * ch)
            )
        hidden = summed(terms)
        for out_row in range(2):
            four = 2 * g + out_row
            row = hidden[:, :, out_row * ch : (out_row + 1) * ch]
            if four == 0:
                row = row * jnp.where(position == 0, 0.0, 1.0)
            if four == 3:
                row = row * jnp.where(position == lax.axis_size("seq") - 1, 0.0, 1.0)
            row = silu(row.astype(BF16).astype(F32))
            parts = shifted(row)
            for j in range(3):
                grid_two[1 : frames + 1, :, (four * 3 + j) * ch : (four * 3 + j + 1) * ch] = parts[j]
    terms = []
    for o in range(3):
        left = grid_two[o : o + frames].reshape(frames * cols, wide)
        terms.append(
            jnp.dot(left, pairs_two[o], preferred_element_type=F32).reshape(frames, cols, 2 * ch)
        )
    residual = summed(terms)
    for out_row in range(2):
        block = own_ref[:, out_row].astype(F32) + residual[:, :, out_row * ch : (out_row + 1) * ch]
        pixels[out_row] = block.astype(BF16).astype(F32).reshape(frames * cols, ch)
    tokens = frames * cols // 2
    patches = jnp.concatenate(
        [pixels[a, pl.ds(b, tokens, 2), :] for a in range(2) for b in range(2)], axis=1
    )
    embedded = jnp.dot(patches.astype(BF16), patch_ref[...], preferred_element_type=F32)
    centered = embedded - jnp.mean(embedded, axis=1, keepdims=True)
    variance = jnp.mean(centered * centered, axis=1, keepdims=True)
    scaled = patches * (1.0 / jnp.sqrt(variance + 1e-06))
    half = tokens // 2
    low, high = scaled[:half], scaled[half:]
    start, _ = long_window(lengths_ref)
    q_cols = cols // 2
    slot = lax.broadcasted_iota(jnp.int32, low.shape, 0)
    token = (slot // q_cols) * (lax.axis_size("seq") * q_cols) + position * q_cols + slot % q_cols
    inside = jnp.where(token >= start, 1, 0)
    mine = inside == jnp.where(position % 2 == 0, 1, 0)
    keep = jnp.where(mine, low, high).astype(BF16)
    send = jnp.where(mine, high, low).astype(BF16)
    keep_ref[...] = keep
    send_ref[...] = send


def convolve(counts, lengths, clip, before, after, pairs_one, pairs_two, patch_weight):
    frames, _, cols, ch = clip.shape
    tokens = frames * cols // 2
    out = jax.ShapeDtypeStruct((tokens // 2, 4 * ch), BF16)
    return pl.pallas_call(
        conv_kernel,
        out_shape=(out, out),
        in_specs=[ANY] * 3 + [VMEM] * 5,
        out_specs=(VMEM, VMEM),
        scratch_shapes=[
            pltpu.VMEM((2, frames + 2, cols, 12 * ch), BF16),
            pltpu.VMEM((frames + 2, cols, 12 * ch), BF16),
            pltpu.VMEM((2, frames * cols, ch), F32),
            pltpu.VMEM(clip.shape, BF16),
            pltpu.SMEM(counts.shape, jnp.int32),
            pltpu.SMEM(lengths.shape, jnp.int32),
            pltpu.SemaphoreType.DMA((3,)),
        ],
        compiler_params=params(),
        name="convolve",
        cost_estimate=pl.CostEstimate(flops=2 << 30, bytes_accessed=4 << 20, transcendentals=1 << 18),
    )(counts, lengths, clip, before, after, pairs_one, pairs_two, patch_weight)


def chip_at(place):
    chips = lax.axis_size("seq") // 2
    place = lax.rem(place + 2 * chips, chips)
    return jnp.where(place < chips // 2, 2 * place, 2 * (chips - 1 - place) + 1)


def ring_place():
    chips = lax.axis_size("seq") // 2
    chip = lax.axis_index("seq") // 2
    return jnp.where(chip % 2 == 0, chip // 2, chips - 1 - chip // 2)


def ring_pairs():
    size = lax.axis_size("seq")
    chips = size // 2
    order = [2 * i for i in range(chips // 2)] + [2 * i + 1 for i in reversed(range(chips // 2))]
    return [
        (2 * order[i] + core, 2 * order[(i + 1) % chips] + core) for i in range(chips) for core in range(2)
    ]


def window_sides(lengths_ref, chip, count):
    size = lax.axis_size("seq")
    core = lax.axis_index("seq") % 2
    start, bound = long_window(lengths_ref)
    lane = lax.broadcasted_iota(jnp.int32, (8, count), 1)
    half = count // 2
    slot = lane % half
    row = 2 * chip + jnp.where(lane < half, core, 1 - core)
    q_cols = 16
    token = (slot // q_cols) * (size * q_cols) + row * q_cols + slot % q_cols
    inside = jnp.where(token >= start, 1, 0)
    upper = inside != jnp.where(core == 0, 1, 0)
    token = jnp.where(upper, token + 4 * size * q_cols, token)
    return jnp.where(token < bound, 1.0, -1.0)


def normed_heads(part, gain):
    count = part.shape[1]
    heads = part.reshape(-1, HD, count)
    factor = lax.rsqrt(jnp.mean(heads * heads, axis=1, keepdims=True) + 1e-06)
    return heads * factor * gain[None, :, :count]


def attend(tokens, sides, folded, key_gain, queries, acc_ref, keys_ref, values_ref, scores_ref, weights_ref):
    count = tokens.shape[0]
    row = lax.broadcasted_iota(jnp.int32, (8, count), 0)
    key_tail = jnp.where(row == 0, sides, jnp.where(row == 1, 1.0, 0.0))
    value_tail = jnp.where(row == 0, 1.0, 0.0)
    heads_at_once = 4
    for first in range(0, HEADS, heads_at_once):
        rows = slice(first * HD, (first + heads_at_once) * HD)
        part = lax.dot_general(folded[rows], tokens, NT, preferred_element_type=F32)
        keys = normed_heads(part, key_gain)
        for h in range(heads_at_once):
            keys_ref[first + h] = jnp.concatenate([keys[h], key_tail], axis=0).astype(BF16)
            scores_ref[first + h] = jnp.dot(queries[first + h], keys_ref[first + h], preferred_element_type=F32)
    for first in range(0, HEADS, heads_at_once):
        rows = slice(D + first * HD, D + (first + heads_at_once) * HD)
        part = lax.dot_general(folded[rows], tokens, NT, preferred_element_type=F32)
        values = part.reshape(heads_at_once, HD, count)
        for h in range(heads_at_once):
            values_ref[first + h] = jnp.concatenate([values[h], value_tail], axis=0).astype(BF16)
    lane = lax.broadcasted_iota(jnp.int32, (128, 128), 1)
    peaks = jnp.zeros((128, 128), F32)
    for h in range(HEADS):
        scores = scores_ref[h]
        peak = jnp.max(scores, axis=1, keepdims=True)
        weights_ref[h] = jnp.exp2(scores - peak).astype(BF16)
        peaks = jnp.where(lane == h, peak, peaks)
    peaks = peaks.T
    tail_row = lax.broadcasted_iota(jnp.int32, (8, 128), 0)
    for h in range(HEADS):
        mixed = lax.dot_general(values_ref[h], weights_ref[h], NT, preferred_element_type=F32)
        acc_ref[h, :HD] = mixed[:HD]
        acc_ref[h, HD:] = jnp.where(tail_row == 1, peaks[h : h + 1], mixed[HD:])


def attend_scratch(count):
    return [
        pltpu.VMEM((HEADS, SLOT, count), BF16),
        pltpu.VMEM((HEADS, SLOT, count), BF16),
        pltpu.VMEM((HEADS, 128, count), F32),
        pltpu.VMEM((HEADS, 128, count), BF16),
    ]


def query_kernel(lengths_ref, block_ref, centered_ref, query_ref, query_gain_ref, queries_ref):
    normed = jnp.dot(block_ref[...], centered_ref[...], preferred_element_type=F32).astype(BF16)
    part = jnp.dot(normed, query_ref[...], preferred_element_type=F32).T
    count = part.shape[1]
    sides = window_sides(lengths_ref, lax.axis_index("seq") // 2, count)
    queries = normed_heads(part, query_gain_ref[...])
    row = lax.broadcasted_iota(jnp.int32, (8, count), 0)
    tail = jnp.where(row == 0, MASK * sides, jnp.where(row == 1, -MASK, 0.0))
    for h in range(HEADS):
        queries_ref[h] = jnp.concatenate([queries[h], tail], axis=0).T.astype(BF16)


def make_queries(lengths, block, centered, query_weight, query_gain):
    return pl.pallas_call(
        query_kernel,
        out_shape=jax.ShapeDtypeStruct((HEADS, 128, SLOT), BF16),
        in_specs=[SMEM] + [VMEM] * 4,
        out_specs=VMEM,
        compiler_params=params(),
        name="queries",
        cost_estimate=pl.CostEstimate(flops=1 << 30, bytes_accessed=4 << 20, transcendentals=0),
    )(lengths, block, centered, query_weight, query_gain)


def step_kernel(offsets, lengths_ref, *refs):
    blocks = refs[: len(offsets)]
    folded_ref, key_gain_ref, queries_ref, acc_ref, *scratch = refs[len(offsets) :]
    place = ring_place()
    tokens = jnp.concatenate([ref[...] for ref in blocks], axis=0)
    sides = jnp.concatenate(
        [window_sides(lengths_ref, chip_at(place + offset), 128) for offset in dict.fromkeys(offsets)], axis=1
    )
    attend(tokens, sides, folded_ref, key_gain_ref[...], queries_ref, acc_ref, *scratch)


ACC = jax.ShapeDtypeStruct((HEADS, SLOT, 128), F32)


def step_attention(offsets, lengths, blocks, folded, key_gain, queries):
    count = sum(block.shape[0] for block in blocks)
    flops = 2 * count * 2 * D * 512 + 4 * HEADS * 128 * 128 * count
    return pl.pallas_call(
        functools.partial(step_kernel, offsets),
        out_shape=ACC,
        in_specs=[SMEM] + [VMEM] * (len(blocks) + 3),
        out_specs=VMEM,
        scratch_shapes=attend_scratch(count),
        compiler_params=params(),
        name="step_attention",
        cost_estimate=pl.CostEstimate(flops=2 * flops, bytes_accessed=5 << 20, transcendentals=HEADS * 128 * count),
    )(lengths, *blocks, folded, key_gain, queries)


RING = (0, -1, 1, -2, 2, -3, 3, 4)


def out_kernel(parts, *refs):
    acc_refs = refs[:parts]
    weight_refs = refs[parts:-3]
    keep_ref, send_ref, mixed_ref = refs[-3:]
    for h in range(HEADS):
        peaks = [acc[h, HD + 1 : HD + 2] for acc in acc_refs]
        peak = functools.reduce(jnp.maximum, peaks)
        total = None
        for acc, own in zip(acc_refs, peaks):
            term = acc[h] * jnp.exp2(own - peak)
            total = term if total is None else total + term
        mixed_ref[h] = total[:HD] / total[HD : HD + 1]
    place = ring_place()
    core = lax.axis_index("seq") % 2
    lefts = []
    for side in range(2):
        heads = [2 * chip_at(place + offset) + jnp.where(core == side, 0, 1) for offset in RING]
        lefts.append(jnp.concatenate([mixed_ref[head] for head in heads], axis=0).T.astype(BF16))
    half = keep_ref.shape[0]
    for first in range(0, D, 256):
        columns = slice(first, min(first + 256, D))
        result = jnp.dot(lefts[0], weight_refs[0][:, columns], preferred_element_type=F32)
        result = result + jnp.dot(lefts[1], weight_refs[1][:, columns], preferred_element_type=F32)
        result = result.astype(BF16)
        keep_ref[:, columns] = result[:half]
        send_ref[:, columns] = result[half:]


def project_out(accs, weights):
    out = jax.ShapeDtypeStruct((64, D), BF16)
    return pl.pallas_call(
        functools.partial(out_kernel, len(accs)),
        out_shape=(out, out),
        in_specs=[VMEM] * (len(accs) + len(weights)),
        out_specs=(VMEM, VMEM),
        scratch_shapes=[pltpu.VMEM((HEADS, HD, 128), F32)],
        compiler_params=params(),
        name="project_out",
        cost_estimate=pl.CostEstimate(flops=2 * 128 * 1280 * D, bytes_accessed=4 << 20, transcendentals=0),
    )(*accs, *weights)


def merge_kernel(lengths_ref, keep_ref, got_ref, out_ref):
    position = lax.axis_index("seq")
    keep = keep_ref[...].astype(F32)
    got = got_ref[...].astype(F32)
    start, _ = long_window(lengths_ref)
    q_cols = 16
    slot = lax.broadcasted_iota(jnp.int32, keep.shape, 0)
    token = (slot // q_cols) * (lax.axis_size("seq") * q_cols) + position * q_cols + slot % q_cols
    inside = jnp.where(token >= start, 1, 0)
    mine = inside == jnp.where(position % 2 == 0, 1, 0)
    half = keep.shape[0]
    out_ref[:half] = jnp.where(mine, keep, got).astype(BF16)
    out_ref[half:] = jnp.where(mine, got, keep).astype(BF16)


def merge(lengths, keep, got):
    return pl.pallas_call(
        merge_kernel,
        out_shape=jax.ShapeDtypeStruct((128, D), BF16),
        in_specs=[SMEM, VMEM, VMEM],
        out_specs=VMEM,
        compiler_params=params(),
        name="merge",
    )(lengths, keep, got)


def shards(
    clip, frame_counts, conv_first, conv_second, patch_weight, qkv_weight, query_gain, key_gain,
    out_weight, window_lengths,
):
    size = lax.axis_size("seq")
    up = [(i, i + 1) for i in range(size - 1)]
    down = [(j, i) for i, j in up]
    cores = [(i, i ^ 1) for i in range(size)]
    forward = ring_pairs()
    backward = [(j, i) for i, j in forward]

    def send(array, pairs):
        return lax.ppermute(array, "seq", pairs)

    def tied(*arrays):
        return lax.optimization_barrier(arrays)

    def tied(*arrays):
        return lax.optimization_barrier(arrays)

    def both_ways(ahead, behind):
        return send(ahead, forward), send(behind, backward)

    before = send(clip, up)
    after = send(clip, down)
    score_scale = math.log2(math.e) / math.sqrt(HD)
    query_rows = jnp.broadcast_to((query_gain * score_scale)[:, None], (HD, 128))
    key_rows = jnp.broadcast_to(key_gain[:, None], (HD, 256))
    weight_one = both_ways(out_weight, out_weight)
    pairs_one, pairs_two, patch, centered = prepare(patch_weight, conv_first, conv_second)
    before, after, *weight_one, pairs_one, query_rows, key_rows = tied(
        before, after, *weight_one, pairs_one, query_rows, key_rows
    )
    weight_two = both_ways(*weight_one)
    keep, other = convolve(
        frame_counts, window_lengths, clip, before, after, pairs_one, pairs_two, patch
    )
    got = send(other, cores)
    got, *weight_two = tied(got, *weight_two)
    block = jnp.concatenate([keep, got], axis=0)
    one = both_ways(block, block)
    weight_three = both_ways(*weight_two)
    folded, query_weight = fold(tied(centered, block)[0], qkv_weight)
    *one, folded, = tied(*one, folded)
    *one, weight_three_a, weight_three_b = tied(*one, *weight_three)
    two = both_ways(*one)
    cut = 40
    weight_four = both_ways(weight_three_a[:cut], weight_three_b[cut:])
    queries = make_queries(window_lengths, block, centered, query_weight, query_rows)
    acc_one = step_attention((-1, 1), window_lengths, one, folded, key_rows, queries)
    *two, acc_one = tied(*two, acc_one)
    three = both_ways(*two)
    acc_two = step_attention((-2, 2), window_lengths, two, folded, key_rows, queries)
    *three, acc_two, wf_a, wf_b = tied(*three, acc_two, *weight_four)
    weights = jnp.concatenate(
        [out_weight, *weight_one, *weight_two, weight_three_a, weight_three_b, wf_a, wf_b], axis=0
    )
    four = both_ways(three[0][:64], three[1][64:])
    sibling = send(weights, cores)
    acc_three = step_attention((-3, 3), window_lengths, three, folded, key_rows, queries)
    *four, acc_three = tied(*four, acc_three)
    acc_four = step_attention((0, 4, 4), window_lengths, [block, *four], folded, key_rows, queries)
    keep_rows, send_rows = project_out((acc_one, acc_two, acc_three, acc_four), (weights, sibling))
    return merge(window_lengths, keep_rows, send(send_rows, cores))


def solution(mesh):
    own = mesh.shape["seq"] == HEADS
    return jax.shard_map(
        shards if own else general_shards,
        mesh=mesh,
        in_specs=(
            P("groups", "seq", None, None),
            P("groups"),
            P(),
            P(),
            P(),
            P(),
            P(),
            P(),
            P("seq", None),
            P("groups", None),
        ),
        out_specs=P(("groups", "seq"), None),
        check_vma=False,
    )
```

```python
import functools
import math

import jax
import jax.numpy as jnp
from jax import lax
from jax.experimental import pallas as pl
from jax.experimental.pallas import tpu as pltpu
from jax.sharding import PartitionSpec as P

D = 1152
HEADS = 16


def extended(array, sides, width):
    for axis, dim in sides:
        size, length = (lax.axis_size(axis), array.shape[dim])
        up = [(i, (i + 1) % size) for i in range(size - 1)]
        down = [(j, i) for i, j in up]
        last = lax.slice_in_dim(array, length - width, length, axis=dim)
        first = lax.slice_in_dim(array, 0, width, axis=dim)
        before = lax.ppermute(last, axis, up)
        after = lax.ppermute(first, axis, down)
        array = jnp.concatenate([before, array, after], axis=dim)
    return array


def frame_weights(frame_counts, frames):
    position = jnp.arange(frames, dtype=jnp.int32)
    clip_ends = jnp.cumsum(frame_counts)

    def clip_of(index):
        return jnp.sum((index[:, None] >= clip_ends[None, :]).astype(jnp.int32), axis=1)

    own_clip = clip_of(position)
    columns = []
    for offset in (-1, 0, 1):
        neighbor = position + offset
        inside = (neighbor >= 0) & (neighbor < frames)
        same_clip = clip_of(jnp.clip(neighbor, 0, frames - 1)) == own_clip
        columns.append((inside & same_clip).astype(jnp.float32))
    return jnp.stack(columns, axis=1)


def convolve_rows(activation, kernel, tap_weights):
    empty_frame = jnp.zeros_like(activation[:1])
    shifted = (
        jnp.concatenate([empty_frame, activation[:-1]], 0),
        activation,
        jnp.concatenate([activation[1:], empty_frame], 0),
    )
    summed = None
    for offset in range(3):
        response = lax.conv_general_dilated(
            shifted[offset],
            kernel[offset],
            (1, 1),
            ((0, 0), (1, 1)),
            dimension_numbers=("NHWC", "HWIO", "NHWC"),
            preferred_element_type=jnp.float32,
        )
        tap_term = tap_weights[:, offset][:, None, None, None] * response
        summed = tap_term if offset == 0 else summed + tap_term
    return summed


def rms_scale(part, gain):
    factor = lax.rsqrt(jnp.mean(part * part, axis=-1, keepdims=True) + 1e-06)
    return (part * factor * gain).astype(jnp.bfloat16)


def general_shards(
    clip,
    frame_counts,
    conv_first,
    conv_second,
    patch_weight,
    qkv_weight,
    query_gain,
    key_gain,
    out_weight,
    window_lengths,
):
    frames, tile_rows, tile_cols, channels = clip.shape
    devices = lax.axis_size("seq")
    position = lax.axis_index("seq")
    head_dim = D // HEADS
    score_scale = 1.0 / math.sqrt(head_dim)
    tap_weights = frame_weights(frame_counts, frames)
    source = clip.astype(jnp.float32)
    padded_clip = extended(clip, (("seq", 1),), 2)
    first_in = jax.nn.silu(padded_clip.astype(jnp.float32)).astype(jnp.bfloat16)
    hidden_wide = convolve_rows(first_in, conv_first, tap_weights)
    global_row = position * tile_rows - 1 + jnp.arange(tile_rows + 2, dtype=jnp.int32)
    inside = ((global_row >= 0) & (global_row < tile_rows * devices)).astype(jnp.float32)
    hidden_one = (hidden_wide * inside[None, :, None, None]).astype(jnp.bfloat16)
    padded_second = jax.nn.silu(hidden_one.astype(jnp.float32)).astype(jnp.bfloat16)
    latent = (source + convolve_rows(padded_second, conv_second, tap_weights)).astype(jnp.bfloat16)
    token_rows = tile_rows // 2
    token_cols = tile_cols // 2
    patches = (
        latent.reshape(frames, token_rows, 2, token_cols, 2, channels)
        .transpose(0, 1, 3, 2, 4, 5)
        .reshape(-1, 4 * channels)
    )
    tok_count = patches.shape[0]
    embedded = jnp.dot(patches, patch_weight, preferred_element_type=jnp.float32).astype(
        jnp.bfloat16
    )
    values_f = embedded.astype(jnp.float32)
    row_mean = jnp.mean(values_f, axis=-1, keepdims=True)
    centered = values_f - row_mean
    variance = jnp.mean(centered * centered, axis=-1, keepdims=True)
    normed = (centered / jnp.sqrt(variance + 1e-06)).astype(jnp.bfloat16)
    projected = jnp.dot(normed, qkv_weight, preferred_element_type=jnp.float32).reshape(
        tok_count, 3, HEADS, head_dim
    )
    stacked = jnp.stack(
        [
            rms_scale(projected[:, 0], query_gain),
            rms_scale(projected[:, 1], key_gain),
            projected[:, 2].astype(jnp.bfloat16),
        ],
        axis=1,
    )
    groups = devices // HEADS
    frame_share = frames // groups
    local_share = tok_count // groups
    span_rows = devices * local_share
    outgoing = (
        stacked.reshape(groups, local_share, 3, HEADS, head_dim)
        .transpose(0, 3, 1, 2, 4)
        .reshape(devices, local_share, 3 * head_dim)
    )
    incoming = lax.all_to_all(outgoing, "seq", split_axis=0, concat_axis=0, tiled=True)
    arranged = (
        incoming.reshape(devices, frame_share, token_rows * token_cols, 3, head_dim)
        .transpose(3, 1, 0, 2, 4)
        .reshape(3, span_rows, head_dim)
    )
    my_group = position // HEADS
    lengths = lax.dynamic_index_in_dim(window_lengths, my_group, 0, keepdims=False)
    window_ends = jnp.cumsum(lengths)
    token_index = jnp.arange(span_rows, dtype=jnp.int32)
    segment = jnp.sum((token_index[:, None] >= window_ends[None, :]).astype(jnp.int32), axis=1)
    key_rows = arranged[1]
    value_rows = arranged[2]
    block_rows = min(512, span_rows)
    block_count = span_rows // block_rows

    def attend_block(inputs):
        query_block, segment_block = inputs
        scores = jnp.dot(query_block, key_rows.T, preferred_element_type=jnp.float32) * score_scale
        allowed = segment_block[:, None] == segment[None, :]
        scores = jnp.where(allowed, scores, -1e30)
        row_peak = jnp.max(scores, axis=-1, keepdims=True)
        weights = jnp.exp(scores - row_peak)
        row_mass = jnp.sum(weights, axis=-1, keepdims=True)
        mixed = (
            jnp.dot(weights.astype(jnp.bfloat16), value_rows, preferred_element_type=jnp.float32)
            / row_mass
        )
        return mixed.astype(jnp.bfloat16)

    mixed_rows = lax.map(
        attend_block,
        (
            arranged[0].reshape(block_count, block_rows, head_dim),
            segment.reshape(block_count, block_rows),
        ),
    ).reshape(span_rows, head_dim)
    outgoing_back = (
        mixed_rows.reshape(frame_share, devices, token_rows * token_cols, head_dim)
        .transpose(1, 0, 2, 3)
        .reshape(devices, local_share, head_dim)
    )
    returned = lax.all_to_all(outgoing_back, "seq", split_axis=0, concat_axis=0, tiled=True)
    merged = (
        returned.reshape(groups, HEADS, local_share, head_dim)
        .transpose(0, 2, 1, 3)
        .reshape(tok_count, D)
    )
    projected_out = jnp.dot(
        merged,
        lax.all_gather(out_weight, "seq", axis=0, tiled=True),
        preferred_element_type=jnp.float32,
    )
    return projected_out.astype(jnp.bfloat16)


HD = D // HEADS
SLOT = 80
MASK = 1024.0
F32 = jnp.float32
BF16 = jnp.bfloat16
VMEM = pl.BlockSpec(memory_space=pltpu.VMEM)
SMEM = pl.BlockSpec(memory_space=pltpu.SMEM)
NT = (((1,), (1,)), ((), ()))


def params(mib=40):
    return pltpu.CompilerParams(vmem_limit_bytes=mib << 20)


def silu(v):
    return v / (1.0 + jnp.exp(-v))


def long_window(lengths):
    first, second = lengths[0, 0], lengths[0, 1]
    half = 1024
    start = jnp.where(first == half, 0, jnp.where(second == half, first, first + second))
    bound = jnp.where(first == half, half + second, first)
    return start, bound


ANY = pl.BlockSpec(memory_space=pl.ANY)
TN = (((0,), (1,)), ((), ()))


def pair_weights(weights, o, ch=128):
    blank = jnp.zeros((ch, ch), BF16)
    rows = []
    for four in range(4):
        for j in range(3):
            taps = [weights[o, four - r, j] if 0 <= four - r < 3 else blank for r in range(2)]
            rows.append(jnp.concatenate(taps, axis=1))
    return jnp.concatenate(rows, axis=0)


def fold_kernel(patch_any, qkv_any, folded_ref, query_ref, centered_ref, patch_ref, qkv_ref, sems):
    copies = [
        pltpu.make_async_copy(patch_any, patch_ref, sems.at[0]),
        pltpu.make_async_copy(qkv_any.at[:, pl.ds(D, D)], qkv_ref.at[0], sems.at[1]),
        pltpu.make_async_copy(qkv_any.at[:, pl.ds(2 * D, D)], qkv_ref.at[1], sems.at[2]),
        pltpu.make_async_copy(qkv_any.at[:, pl.ds(0, D)], query_ref, sems.at[3]),
    ]
    for copy in copies:
        copy.start()
    copies[0].wait()
    patch = patch_ref[...].astype(F32)
    centered_ref[...] = (patch - jnp.mean(patch, axis=1, keepdims=True)).astype(BF16)
    for part in range(2):
        copies[part + 1].wait()
        product = lax.dot_general(qkv_ref[part], centered_ref[...], TN, preferred_element_type=F32)
        folded_ref[part * D : (part + 1) * D] = product.astype(BF16)
    copies[3].wait()


def fold(patch_weight, qkv_weight):
    inner = patch_weight.shape[0]
    return pl.pallas_call(
        fold_kernel,
        out_shape=(
            jax.ShapeDtypeStruct((2 * D, inner), BF16),
            jax.ShapeDtypeStruct((D, D), BF16),
            jax.ShapeDtypeStruct((inner, D), BF16),
        ),
        in_specs=[ANY, ANY],
        out_specs=(VMEM, VMEM, VMEM),
        scratch_shapes=[
            pltpu.VMEM((inner, D), BF16),
            pltpu.VMEM((2, D, D), BF16),
            pltpu.SemaphoreType.DMA((4,)),
        ],
        compiler_params=params(),
        name="fold",
        cost_estimate=pl.CostEstimate(flops=2 * inner * D * 2 * D, bytes_accessed=12 << 20, transcendentals=0),
    )(patch_weight, qkv_weight)


def frame_taps(counts_ref, frames):
    def clip_of(frame):
        end = 0
        index = 0
        for c in range(counts_ref.shape[0]):
            end = end + counts_ref[c]
            index = index + jnp.where(frame >= end, 1, 0)
        return index

    own = [clip_of(f) for f in range(frames)]
    joined = [jnp.where(own[f] == own[f + 1], 1.0, 0.0) for f in range(frames - 1)]
    return [0.0] + joined, joined + [0.0]


def conv_kernel(
    counts_any, lengths_any, own_any, before_ref, after_ref, first_ref, second_ref, patch_ref,
    keep_ref, send_ref, grid_one, grid_two, pixels, own_ref, counts_ref, lengths_ref, sems,
):
    copies = [
        pltpu.make_async_copy(own_any, own_ref, sems.at[0]),
        pltpu.make_async_copy(counts_any, counts_ref, sems.at[1]),
        pltpu.make_async_copy(lengths_any, lengths_ref, sems.at[2]),
    ]
    for copy in copies:
        copy.start()
    frames, _, cols, ch = own_ref.shape
    wide = 12 * ch
    position = lax.axis_index("seq")
    column = lax.broadcasted_iota(jnp.int32, (frames, cols, ch), 1)

    def shifted(row):
        left = jnp.where(column == 0, 0.0, pltpu.roll(row, 1, 1))
        right = jnp.where(column == cols - 1, 0.0, pltpu.roll(row, cols - 1, 1))
        return [part.astype(BF16) for part in (left, row, right)]

    blank = jnp.zeros((cols, wide), BF16)
    for g in range(2):
        grid_one[g, 0] = blank
        grid_one[g, frames + 1] = blank
    grid_two[0] = blank
    grid_two[frames + 1] = blank
    sources = [before_ref, before_ref, own_ref, own_ref, after_ref, after_ref]
    for r in (0, 1, 4, 5, 2, 3):
        if r == 2:
            copies[0].wait()
        row = silu(sources[r][:, r % 2].astype(F32))
        parts = shifted(row)
        for g in range(2):
            four = r - 2 * g
            if 0 <= four < 4:
                for j in range(3):
                    grid_one[g, 1 : frames + 1, :, (four * 3 + j) * ch : (four * 3 + j + 1) * ch] = parts[j]

    copies[1].wait()
    copies[2].wait()
    before_tap, after_tap = frame_taps(counts_ref, frames)

    def summed(terms):
        rows = []
        for f in range(frames):
            total = terms[1][f]
            if f > 0:
                total = total + before_tap[f] * terms[0][f]
            if f < frames - 1:
                total = total + after_tap[f] * terms[2][f]
            rows.append(total)
        return jnp.stack(rows)

    for g in range(2):
        terms = []
        for o in range(3):
            left = grid_one[g, o : o + frames].reshape(frames * cols, wide)
            terms.append(
                jnp.dot(left, pair_weights(first_ref, o), preferred_element_type=F32).reshape(frames, cols, 2 * ch)
            )
        hidden = summed(terms)
        for out_row in range(2):
            four = 2 * g + out_row
            row = hidden[:, :, out_row * ch : (out_row + 1) * ch]
            if four == 0:
                row = row * jnp.where(position == 0, 0.0, 1.0)
            if four == 3:
                row = row * jnp.where(position == lax.axis_size("seq") - 1, 0.0, 1.0)
            row = silu(row.astype(BF16).astype(F32))
            parts = shifted(row)
            for j in range(3):
                grid_two[1 : frames + 1, :, (four * 3 + j) * ch : (four * 3 + j + 1) * ch] = parts[j]
    terms = []
    for o in range(3):
        left = grid_two[o : o + frames].reshape(frames * cols, wide)
        terms.append(
            jnp.dot(left, pair_weights(second_ref, o), preferred_element_type=F32).reshape(frames, cols, 2 * ch)
        )
    residual = summed(terms)
    for out_row in range(2):
        block = own_ref[:, out_row].astype(F32) + residual[:, :, out_row * ch : (out_row + 1) * ch]
        pixels[out_row] = block.astype(BF16).astype(F32).reshape(frames * cols, ch)
    tokens = frames * cols // 2
    patches = jnp.concatenate(
        [pixels[a, pl.ds(b, tokens, 2), :] for a in range(2) for b in range(2)], axis=1
    )
    embedded = jnp.dot(patches.astype(BF16), patch_ref[...], preferred_element_type=F32)
    centered = embedded - jnp.mean(embedded, axis=1, keepdims=True)
    variance = jnp.mean(centered * centered, axis=1, keepdims=True)
    scaled = patches * (1.0 / jnp.sqrt(variance + 1e-06))
    half = tokens // 2
    low, high = scaled[:half], scaled[half:]
    start, _ = long_window(lengths_ref)
    q_cols = cols // 2
    slot = lax.broadcasted_iota(jnp.int32, low.shape, 0)
    token = (slot // q_cols) * (lax.axis_size("seq") * q_cols) + position * q_cols + slot % q_cols
    inside = jnp.where(token >= start, 1, 0)
    mine = inside == jnp.where(position % 2 == 0, 1, 0)
    keep = jnp.where(mine, low, high).astype(BF16)
    send = jnp.where(mine, high, low).astype(BF16)
    keep_ref[...] = keep
    send_ref[...] = send


def convolve(counts, lengths, clip, before, after, conv_first, conv_second, patch_weight):
    frames, _, cols, ch = clip.shape
    tokens = frames * cols // 2
    out = jax.ShapeDtypeStruct((tokens // 2, 4 * ch), BF16)
    return pl.pallas_call(
        conv_kernel,
        out_shape=(out, out),
        in_specs=[ANY] * 3 + [VMEM] * 5,
        out_specs=(VMEM, VMEM),
        scratch_shapes=[
            pltpu.VMEM((2, frames + 2, cols, 12 * ch), BF16),
            pltpu.VMEM((frames + 2, cols, 12 * ch), BF16),
            pltpu.VMEM((2, frames * cols, ch), F32),
            pltpu.VMEM(clip.shape, BF16),
            pltpu.SMEM(counts.shape, jnp.int32),
            pltpu.SMEM(lengths.shape, jnp.int32),
            pltpu.SemaphoreType.DMA((3,)),
        ],
        compiler_params=params(),
        name="convolve",
        cost_estimate=pl.CostEstimate(flops=2 << 30, bytes_accessed=4 << 20, transcendentals=1 << 18),
    )(counts, lengths, clip, before, after, conv_first, conv_second, patch_weight)


def chip_at(place):
    chips = lax.axis_size("seq") // 2
    place = lax.rem(place + 2 * chips, chips)
    return jnp.where(place < chips // 2, 2 * place, 2 * (chips - 1 - place) + 1)


def ring_place():
    chips = lax.axis_size("seq") // 2
    chip = lax.axis_index("seq") // 2
    return jnp.where(chip % 2 == 0, chip // 2, chips - 1 - chip // 2)


def ring_pairs():
    size = lax.axis_size("seq")
    chips = size // 2
    order = [2 * i for i in range(chips // 2)] + [2 * i + 1 for i in reversed(range(chips // 2))]
    return [
        (2 * order[i] + core, 2 * order[(i + 1) % chips] + core) for i in range(chips) for core in range(2)
    ]


def window_sides(lengths_ref, chip, count):
    size = lax.axis_size("seq")
    core = lax.axis_index("seq") % 2
    start, bound = long_window(lengths_ref)
    lane = lax.broadcasted_iota(jnp.int32, (8, count), 1)
    half = count // 2
    slot = lane % half
    row = 2 * chip + jnp.where(lane < half, core, 1 - core)
    q_cols = 16
    token = (slot // q_cols) * (size * q_cols) + row * q_cols + slot % q_cols
    inside = jnp.where(token >= start, 1, 0)
    upper = inside != jnp.where(core == 0, 1, 0)
    token = jnp.where(upper, token + 4 * size * q_cols, token)
    return jnp.where(token < bound, 1.0, -1.0)


def normed_heads(part, gain):
    count = part.shape[1]
    heads = part.reshape(-1, HD, count)
    factor = lax.rsqrt(jnp.mean(heads * heads, axis=1, keepdims=True) + 1e-06)
    return heads * factor * gain[None]


def as_column(row):
    size = row.shape[1]
    square = (size, size)
    same = lax.broadcasted_iota(jnp.int32, square, 0) == lax.broadcasted_iota(jnp.int32, square, 1)
    return jnp.sum(jnp.where(same, jnp.broadcast_to(row, square), 0.0), axis=1, keepdims=True)


def attend(tokens, sides, folded, key_gain, queries, acc_ref, keys_ref, values_ref, scores_ref, weights_ref):
    count = tokens.shape[0]
    row = lax.broadcasted_iota(jnp.int32, (8, count), 0)
    key_tail = jnp.where(row == 0, sides, jnp.where(row == 1, 1.0, 0.0))
    value_tail = jnp.where(row == 0, 1.0, 0.0)
    heads_at_once = 4
    for first in range(0, HEADS, heads_at_once):
        rows = slice(first * HD, (first + heads_at_once) * HD)
        part = lax.dot_general(folded[rows], tokens, NT, preferred_element_type=F32)
        keys = normed_heads(part, key_gain)
        for h in range(heads_at_once):
            keys_ref[first + h] = jnp.concatenate([keys[h], key_tail], axis=0).astype(BF16)
            scores_ref[first + h] = jnp.dot(queries[first + h], keys_ref[first + h], preferred_element_type=F32)
    for first in range(0, HEADS, heads_at_once):
        rows = slice(D + first * HD, D + (first + heads_at_once) * HD)
        part = lax.dot_general(folded[rows], tokens, NT, preferred_element_type=F32)
        values = part.reshape(heads_at_once, HD, count)
        for h in range(heads_at_once):
            values_ref[first + h] = jnp.concatenate([values[h], value_tail], axis=0).astype(BF16)
    lane = lax.broadcasted_iota(jnp.int32, (128, 128), 1)
    peaks = jnp.zeros((128, 128), F32)
    for h in range(HEADS):
        scores = scores_ref[h]
        peak = jnp.max(scores, axis=1, keepdims=True)
        weights_ref[h] = jnp.exp2(scores - peak).astype(BF16)
        peaks = jnp.where(lane == h, peak, peaks)
    peaks = peaks.T
    tail_row = lax.broadcasted_iota(jnp.int32, (8, 128), 0)
    for h in range(HEADS):
        mixed = lax.dot_general(values_ref[h], weights_ref[h], NT, preferred_element_type=F32)
        acc_ref[h, :HD] = mixed[:HD]
        acc_ref[h, HD:] = jnp.where(tail_row == 1, peaks[h : h + 1], mixed[HD:])


def attend_scratch(count):
    return [
        pltpu.VMEM((HEADS, SLOT, count), BF16),
        pltpu.VMEM((HEADS, SLOT, count), BF16),
        pltpu.VMEM((HEADS, 128, count), F32),
        pltpu.VMEM((HEADS, 128, count), BF16),
    ]


def query_kernel(lengths_ref, block_ref, centered_ref, query_ref, query_gain_ref, queries_ref):
    normed = jnp.dot(block_ref[...], centered_ref[...], preferred_element_type=F32).astype(BF16)
    part = jnp.dot(normed, query_ref[...], preferred_element_type=F32).T
    count = part.shape[1]
    sides = window_sides(lengths_ref, lax.axis_index("seq") // 2, count)
    queries = normed_heads(part, as_column(query_gain_ref[...] * (math.log2(math.e) / math.sqrt(HD))))
    row = lax.broadcasted_iota(jnp.int32, (8, count), 0)
    tail = jnp.where(row == 0, MASK * sides, jnp.where(row == 1, -MASK, 0.0))
    for h in range(HEADS):
        queries_ref[h] = jnp.concatenate([queries[h], tail], axis=0).T.astype(BF16)


def make_queries(lengths, block, centered, query_weight, query_gain):
    return pl.pallas_call(
        query_kernel,
        out_shape=jax.ShapeDtypeStruct((HEADS, 128, SLOT), BF16),
        in_specs=[SMEM] + [VMEM] * 4,
        out_specs=VMEM,
        compiler_params=params(),
        name="queries",
        cost_estimate=pl.CostEstimate(flops=1 << 30, bytes_accessed=4 << 20, transcendentals=0),
    )(lengths, block, centered, query_weight, query_gain)


def step_kernel(offsets, lengths_ref, *refs):
    blocks = refs[: len(offsets)]
    folded_ref, key_gain_ref, queries_ref, acc_ref, *scratch = refs[len(offsets) :]
    place = ring_place()
    tokens = jnp.concatenate([ref[...] for ref in blocks], axis=0)
    sides = jnp.concatenate(
        [window_sides(lengths_ref, chip_at(place + offset), 128) for offset in dict.fromkeys(offsets)], axis=1
    )
    attend(tokens, sides, folded_ref, as_column(key_gain_ref[...]), queries_ref, acc_ref, *scratch)


ACC = jax.ShapeDtypeStruct((HEADS, SLOT, 128), F32)


def step_attention(offsets, lengths, blocks, folded, key_gain, queries):
    count = sum(block.shape[0] for block in blocks)
    flops = 2 * count * 2 * D * 512 + 4 * HEADS * 128 * 128 * count
    return pl.pallas_call(
        functools.partial(step_kernel, offsets),
        out_shape=ACC,
        in_specs=[SMEM] + [VMEM] * (len(blocks) + 3),
        out_specs=VMEM,
        scratch_shapes=attend_scratch(count),
        compiler_params=params(),
        name="step_attention",
        cost_estimate=pl.CostEstimate(flops=2 * flops, bytes_accessed=5 << 20, transcendentals=HEADS * 128 * count),
    )(lengths, *blocks, folded, key_gain, queries)


RING = (0, -1, 1, -2, 2, -3, 3, 4)


def out_kernel(parts, *refs):
    acc_refs = refs[:parts]
    weight_refs = refs[parts:-3]
    keep_ref, send_ref, mixed_ref = refs[-3:]
    for h in range(HEADS):
        peaks = [acc[h, HD + 1 : HD + 2] for acc in acc_refs]
        peak = functools.reduce(jnp.maximum, peaks)
        total = None
        for acc, own in zip(acc_refs, peaks):
            term = acc[h] * jnp.exp2(own - peak)
            total = term if total is None else total + term
        mixed_ref[h] = total[:HD] / total[HD : HD + 1]
    place = ring_place()
    core = lax.axis_index("seq") % 2
    lefts = []
    for side in range(2):
        heads = [2 * chip_at(place + offset) + jnp.where(core == side, 0, 1) for offset in RING]
        lefts.append(jnp.concatenate([mixed_ref[head] for head in heads], axis=0).T.astype(BF16))
    half = keep_ref.shape[0]
    for first in range(0, D, 256):
        columns = slice(first, min(first + 256, D))
        result = jnp.dot(lefts[0], weight_refs[0][:, columns], preferred_element_type=F32)
        result = result + jnp.dot(lefts[1], weight_refs[1][:, columns], preferred_element_type=F32)
        result = result.astype(BF16)
        keep_ref[:, columns] = result[:half]
        send_ref[:, columns] = result[half:]


def project_out(accs, weights):
    out = jax.ShapeDtypeStruct((64, D), BF16)
    return pl.pallas_call(
        functools.partial(out_kernel, len(accs)),
        out_shape=(out, out),
        in_specs=[VMEM] * (len(accs) + len(weights)),
        out_specs=(VMEM, VMEM),
        scratch_shapes=[pltpu.VMEM((HEADS, HD, 128), F32)],
        compiler_params=params(),
        name="project_out",
        cost_estimate=pl.CostEstimate(flops=2 * 128 * 1280 * D, bytes_accessed=4 << 20, transcendentals=0),
    )(*accs, *weights)


def pack_kernel(*refs):
    out_ref = refs[-1]
    for i in range(7):
        out_ref[i] = refs[i][...]
    cut = refs[7].shape[1]
    out_ref[7, :, :cut] = refs[7][...]
    out_ref[7, :, cut:] = refs[8][...]


def pack(pieces):
    rows, columns = pieces[0].shape
    out = pl.pallas_call(
        pack_kernel,
        out_shape=jax.ShapeDtypeStruct((8, rows, columns), BF16),
        in_specs=[VMEM] * 9,
        out_specs=VMEM,
        compiler_params=params(),
        name="pack",
    )(*pieces)
    return out.reshape(8 * rows, columns)


def merge_kernel(lengths_ref, keep_ref, got_ref, out_ref):
    position = lax.axis_index("seq")
    keep = keep_ref[...].astype(F32)
    got = got_ref[...].astype(F32)
    start, _ = long_window(lengths_ref)
    q_cols = 16
    slot = lax.broadcasted_iota(jnp.int32, keep.shape, 0)
    token = (slot // q_cols) * (lax.axis_size("seq") * q_cols) + position * q_cols + slot % q_cols
    inside = jnp.where(token >= start, 1, 0)
    mine = inside == jnp.where(position % 2 == 0, 1, 0)
    half = keep.shape[0]
    out_ref[:half] = jnp.where(mine, keep, got).astype(BF16)
    out_ref[half:] = jnp.where(mine, got, keep).astype(BF16)


def merge(lengths, keep, got):
    return pl.pallas_call(
        merge_kernel,
        out_shape=jax.ShapeDtypeStruct((128, D), BF16),
        in_specs=[SMEM, VMEM, VMEM],
        out_specs=VMEM,
        compiler_params=params(),
        name="merge",
    )(lengths, keep, got)


def shards(
    clip, frame_counts, conv_first, conv_second, patch_weight, qkv_weight, query_gain, key_gain,
    out_weight, window_lengths,
):
    size = lax.axis_size("seq")
    up = [(i, i + 1) for i in range(size - 1)]
    down = [(j, i) for i, j in up]
    cores = [(i, i ^ 1) for i in range(size)]
    forward = ring_pairs()
    backward = [(j, i) for i, j in forward]

    def send(array, pairs):
        return lax.ppermute(array, "seq", pairs)

    def tied(*arrays):
        return lax.optimization_barrier(arrays)

    def tied(*arrays):
        return lax.optimization_barrier(arrays)

    def both_ways(ahead, behind):
        return send(ahead, forward), send(behind, backward)

    def tied(*arrays):
        return lax.optimization_barrier(arrays)

    def both_ways(ahead, behind):
        return send(ahead, forward), send(behind, backward)

    before = send(clip, up)
    after = send(clip, down)
    query_row, key_row = query_gain[None], key_gain[None]
    weight_one = both_ways(out_weight, out_weight)
    folded, query_weight, centered = fold(patch_weight, qkv_weight)
    before, after, *weight_one, folded = tied(before, after, *weight_one, folded)
    weight_two = both_ways(*weight_one)
    keep, other = convolve(
        frame_counts, window_lengths, clip, before, after, conv_first, conv_second, patch_weight
    )
    got = send(other, cores)
    block = jnp.concatenate([keep, got], axis=0)
    one = both_ways(block, block)
    queries = make_queries(window_lengths, block, centered, query_weight, query_row)
    *one, queries, wu_a, wu_b = tied(*one, queries, *weight_two)
    weight_two = (wu_a, wu_b)
    two = both_ways(*one)
    weight_three = both_ways(*weight_two)
    acc_one = step_attention((-1, 1), window_lengths, one, folded, key_row, queries)
    *two, acc_one, wt_a, wt_b = tied(*two, acc_one, *weight_three)
    three = both_ways(*two)
    cut = 640
    weight_four = both_ways(wt_a[:, :cut], wt_b[:, cut:])
    acc_two = step_attention((-2, 2), window_lengths, two, folded, key_row, queries)
    *three, acc_two, wf_a, wf_b = tied(*three, acc_two, *weight_four)
    four = both_ways(three[0][:64], three[1][64:])
    weights = pack([out_weight, *weight_one, *weight_two, wt_a, wt_b, wf_a, wf_b])
    sibling = send(weights, cores)
    acc_three = step_attention((-3, 3), window_lengths, three, folded, key_row, queries)
    *four, acc_three = tied(*four, acc_three)
    acc_four = step_attention((0, 4, 4), window_lengths, [block, *four], folded, key_row, queries)
    keep_rows, send_rows = project_out((acc_one, acc_two, acc_three, acc_four), (weights, sibling))
    return merge(window_lengths, keep_rows, send(send_rows, cores))


def solution(mesh):
    own = mesh.shape["seq"] == HEADS
    return jax.shard_map(
        shards if own else general_shards,
        mesh=mesh,
        in_specs=(
            P("groups", "seq", None, None),
            P("groups"),
            P(),
            P(),
            P(),
            P(),
            P(),
            P(),
            P("seq", None),
            P("groups", None),
        ),
        out_specs=P(("groups", "seq"), None),
        check_vma=False,
    )
```

```python
import functools
import math

import jax
import jax.numpy as jnp
from jax import lax
from jax.experimental import pallas as pl
from jax.experimental.pallas import tpu as pltpu
from jax.sharding import PartitionSpec as P

D = 1152
HEADS = 16


def extended(array, sides, width):
    for axis, dim in sides:
        size, length = (lax.axis_size(axis), array.shape[dim])
        up = [(i, (i + 1) % size) for i in range(size - 1)]
        down = [(j, i) for i, j in up]
        last = lax.slice_in_dim(array, length - width, length, axis=dim)
        first = lax.slice_in_dim(array, 0, width, axis=dim)
        before = lax.ppermute(last, axis, up)
        after = lax.ppermute(first, axis, down)
        array = jnp.concatenate([before, array, after], axis=dim)
    return array


def frame_weights(frame_counts, frames):
    position = jnp.arange(frames, dtype=jnp.int32)
    clip_ends = jnp.cumsum(frame_counts)

    def clip_of(index):
        return jnp.sum((index[:, None] >= clip_ends[None, :]).astype(jnp.int32), axis=1)

    own_clip = clip_of(position)
    columns = []
    for offset in (-1, 0, 1):
        neighbor = position + offset
        inside = (neighbor >= 0) & (neighbor < frames)
        same_clip = clip_of(jnp.clip(neighbor, 0, frames - 1)) == own_clip
        columns.append((inside & same_clip).astype(jnp.float32))
    return jnp.stack(columns, axis=1)


def convolve_rows(activation, kernel, tap_weights):
    empty_frame = jnp.zeros_like(activation[:1])
    shifted = (
        jnp.concatenate([empty_frame, activation[:-1]], 0),
        activation,
        jnp.concatenate([activation[1:], empty_frame], 0),
    )
    summed = None
    for offset in range(3):
        response = lax.conv_general_dilated(
            shifted[offset],
            kernel[offset],
            (1, 1),
            ((0, 0), (1, 1)),
            dimension_numbers=("NHWC", "HWIO", "NHWC"),
            preferred_element_type=jnp.float32,
        )
        tap_term = tap_weights[:, offset][:, None, None, None] * response
        summed = tap_term if offset == 0 else summed + tap_term
    return summed


def rms_scale(part, gain):
    factor = lax.rsqrt(jnp.mean(part * part, axis=-1, keepdims=True) + 1e-06)
    return (part * factor * gain).astype(jnp.bfloat16)


def general_shards(
    clip,
    frame_counts,
    conv_first,
    conv_second,
    patch_weight,
    qkv_weight,
    query_gain,
    key_gain,
    out_weight,
    window_lengths,
):
    frames, tile_rows, tile_cols, channels = clip.shape
    devices = lax.axis_size("seq")
    position = lax.axis_index("seq")
    head_dim = D // HEADS
    score_scale = 1.0 / math.sqrt(head_dim)
    tap_weights = frame_weights(frame_counts, frames)
    source = clip.astype(jnp.float32)
    padded_clip = extended(clip, (("seq", 1),), 2)
    first_in = jax.nn.silu(padded_clip.astype(jnp.float32)).astype(jnp.bfloat16)
    hidden_wide = convolve_rows(first_in, conv_first, tap_weights)
    global_row = position * tile_rows - 1 + jnp.arange(tile_rows + 2, dtype=jnp.int32)
    inside = ((global_row >= 0) & (global_row < tile_rows * devices)).astype(jnp.float32)
    hidden_one = (hidden_wide * inside[None, :, None, None]).astype(jnp.bfloat16)
    padded_second = jax.nn.silu(hidden_one.astype(jnp.float32)).astype(jnp.bfloat16)
    latent = (source + convolve_rows(padded_second, conv_second, tap_weights)).astype(jnp.bfloat16)
    token_rows = tile_rows // 2
    token_cols = tile_cols // 2
    patches = (
        latent.reshape(frames, token_rows, 2, token_cols, 2, channels)
        .transpose(0, 1, 3, 2, 4, 5)
        .reshape(-1, 4 * channels)
    )
    tok_count = patches.shape[0]
    embedded = jnp.dot(patches, patch_weight, preferred_element_type=jnp.float32).astype(
        jnp.bfloat16
    )
    values_f = embedded.astype(jnp.float32)
    row_mean = jnp.mean(values_f, axis=-1, keepdims=True)
    centered = values_f - row_mean
    variance = jnp.mean(centered * centered, axis=-1, keepdims=True)
    normed = (centered / jnp.sqrt(variance + 1e-06)).astype(jnp.bfloat16)
    projected = jnp.dot(normed, qkv_weight, preferred_element_type=jnp.float32).reshape(
        tok_count, 3, HEADS, head_dim
    )
    stacked = jnp.stack(
        [
            rms_scale(projected[:, 0], query_gain),
            rms_scale(projected[:, 1], key_gain),
            projected[:, 2].astype(jnp.bfloat16),
        ],
        axis=1,
    )
    groups = devices // HEADS
    frame_share = frames // groups
    local_share = tok_count // groups
    span_rows = devices * local_share
    outgoing = (
        stacked.reshape(groups, local_share, 3, HEADS, head_dim)
        .transpose(0, 3, 1, 2, 4)
        .reshape(devices, local_share, 3 * head_dim)
    )
    incoming = lax.all_to_all(outgoing, "seq", split_axis=0, concat_axis=0, tiled=True)
    arranged = (
        incoming.reshape(devices, frame_share, token_rows * token_cols, 3, head_dim)
        .transpose(3, 1, 0, 2, 4)
        .reshape(3, span_rows, head_dim)
    )
    my_group = position // HEADS
    lengths = lax.dynamic_index_in_dim(window_lengths, my_group, 0, keepdims=False)
    window_ends = jnp.cumsum(lengths)
    token_index = jnp.arange(span_rows, dtype=jnp.int32)
    segment = jnp.sum((token_index[:, None] >= window_ends[None, :]).astype(jnp.int32), axis=1)
    key_rows = arranged[1]
    value_rows = arranged[2]
    block_rows = min(512, span_rows)
    block_count = span_rows // block_rows

    def attend_block(inputs):
        query_block, segment_block = inputs
        scores = jnp.dot(query_block, key_rows.T, preferred_element_type=jnp.float32) * score_scale
        allowed = segment_block[:, None] == segment[None, :]
        scores = jnp.where(allowed, scores, -1e30)
        row_peak = jnp.max(scores, axis=-1, keepdims=True)
        weights = jnp.exp(scores - row_peak)
        row_mass = jnp.sum(weights, axis=-1, keepdims=True)
        mixed = (
            jnp.dot(weights.astype(jnp.bfloat16), value_rows, preferred_element_type=jnp.float32)
            / row_mass
        )
        return mixed.astype(jnp.bfloat16)

    mixed_rows = lax.map(
        attend_block,
        (
            arranged[0].reshape(block_count, block_rows, head_dim),
            segment.reshape(block_count, block_rows),
        ),
    ).reshape(span_rows, head_dim)
    outgoing_back = (
        mixed_rows.reshape(frame_share, devices, token_rows * token_cols, head_dim)
        .transpose(1, 0, 2, 3)
        .reshape(devices, local_share, head_dim)
    )
    returned = lax.all_to_all(outgoing_back, "seq", split_axis=0, concat_axis=0, tiled=True)
    merged = (
        returned.reshape(groups, HEADS, local_share, head_dim)
        .transpose(0, 2, 1, 3)
        .reshape(tok_count, D)
    )
    projected_out = jnp.dot(
        merged,
        lax.all_gather(out_weight, "seq", axis=0, tiled=True),
        preferred_element_type=jnp.float32,
    )
    return projected_out.astype(jnp.bfloat16)


HD = D // HEADS
SLOT = 80
MASK = 1024.0
F32 = jnp.float32
BF16 = jnp.bfloat16
VMEM = pl.BlockSpec(memory_space=pltpu.VMEM)
SMEM = pl.BlockSpec(memory_space=pltpu.SMEM)
NT = (((1,), (1,)), ((), ()))


def params(mib=40):
    return pltpu.CompilerParams(vmem_limit_bytes=mib << 20)


def silu(v):
    return v / (1.0 + jnp.exp(-v))


def long_window(lengths):
    first, second = lengths[0, 0], lengths[0, 1]
    half = 1024
    start = jnp.where(first == half, 0, jnp.where(second == half, first, first + second))
    bound = jnp.where(first == half, half + second, first)
    return start, bound


ANY = pl.BlockSpec(memory_space=pl.ANY)
TN = (((0,), (1,)), ((), ()))


def pair_weights(weights, o, ch=128):
    blank = jnp.zeros((ch, ch), BF16)
    rows = []
    for four in range(4):
        for j in range(3):
            taps = [weights[o, four - r, j] if 0 <= four - r < 3 else blank for r in range(2)]
            rows.append(jnp.concatenate(taps, axis=1))
    return jnp.concatenate(rows, axis=0)


def fold_kernel(patch_any, qkv_any, folded_ref, query_ref, centered_ref, patch_ref, qkv_ref, sems):
    copies = [
        pltpu.make_async_copy(patch_any, patch_ref, sems.at[0]),
        pltpu.make_async_copy(qkv_any.at[:, pl.ds(D, D)], qkv_ref.at[0], sems.at[1]),
        pltpu.make_async_copy(qkv_any.at[:, pl.ds(2 * D, D)], qkv_ref.at[1], sems.at[2]),
        pltpu.make_async_copy(qkv_any.at[:, pl.ds(0, D)], query_ref, sems.at[3]),
    ]
    for copy in copies:
        copy.start()
    copies[0].wait()
    patch = patch_ref[...].astype(F32)
    centered_ref[...] = (patch - jnp.mean(patch, axis=1, keepdims=True)).astype(BF16)
    for part in range(2):
        copies[part + 1].wait()
        product = lax.dot_general(qkv_ref[part], centered_ref[...], TN, preferred_element_type=F32)
        folded_ref[part * D : (part + 1) * D] = product.astype(BF16)
    copies[3].wait()


def fold(patch_weight, qkv_weight):
    inner = patch_weight.shape[0]
    return pl.pallas_call(
        fold_kernel,
        out_shape=(
            jax.ShapeDtypeStruct((2 * D, inner), BF16),
            jax.ShapeDtypeStruct((D, D), BF16),
            jax.ShapeDtypeStruct((inner, D), BF16),
        ),
        in_specs=[ANY, ANY],
        out_specs=(VMEM, VMEM, VMEM),
        scratch_shapes=[
            pltpu.VMEM((inner, D), BF16),
            pltpu.VMEM((2, D, D), BF16),
            pltpu.SemaphoreType.DMA((4,)),
        ],
        compiler_params=params(),
        name="fold",
        cost_estimate=pl.CostEstimate(flops=2 * inner * D * 2 * D, bytes_accessed=12 << 20, transcendentals=0),
    )(patch_weight, qkv_weight)


def frame_taps(counts_ref, frames):
    def clip_of(frame):
        end = 0
        index = 0
        for c in range(counts_ref.shape[0]):
            end = end + counts_ref[c]
            index = index + jnp.where(frame >= end, 1, 0)
        return index

    own = [clip_of(f) for f in range(frames)]
    joined = [jnp.where(own[f] == own[f + 1], 1.0, 0.0) for f in range(frames - 1)]
    return [0.0] + joined, joined + [0.0]


def conv_kernel(
    counts_any, lengths_any, own_any, before_ref, after_ref, first_ref, second_ref, patch_ref,
    keep_ref, send_ref, grid_one, grid_two, pixels, own_ref, counts_ref, lengths_ref, sems,
):
    copies = [
        pltpu.make_async_copy(own_any, own_ref, sems.at[0]),
        pltpu.make_async_copy(counts_any, counts_ref, sems.at[1]),
        pltpu.make_async_copy(lengths_any, lengths_ref, sems.at[2]),
    ]
    for copy in copies:
        copy.start()
    frames, _, cols, ch = own_ref.shape
    wide = 12 * ch
    position = lax.axis_index("seq")
    column = lax.broadcasted_iota(jnp.int32, (frames, cols, ch), 1)

    def shifted(row):
        left = jnp.where(column == 0, 0.0, pltpu.roll(row, 1, 1))
        right = jnp.where(column == cols - 1, 0.0, pltpu.roll(row, cols - 1, 1))
        return [part.astype(BF16) for part in (left, row, right)]

    blank = jnp.zeros((cols, wide), BF16)
    for g in range(2):
        grid_one[g, 0] = blank
        grid_one[g, frames + 1] = blank
    grid_two[0] = blank
    grid_two[frames + 1] = blank
    sources = [before_ref, before_ref, own_ref, own_ref, after_ref, after_ref]
    for r in (0, 1, 4, 5, 2, 3):
        if r == 2:
            copies[0].wait()
        row = silu(sources[r][:, r % 2].astype(F32))
        parts = shifted(row)
        for g in range(2):
            four = r - 2 * g
            if 0 <= four < 4:
                for j in range(3):
                    grid_one[g, 1 : frames + 1, :, (four * 3 + j) * ch : (four * 3 + j + 1) * ch] = parts[j]

    copies[1].wait()
    copies[2].wait()
    before_tap, after_tap = frame_taps(counts_ref, frames)

    def summed(terms):
        rows = []
        for f in range(frames):
            total = terms[1][f]
            if f > 0:
                total = total + before_tap[f] * terms[0][f]
            if f < frames - 1:
                total = total + after_tap[f] * terms[2][f]
            rows.append(total)
        return jnp.stack(rows)

    for g in range(2):
        terms = []
        for o in range(3):
            left = grid_one[g, o : o + frames].reshape(frames * cols, wide)
            terms.append(
                jnp.dot(left, pair_weights(first_ref, o), preferred_element_type=F32).reshape(frames, cols, 2 * ch)
            )
        hidden = summed(terms)
        for out_row in range(2):
            four = 2 * g + out_row
            row = hidden[:, :, out_row * ch : (out_row + 1) * ch]
            if four == 0:
                row = row * jnp.where(position == 0, 0.0, 1.0)
            if four == 3:
                row = row * jnp.where(position == lax.axis_size("seq") - 1, 0.0, 1.0)
            row = silu(row.astype(BF16).astype(F32))
            parts = shifted(row)
            for j in range(3):
                grid_two[1 : frames + 1, :, (four * 3 + j) * ch : (four * 3 + j + 1) * ch] = parts[j]
    terms = []
    for o in range(3):
        left = grid_two[o : o + frames].reshape(frames * cols, wide)
        terms.append(
            jnp.dot(left, pair_weights(second_ref, o), preferred_element_type=F32).reshape(frames, cols, 2 * ch)
        )
    residual = summed(terms)
    for out_row in range(2):
        block = own_ref[:, out_row].astype(F32) + residual[:, :, out_row * ch : (out_row + 1) * ch]
        pixels[out_row] = block.astype(BF16).astype(F32).reshape(frames * cols, ch)
    tokens = frames * cols // 2
    patches = jnp.concatenate(
        [pixels[a, pl.ds(b, tokens, 2), :] for a in range(2) for b in range(2)], axis=1
    )
    embedded = jnp.dot(patches.astype(BF16), patch_ref[...], preferred_element_type=F32)
    centered = embedded - jnp.mean(embedded, axis=1, keepdims=True)
    variance = jnp.mean(centered * centered, axis=1, keepdims=True)
    scaled = patches * (1.0 / jnp.sqrt(variance + 1e-06))
    half = tokens // 2
    low, high = scaled[:half], scaled[half:]
    start, _ = long_window(lengths_ref)
    q_cols = cols // 2
    slot = lax.broadcasted_iota(jnp.int32, low.shape, 0)
    token = (slot // q_cols) * (lax.axis_size("seq") * q_cols) + position * q_cols + slot % q_cols
    inside = jnp.where(token >= start, 1, 0)
    mine = inside == jnp.where(position % 2 == 0, 1, 0)
    keep = jnp.where(mine, low, high).astype(BF16)
    send = jnp.where(mine, high, low).astype(BF16)
    keep_ref[...] = keep
    send_ref[...] = send


def convolve(counts, lengths, clip, before, after, conv_first, conv_second, patch_weight):
    frames, _, cols, ch = clip.shape
    tokens = frames * cols // 2
    out = jax.ShapeDtypeStruct((tokens // 2, 4 * ch), BF16)
    return pl.pallas_call(
        conv_kernel,
        out_shape=(out, out),
        in_specs=[ANY] * 3 + [VMEM] * 5,
        out_specs=(VMEM, VMEM),
        scratch_shapes=[
            pltpu.VMEM((2, frames + 2, cols, 12 * ch), BF16),
            pltpu.VMEM((frames + 2, cols, 12 * ch), BF16),
            pltpu.VMEM((2, frames * cols, ch), F32),
            pltpu.VMEM(clip.shape, BF16),
            pltpu.SMEM(counts.shape, jnp.int32),
            pltpu.SMEM(lengths.shape, jnp.int32),
            pltpu.SemaphoreType.DMA((3,)),
        ],
        compiler_params=params(),
        name="convolve",
        cost_estimate=pl.CostEstimate(flops=2 << 30, bytes_accessed=4 << 20, transcendentals=1 << 18),
    )(counts, lengths, clip, before, after, conv_first, conv_second, patch_weight)


def chip_at(place):
    chips = lax.axis_size("seq") // 2
    place = lax.rem(place + 2 * chips, chips)
    return jnp.where(place < chips // 2, 2 * place, 2 * (chips - 1 - place) + 1)


def ring_place():
    chips = lax.axis_size("seq") // 2
    chip = lax.axis_index("seq") // 2
    return jnp.where(chip % 2 == 0, chip // 2, chips - 1 - chip // 2)


def ring_pairs():
    size = lax.axis_size("seq")
    chips = size // 2
    order = [2 * i for i in range(chips // 2)] + [2 * i + 1 for i in reversed(range(chips // 2))]
    return [
        (2 * order[i] + core, 2 * order[(i + 1) % chips] + core) for i in range(chips) for core in range(2)
    ]


def window_sides(lengths_ref, chip, count):
    size = lax.axis_size("seq")
    core = lax.axis_index("seq") % 2
    start, bound = long_window(lengths_ref)
    lane = lax.broadcasted_iota(jnp.int32, (8, count), 1)
    half = count // 2
    slot = lane % half
    row = 2 * chip + jnp.where(lane < half, core, 1 - core)
    q_cols = 16
    token = (slot // q_cols) * (size * q_cols) + row * q_cols + slot % q_cols
    inside = jnp.where(token >= start, 1, 0)
    upper = inside != jnp.where(core == 0, 1, 0)
    token = jnp.where(upper, token + 4 * size * q_cols, token)
    return jnp.where(token < bound, 1.0, -1.0)


def normed_heads(part, gain):
    count = part.shape[1]
    heads = part.reshape(-1, HD, count)
    factor = lax.rsqrt(jnp.mean(heads * heads, axis=1, keepdims=True) + 1e-06)
    return heads * factor * gain[None]


def as_column(row):
    size = row.shape[1]
    square = (size, size)
    same = lax.broadcasted_iota(jnp.int32, square, 0) == lax.broadcasted_iota(jnp.int32, square, 1)
    return jnp.sum(jnp.where(same, jnp.broadcast_to(row, square), 0.0), axis=1, keepdims=True)


def attend(tokens, sides, folded, key_gain, queries, acc_ref, keys_ref, values_ref, scores_ref, weights_ref):
    count = tokens.shape[0]
    row = lax.broadcasted_iota(jnp.int32, (8, count), 0)
    key_tail = jnp.where(row == 0, sides, jnp.where(row == 1, 1.0, 0.0))
    value_tail = jnp.where(row == 0, 1.0, 0.0)
    heads_at_once = 4
    for first in range(0, HEADS, heads_at_once):
        rows = slice(first * HD, (first + heads_at_once) * HD)
        part = lax.dot_general(folded[rows], tokens, NT, preferred_element_type=F32)
        keys = normed_heads(part, key_gain)
        for h in range(heads_at_once):
            keys_ref[first + h] = jnp.concatenate([keys[h], key_tail], axis=0).astype(BF16)
            scores_ref[first + h] = jnp.dot(queries[first + h], keys_ref[first + h], preferred_element_type=F32)
    for first in range(0, HEADS, heads_at_once):
        rows = slice(D + first * HD, D + (first + heads_at_once) * HD)
        part = lax.dot_general(folded[rows], tokens, NT, preferred_element_type=F32)
        values = part.reshape(heads_at_once, HD, count)
        for h in range(heads_at_once):
            values_ref[first + h] = jnp.concatenate([values[h], value_tail], axis=0).astype(BF16)
    lane = lax.broadcasted_iota(jnp.int32, (128, 128), 1)
    peaks = jnp.zeros((128, 128), F32)
    for h in range(HEADS):
        scores = scores_ref[h]
        peak = jnp.max(scores, axis=1, keepdims=True)
        weights_ref[h] = jnp.exp2(scores - peak).astype(BF16)
        peaks = jnp.where(lane == h, peak, peaks)
    peaks = peaks.T
    tail_row = lax.broadcasted_iota(jnp.int32, (8, 128), 0)
    for h in range(HEADS):
        mixed = lax.dot_general(values_ref[h], weights_ref[h], NT, preferred_element_type=F32)
        acc_ref[h, :HD] = mixed[:HD]
        acc_ref[h, HD:] = jnp.where(tail_row == 1, peaks[h : h + 1], mixed[HD:])


def attend_scratch(count):
    return [
        pltpu.VMEM((HEADS, SLOT, count), BF16),
        pltpu.VMEM((HEADS, SLOT, count), BF16),
        pltpu.VMEM((HEADS, 128, count), F32),
        pltpu.VMEM((HEADS, 128, count), BF16),
    ]


def query_kernel(lengths_ref, block_ref, centered_ref, query_ref, query_gain_ref, queries_ref):
    normed = jnp.dot(block_ref[...], centered_ref[...], preferred_element_type=F32).astype(BF16)
    part = jnp.dot(normed, query_ref[...], preferred_element_type=F32).T
    count = part.shape[1]
    sides = window_sides(lengths_ref, lax.axis_index("seq") // 2, count)
    queries = normed_heads(part, as_column(query_gain_ref[...] * (math.log2(math.e) / math.sqrt(HD))))
    row = lax.broadcasted_iota(jnp.int32, (8, count), 0)
    tail = jnp.where(row == 0, MASK * sides, jnp.where(row == 1, -MASK, 0.0))
    for h in range(HEADS):
        queries_ref[h] = jnp.concatenate([queries[h], tail], axis=0).T.astype(BF16)


def make_queries(lengths, block, centered, query_weight, query_gain):
    return pl.pallas_call(
        query_kernel,
        out_shape=jax.ShapeDtypeStruct((HEADS, 128, SLOT), BF16),
        in_specs=[SMEM] + [VMEM] * 4,
        out_specs=VMEM,
        compiler_params=params(),
        name="queries",
        cost_estimate=pl.CostEstimate(flops=1 << 30, bytes_accessed=4 << 20, transcendentals=0),
    )(lengths, block, centered, query_weight, query_gain)


def step_kernel(offsets, lengths_ref, *refs):
    blocks = refs[: len(offsets)]
    folded_ref, key_gain_ref, queries_ref, acc_ref, *scratch = refs[len(offsets) :]
    place = ring_place()
    tokens = jnp.concatenate([ref[...] for ref in blocks], axis=0)
    sides = jnp.concatenate(
        [window_sides(lengths_ref, chip_at(place + offset), 128) for offset in dict.fromkeys(offsets)], axis=1
    )
    attend(tokens, sides, folded_ref, as_column(key_gain_ref[...]), queries_ref, acc_ref, *scratch)


ACC = jax.ShapeDtypeStruct((HEADS, SLOT, 128), F32)


def step_attention(offsets, lengths, blocks, folded, key_gain, queries):
    count = sum(block.shape[0] for block in blocks)
    flops = 2 * count * 2 * D * 512 + 4 * HEADS * 128 * 128 * count
    return pl.pallas_call(
        functools.partial(step_kernel, offsets),
        out_shape=ACC,
        in_specs=[SMEM] + [VMEM] * (len(blocks) + 3),
        out_specs=VMEM,
        scratch_shapes=attend_scratch(count),
        compiler_params=params(),
        name="step_attention",
        cost_estimate=pl.CostEstimate(flops=2 * flops, bytes_accessed=5 << 20, transcendentals=HEADS * 128 * count),
    )(lengths, *blocks, folded, key_gain, queries)


RING = (0, -1, 1, -2, 2, -3, 3, 4)


def out_kernel(parts, *refs):
    acc_refs = refs[:parts]
    weight_refs = refs[parts:-3]
    keep_ref, send_ref, mixed_ref = refs[-3:]
    for h in range(HEADS):
        peaks = [acc[h, HD + 1 : HD + 2] for acc in acc_refs]
        peak = functools.reduce(jnp.maximum, peaks)
        total = None
        for acc, own in zip(acc_refs, peaks):
            term = acc[h] * jnp.exp2(own - peak)
            total = term if total is None else total + term
        mixed_ref[h] = total[:HD] / total[HD : HD + 1]
    place = ring_place()
    core = lax.axis_index("seq") % 2
    lefts = []
    for side in range(2):
        heads = [2 * chip_at(place + offset) + jnp.where(core == side, 0, 1) for offset in RING]
        lefts.append(jnp.concatenate([mixed_ref[head] for head in heads], axis=0).T.astype(BF16))
    half = keep_ref.shape[0]
    for first in range(0, D, 256):
        columns = slice(first, min(first + 256, D))
        result = jnp.dot(lefts[0], weight_refs[0][:, columns], preferred_element_type=F32)
        result = result + jnp.dot(lefts[1], weight_refs[1][:, columns], preferred_element_type=F32)
        result = result.astype(BF16)
        keep_ref[:, columns] = result[:half]
        send_ref[:, columns] = result[half:]


def project_out(accs, weights):
    out = jax.ShapeDtypeStruct((64, D), BF16)
    return pl.pallas_call(
        functools.partial(out_kernel, len(accs)),
        out_shape=(out, out),
        in_specs=[VMEM] * (len(accs) + len(weights)),
        out_specs=(VMEM, VMEM),
        scratch_shapes=[pltpu.VMEM((HEADS, HD, 128), F32)],
        compiler_params=params(),
        name="project_out",
        cost_estimate=pl.CostEstimate(flops=2 * 128 * 1280 * D, bytes_accessed=4 << 20, transcendentals=0),
    )(*accs, *weights)


def pack_kernel(*refs):
    out_ref = refs[-1]
    for i in range(7):
        out_ref[i] = refs[i][...]
    cut = refs[7].shape[1]
    out_ref[7, :, :cut] = refs[7][...]
    out_ref[7, :, cut:] = refs[8][...]


def pack(pieces):
    rows, columns = pieces[0].shape
    out = pl.pallas_call(
        pack_kernel,
        out_shape=jax.ShapeDtypeStruct((8, rows, columns), BF16),
        in_specs=[VMEM] * 9,
        out_specs=VMEM,
        compiler_params=params(),
        name="pack",
    )(*pieces)
    return out.reshape(8 * rows, columns)


def merge_kernel(lengths_ref, keep_ref, got_ref, out_ref):
    position = lax.axis_index("seq")
    keep = keep_ref[...].astype(F32)
    got = got_ref[...].astype(F32)
    start, _ = long_window(lengths_ref)
    q_cols = 16
    slot = lax.broadcasted_iota(jnp.int32, keep.shape, 0)
    token = (slot // q_cols) * (lax.axis_size("seq") * q_cols) + position * q_cols + slot % q_cols
    inside = jnp.where(token >= start, 1, 0)
    mine = inside == jnp.where(position % 2 == 0, 1, 0)
    half = keep.shape[0]
    out_ref[:half] = jnp.where(mine, keep, got).astype(BF16)
    out_ref[half:] = jnp.where(mine, got, keep).astype(BF16)


def merge(lengths, keep, got):
    return pl.pallas_call(
        merge_kernel,
        out_shape=jax.ShapeDtypeStruct((128, D), BF16),
        in_specs=[SMEM, VMEM, VMEM],
        out_specs=VMEM,
        compiler_params=params(),
        name="merge",
    )(lengths, keep, got)


def shards(
    clip, frame_counts, conv_first, conv_second, patch_weight, qkv_weight, query_gain, key_gain,
    out_weight, window_lengths,
):
    size = lax.axis_size("seq")
    up = [(i, i + 1) for i in range(size - 1)]
    down = [(j, i) for i, j in up]
    cores = [(i, i ^ 1) for i in range(size)]
    forward = ring_pairs()
    backward = [(j, i) for i, j in forward]

    def send(array, pairs):
        return lax.ppermute(array, "seq", pairs)

    def tied(*arrays):
        return lax.optimization_barrier(arrays)

    def tied(*arrays):
        return lax.optimization_barrier(arrays)

    def both_ways(ahead, behind):
        return send(ahead, forward), send(behind, backward)

    def tied(*arrays):
        return lax.optimization_barrier(arrays)

    def both_ways(ahead, behind):
        return send(ahead, forward), send(behind, backward)

    before = send(clip, up)
    after = send(clip, down)
    query_row, key_row = query_gain[None], key_gain[None]
    weight_one = both_ways(out_weight, out_weight)
    folded, query_weight, centered = fold(patch_weight, qkv_weight)
    before, after, *weight_one, folded = tied(before, after, *weight_one, folded)
    weight_two = both_ways(*weight_one)
    keep, other = convolve(
        frame_counts, window_lengths, clip, before, after, conv_first, conv_second, patch_weight
    )
    other, wu_a, wu_b = tied(other, *weight_two)
    weight_two = (wu_a, wu_b)
    got = send(other, cores)
    weight_three = both_ways(*weight_two)
    block = jnp.concatenate([keep, got], axis=0)
    one = both_ways(block, block)
    queries = make_queries(window_lengths, block, centered, query_weight, query_row)
    *one, queries = tied(*one, queries)
    two = both_ways(*one)
    acc_one = step_attention((-1, 1), window_lengths, one, folded, key_row, queries)
    wt_a, wt_b, acc_one = tied(*weight_three, acc_one)
    cut = 640
    weight_four = both_ways(wt_a[:, :cut], wt_b[:, cut:])
    *two, acc_one = tied(*two, acc_one)
    three = both_ways(*two)
    acc_two = step_attention((-2, 2), window_lengths, two, folded, key_row, queries)
    *three, acc_two, wf_a, wf_b = tied(*three, acc_two, *weight_four)
    four = both_ways(three[0][:64], three[1][64:])
    weights = pack([out_weight, *weight_one, *weight_two, wt_a, wt_b, wf_a, wf_b])
    sibling = send(weights, cores)
    acc_three = step_attention((-3, 3), window_lengths, three, folded, key_row, queries)
    *four, acc_three = tied(*four, acc_three)
    acc_four = step_attention((0, 4, 4), window_lengths, [block, *four], folded, key_row, queries)
    keep_rows, send_rows = project_out((acc_one, acc_two, acc_three, acc_four), (weights, sibling))
    return merge(window_lengths, keep_rows, send(send_rows, cores))


def solution(mesh):
    own = mesh.shape["seq"] == HEADS
    return jax.shard_map(
        shards if own else general_shards,
        mesh=mesh,
        in_specs=(
            P("groups", "seq", None, None),
            P("groups"),
            P(),
            P(),
            P(),
            P(),
            P(),
            P(),
            P("seq", None),
            P("groups", None),
        ),
        out_specs=P(("groups", "seq"), None),
        check_vma=False,
    )
```

```python
import functools
import math

import jax
import jax.numpy as jnp
from jax import lax
from jax.experimental import pallas as pl
from jax.experimental.pallas import tpu as pltpu
from jax.sharding import PartitionSpec as P

D = 1152
HEADS = 16


def extended(array, sides, width):
    for axis, dim in sides:
        size, length = (lax.axis_size(axis), array.shape[dim])
        up = [(i, (i + 1) % size) for i in range(size - 1)]
        down = [(j, i) for i, j in up]
        last = lax.slice_in_dim(array, length - width, length, axis=dim)
        first = lax.slice_in_dim(array, 0, width, axis=dim)
        before = lax.ppermute(last, axis, up)
        after = lax.ppermute(first, axis, down)
        array = jnp.concatenate([before, array, after], axis=dim)
    return array


def frame_weights(frame_counts, frames):
    position = jnp.arange(frames, dtype=jnp.int32)
    clip_ends = jnp.cumsum(frame_counts)

    def clip_of(index):
        return jnp.sum((index[:, None] >= clip_ends[None, :]).astype(jnp.int32), axis=1)

    own_clip = clip_of(position)
    columns = []
    for offset in (-1, 0, 1):
        neighbor = position + offset
        inside = (neighbor >= 0) & (neighbor < frames)
        same_clip = clip_of(jnp.clip(neighbor, 0, frames - 1)) == own_clip
        columns.append((inside & same_clip).astype(jnp.float32))
    return jnp.stack(columns, axis=1)


def convolve_rows(activation, kernel, tap_weights):
    empty_frame = jnp.zeros_like(activation[:1])
    shifted = (
        jnp.concatenate([empty_frame, activation[:-1]], 0),
        activation,
        jnp.concatenate([activation[1:], empty_frame], 0),
    )
    summed = None
    for offset in range(3):
        response = lax.conv_general_dilated(
            shifted[offset],
            kernel[offset],
            (1, 1),
            ((0, 0), (1, 1)),
            dimension_numbers=("NHWC", "HWIO", "NHWC"),
            preferred_element_type=jnp.float32,
        )
        tap_term = tap_weights[:, offset][:, None, None, None] * response
        summed = tap_term if offset == 0 else summed + tap_term
    return summed


def rms_scale(part, gain):
    factor = lax.rsqrt(jnp.mean(part * part, axis=-1, keepdims=True) + 1e-06)
    return (part * factor * gain).astype(jnp.bfloat16)


def general_shards(
    clip,
    frame_counts,
    conv_first,
    conv_second,
    patch_weight,
    qkv_weight,
    query_gain,
    key_gain,
    out_weight,
    window_lengths,
):
    frames, tile_rows, tile_cols, channels = clip.shape
    devices = lax.axis_size("seq")
    position = lax.axis_index("seq")
    head_dim = D // HEADS
    score_scale = 1.0 / math.sqrt(head_dim)
    tap_weights = frame_weights(frame_counts, frames)
    source = clip.astype(jnp.float32)
    padded_clip = extended(clip, (("seq", 1),), 2)
    first_in = jax.nn.silu(padded_clip.astype(jnp.float32)).astype(jnp.bfloat16)
    hidden_wide = convolve_rows(first_in, conv_first, tap_weights)
    global_row = position * tile_rows - 1 + jnp.arange(tile_rows + 2, dtype=jnp.int32)
    inside = ((global_row >= 0) & (global_row < tile_rows * devices)).astype(jnp.float32)
    hidden_one = (hidden_wide * inside[None, :, None, None]).astype(jnp.bfloat16)
    padded_second = jax.nn.silu(hidden_one.astype(jnp.float32)).astype(jnp.bfloat16)
    latent = (source + convolve_rows(padded_second, conv_second, tap_weights)).astype(jnp.bfloat16)
    token_rows = tile_rows // 2
    token_cols = tile_cols // 2
    patches = (
        latent.reshape(frames, token_rows, 2, token_cols, 2, channels)
        .transpose(0, 1, 3, 2, 4, 5)
        .reshape(-1, 4 * channels)
    )
    tok_count = patches.shape[0]
    embedded = jnp.dot(patches, patch_weight, preferred_element_type=jnp.float32).astype(
        jnp.bfloat16
    )
    values_f = embedded.astype(jnp.float32)
    row_mean = jnp.mean(values_f, axis=-1, keepdims=True)
    centered = values_f - row_mean
    variance = jnp.mean(centered * centered, axis=-1, keepdims=True)
    normed = (centered / jnp.sqrt(variance + 1e-06)).astype(jnp.bfloat16)
    projected = jnp.dot(normed, qkv_weight, preferred_element_type=jnp.float32).reshape(
        tok_count, 3, HEADS, head_dim
    )
    stacked = jnp.stack(
        [
            rms_scale(projected[:, 0], query_gain),
            rms_scale(projected[:, 1], key_gain),
            projected[:, 2].astype(jnp.bfloat16),
        ],
        axis=1,
    )
    groups = devices // HEADS
    frame_share = frames // groups
    local_share = tok_count // groups
    span_rows = devices * local_share
    outgoing = (
        stacked.reshape(groups, local_share, 3, HEADS, head_dim)
        .transpose(0, 3, 1, 2, 4)
        .reshape(devices, local_share, 3 * head_dim)
    )
    incoming = lax.all_to_all(outgoing, "seq", split_axis=0, concat_axis=0, tiled=True)
    arranged = (
        incoming.reshape(devices, frame_share, token_rows * token_cols, 3, head_dim)
        .transpose(3, 1, 0, 2, 4)
        .reshape(3, span_rows, head_dim)
    )
    my_group = position // HEADS
    lengths = lax.dynamic_index_in_dim(window_lengths, my_group, 0, keepdims=False)
    window_ends = jnp.cumsum(lengths)
    token_index = jnp.arange(span_rows, dtype=jnp.int32)
    segment = jnp.sum((token_index[:, None] >= window_ends[None, :]).astype(jnp.int32), axis=1)
    key_rows = arranged[1]
    value_rows = arranged[2]
    block_rows = min(512, span_rows)
    block_count = span_rows // block_rows

    def attend_block(inputs):
        query_block, segment_block = inputs
        scores = jnp.dot(query_block, key_rows.T, preferred_element_type=jnp.float32) * score_scale
        allowed = segment_block[:, None] == segment[None, :]
        scores = jnp.where(allowed, scores, -1e30)
        row_peak = jnp.max(scores, axis=-1, keepdims=True)
        weights = jnp.exp(scores - row_peak)
        row_mass = jnp.sum(weights, axis=-1, keepdims=True)
        mixed = (
            jnp.dot(weights.astype(jnp.bfloat16), value_rows, preferred_element_type=jnp.float32)
            / row_mass
        )
        return mixed.astype(jnp.bfloat16)

    mixed_rows = lax.map(
        attend_block,
        (
            arranged[0].reshape(block_count, block_rows, head_dim),
            segment.reshape(block_count, block_rows),
        ),
    ).reshape(span_rows, head_dim)
    outgoing_back = (
        mixed_rows.reshape(frame_share, devices, token_rows * token_cols, head_dim)
        .transpose(1, 0, 2, 3)
        .reshape(devices, local_share, head_dim)
    )
    returned = lax.all_to_all(outgoing_back, "seq", split_axis=0, concat_axis=0, tiled=True)
    merged = (
        returned.reshape(groups, HEADS, local_share, head_dim)
        .transpose(0, 2, 1, 3)
        .reshape(tok_count, D)
    )
    projected_out = jnp.dot(
        merged,
        lax.all_gather(out_weight, "seq", axis=0, tiled=True),
        preferred_element_type=jnp.float32,
    )
    return projected_out.astype(jnp.bfloat16)


HD = D // HEADS
SLOT = 80
MASK = 1024.0
FOLD_MIB = 52
CONV_MIB = 44
F32 = jnp.float32
BF16 = jnp.bfloat16
VMEM = pl.BlockSpec(memory_space=pltpu.VMEM)
SMEM = pl.BlockSpec(memory_space=pltpu.SMEM)
NT = (((1,), (1,)), ((), ()))


def params(mib=40):
    return pltpu.CompilerParams(vmem_limit_bytes=mib << 20)


def silu(v):
    return v / (1.0 + jnp.exp(-v))


def long_window(lengths):
    first, second = lengths[0, 0], lengths[0, 1]
    half = 1024
    start = jnp.where(first == half, 0, jnp.where(second == half, first, first + second))
    bound = jnp.where(first == half, half + second, first)
    return start, bound


ANY = pl.BlockSpec(memory_space=pl.ANY)
TN = (((0,), (1,)), ((), ()))


def pair_weights(weights, o, ch=128):
    blank = jnp.zeros((ch, ch), BF16)
    rows = []
    for four in range(4):
        for j in range(3):
            taps = [weights[o, four - r, j] if 0 <= four - r < 3 else blank for r in range(2)]
            rows.append(jnp.concatenate(taps, axis=1))
    return jnp.concatenate(rows, axis=0)


def fold_kernel(
    patch_any, qkv_any, first_any, second_any,
    folded_ref, query_ref, centered_ref, first_ref, second_ref, patch_ref, qkv_ref, sems,
):
    chunk = 384
    pieces = 2 * D // chunk

    def piece_copy(i):
        columns = pl.ds(D + i * chunk, chunk)
        return pltpu.make_async_copy(qkv_any.at[:, columns], qkv_ref.at[i], sems.at[i])

    patch_copy = pltpu.make_async_copy(patch_any, patch_ref, sems.at[pieces])
    late = [
        pltpu.make_async_copy(first_any, first_ref, sems.at[pieces + 1]),
        pltpu.make_async_copy(second_any, second_ref, sems.at[pieces + 2]),
        pltpu.make_async_copy(qkv_any.at[:, pl.ds(0, D)], query_ref, sems.at[pieces + 3]),
    ]
    copies = [piece_copy(i) for i in range(pieces)]
    for copy in [patch_copy, *copies, *late]:
        copy.start()
    patch_copy.wait()
    patch = patch_ref[...].astype(F32)
    centered_ref[...] = (patch - jnp.mean(patch, axis=1, keepdims=True)).astype(BF16)
    for i in range(pieces):
        copies[i].wait()
        product = lax.dot_general(qkv_ref[i], centered_ref[...], TN, preferred_element_type=F32)
        folded_ref[i * chunk : (i + 1) * chunk] = product.astype(BF16)
    for copy in late:
        copy.wait()


def fold(patch_weight, qkv_weight, conv_first, conv_second):
    inner = patch_weight.shape[0]
    return pl.pallas_call(
        fold_kernel,
        out_shape=(
            jax.ShapeDtypeStruct((2 * D, inner), BF16),
            jax.ShapeDtypeStruct((D, D), BF16),
            jax.ShapeDtypeStruct((inner, D), BF16),
            jax.ShapeDtypeStruct(conv_first.shape, BF16),
            jax.ShapeDtypeStruct(conv_second.shape, BF16),
        ),
        in_specs=[ANY] * 4,
        out_specs=(VMEM,) * 5,
        scratch_shapes=[
            pltpu.VMEM(patch_weight.shape, BF16),
            pltpu.VMEM((6, D, 384), BF16),
            pltpu.SemaphoreType.DMA((10,)),
        ],
        compiler_params=params(FOLD_MIB),
        name="fold",
        cost_estimate=pl.CostEstimate(flops=2 * inner * D * 2 * D, bytes_accessed=12 << 20, transcendentals=0),
    )(patch_weight, qkv_weight, conv_first, conv_second)


def frame_taps(counts_ref, frames):
    def clip_of(frame):
        end = 0
        index = 0
        for c in range(counts_ref.shape[0]):
            end = end + counts_ref[c]
            index = index + jnp.where(frame >= end, 1, 0)
        return index

    own = [clip_of(f) for f in range(frames)]
    joined = [jnp.where(own[f] == own[f + 1], 1.0, 0.0) for f in range(frames - 1)]
    return [0.0] + joined, joined + [0.0]


def conv_kernel(
    counts_any, lengths_any, own_any, patch_any, sibling_ref, other_ref, first_ref, second_ref,
    keep_ref, send_ref, grid_one, grid_two, pixels, own_ref, patch_ref, counts_ref, lengths_ref, sems,
):
    copies = [
        pltpu.make_async_copy(own_any, own_ref, sems.at[0]),
        pltpu.make_async_copy(counts_any, counts_ref, sems.at[1]),
        pltpu.make_async_copy(lengths_any, lengths_ref, sems.at[2]),
        pltpu.make_async_copy(patch_any, patch_ref, sems.at[3]),
    ]
    for copy in copies:
        copy.start()
    frames, _, cols, ch = own_ref.shape
    wide = 12 * ch
    position = lax.axis_index("seq")
    column = lax.broadcasted_iota(jnp.int32, (frames, cols, ch), 1)

    def shifted(row):
        left = jnp.where(column == 0, 0.0, pltpu.roll(row, 1, 1))
        right = jnp.where(column == cols - 1, 0.0, pltpu.roll(row, cols - 1, 1))
        return [part.astype(BF16) for part in (left, row, right)]

    blank = jnp.zeros((cols, wide), BF16)
    for g in range(2):
        grid_one[g, 0] = blank
        grid_one[g, frames + 1] = blank
    grid_two[0] = blank
    grid_two[frames + 1] = blank
    on_first = position % 2 == 0

    def source_row(r):
        if r in (2, 3):
            return own_ref[:, r - 2].astype(F32)
        sibling, other = sibling_ref[:, r % 2].astype(F32), other_ref[:, r % 2].astype(F32)
        return jnp.where(on_first, other, sibling) if r < 2 else jnp.where(on_first, sibling, other)

    for r in (0, 1, 4, 5, 2, 3):
        if r == 2:
            copies[0].wait()
        row = silu(source_row(r))
        parts = shifted(row)
        for g in range(2):
            four = r - 2 * g
            if 0 <= four < 4:
                for j in range(3):
                    grid_one[g, 1 : frames + 1, :, (four * 3 + j) * ch : (four * 3 + j + 1) * ch] = parts[j]

    copies[1].wait()
    copies[2].wait()
    before_tap, after_tap = frame_taps(counts_ref, frames)

    def summed(terms):
        rows = []
        for f in range(frames):
            total = terms[1][f]
            if f > 0:
                total = total + before_tap[f] * terms[0][f]
            if f < frames - 1:
                total = total + after_tap[f] * terms[2][f]
            rows.append(total)
        return jnp.stack(rows)

    for g in range(2):
        terms = []
        for o in range(3):
            left = grid_one[g, o : o + frames].reshape(frames * cols, wide)
            terms.append(
                jnp.dot(left, pair_weights(first_ref, o), preferred_element_type=F32).reshape(frames, cols, 2 * ch)
            )
        hidden = summed(terms)
        for out_row in range(2):
            four = 2 * g + out_row
            row = hidden[:, :, out_row * ch : (out_row + 1) * ch]
            if four == 0:
                row = row * jnp.where(position == 0, 0.0, 1.0)
            if four == 3:
                row = row * jnp.where(position == lax.axis_size("seq") - 1, 0.0, 1.0)
            row = silu(row.astype(BF16).astype(F32))
            parts = shifted(row)
            for j in range(3):
                grid_two[1 : frames + 1, :, (four * 3 + j) * ch : (four * 3 + j + 1) * ch] = parts[j]
    terms = []
    for o in range(3):
        left = grid_two[o : o + frames].reshape(frames * cols, wide)
        terms.append(
            jnp.dot(left, pair_weights(second_ref, o), preferred_element_type=F32).reshape(frames, cols, 2 * ch)
        )
    residual = summed(terms)
    for out_row in range(2):
        block = own_ref[:, out_row].astype(F32) + residual[:, :, out_row * ch : (out_row + 1) * ch]
        pixels[out_row] = block.astype(BF16).astype(F32).reshape(frames * cols, ch)
    tokens = frames * cols // 2
    patches = jnp.concatenate(
        [pixels[a, pl.ds(b, tokens, 2), :] for a in range(2) for b in range(2)], axis=1
    )
    copies[3].wait()
    embedded = jnp.dot(patches.astype(BF16), patch_ref[...], preferred_element_type=F32)
    centered = embedded - jnp.mean(embedded, axis=1, keepdims=True)
    variance = jnp.mean(centered * centered, axis=1, keepdims=True)
    scaled = patches * (1.0 / jnp.sqrt(variance + 1e-06))
    half = tokens // 2
    low, high = scaled[:half], scaled[half:]
    start, _ = long_window(lengths_ref)
    q_cols = cols // 2
    slot = lax.broadcasted_iota(jnp.int32, low.shape, 0)
    token = (slot // q_cols) * (lax.axis_size("seq") * q_cols) + position * q_cols + slot % q_cols
    inside = jnp.where(token >= start, 1, 0)
    mine = inside == jnp.where(position % 2 == 0, 1, 0)
    keep = jnp.where(mine, low, high).astype(BF16)
    send = jnp.where(mine, high, low).astype(BF16)
    keep_ref[...] = keep
    send_ref[...] = send


def convolve(counts, lengths, clip, sibling_rows, other_rows, conv_first, conv_second, patch_weight):
    frames, _, cols, ch = clip.shape
    tokens = frames * cols // 2
    out = jax.ShapeDtypeStruct((tokens // 2, 4 * ch), BF16)
    return pl.pallas_call(
        conv_kernel,
        out_shape=(out, out),
        in_specs=[ANY] * 4 + [VMEM] * 4,
        out_specs=(VMEM, VMEM),
        scratch_shapes=[
            pltpu.VMEM((2, frames + 2, cols, 12 * ch), BF16),
            pltpu.VMEM((frames + 2, cols, 12 * ch), BF16),
            pltpu.VMEM((2, frames * cols, ch), F32),
            pltpu.VMEM(clip.shape, BF16),
            pltpu.VMEM(patch_weight.shape, BF16),
            pltpu.SMEM(counts.shape, jnp.int32),
            pltpu.SMEM(lengths.shape, jnp.int32),
            pltpu.SemaphoreType.DMA((4,)),
        ],
        compiler_params=params(CONV_MIB),
        name="convolve",
        cost_estimate=pl.CostEstimate(flops=2 << 30, bytes_accessed=4 << 20, transcendentals=1 << 18),
    )(counts, lengths, clip, patch_weight, sibling_rows, other_rows, conv_first, conv_second)


def chip_at(place):
    chips = lax.axis_size("seq") // 2
    place = lax.rem(place + 2 * chips, chips)
    return jnp.where(place < chips // 2, 2 * place, 2 * (chips - 1 - place) + 1)


def ring_place():
    chips = lax.axis_size("seq") // 2
    chip = lax.axis_index("seq") // 2
    return jnp.where(chip % 2 == 0, chip // 2, chips - 1 - chip // 2)


def ring_pairs():
    size = lax.axis_size("seq")
    chips = size // 2
    order = [2 * i for i in range(chips // 2)] + [2 * i + 1 for i in reversed(range(chips // 2))]
    return [
        (2 * order[i] + core, 2 * order[(i + 1) % chips] + core) for i in range(chips) for core in range(2)
    ]


def window_sides(lengths_ref, chip, count):
    size = lax.axis_size("seq")
    core = lax.axis_index("seq") % 2
    start, bound = long_window(lengths_ref)
    lane = lax.broadcasted_iota(jnp.int32, (8, count), 1)
    half = count // 2
    slot = lane % half
    row = 2 * chip + jnp.where(lane < half, core, 1 - core)
    q_cols = 16
    token = (slot // q_cols) * (size * q_cols) + row * q_cols + slot % q_cols
    inside = jnp.where(token >= start, 1, 0)
    upper = inside != jnp.where(core == 0, 1, 0)
    token = jnp.where(upper, token + 4 * size * q_cols, token)
    return jnp.where(token < bound, 1.0, -1.0)


def normed_heads(part, gain):
    count = part.shape[1]
    heads = part.reshape(-1, HD, count)
    factor = lax.rsqrt(jnp.mean(heads * heads, axis=1, keepdims=True) + 1e-06)
    return heads * factor * gain[None]


def as_column(row):
    size = row.shape[1]
    square = (size, size)
    same = lax.broadcasted_iota(jnp.int32, square, 0) == lax.broadcasted_iota(jnp.int32, square, 1)
    return jnp.sum(jnp.where(same, jnp.broadcast_to(row, square), 0.0), axis=1, keepdims=True)


def attend(tokens, sides, folded, key_gain, queries, acc_ref, keys_ref, values_ref, scores_ref, weights_ref):
    count = tokens.shape[0]
    row = lax.broadcasted_iota(jnp.int32, (8, count), 0)
    key_tail = jnp.where(row == 0, sides, jnp.where(row == 1, 1.0, 0.0))
    value_tail = jnp.where(row == 0, 1.0, 0.0)
    heads_at_once = 4
    for first in range(0, HEADS, heads_at_once):
        rows = slice(first * HD, (first + heads_at_once) * HD)
        part = lax.dot_general(folded[rows], tokens, NT, preferred_element_type=F32)
        keys = normed_heads(part, key_gain)
        for h in range(heads_at_once):
            keys_ref[first + h] = jnp.concatenate([keys[h], key_tail], axis=0).astype(BF16)
            scores_ref[first + h] = jnp.dot(queries[first + h], keys_ref[first + h], preferred_element_type=F32)
    for first in range(0, HEADS, heads_at_once):
        rows = slice(D + first * HD, D + (first + heads_at_once) * HD)
        part = lax.dot_general(folded[rows], tokens, NT, preferred_element_type=F32)
        values = part.reshape(heads_at_once, HD, count)
        for h in range(heads_at_once):
            values_ref[first + h] = jnp.concatenate([values[h], value_tail], axis=0).astype(BF16)
    lane = lax.broadcasted_iota(jnp.int32, (128, 128), 1)
    peaks = jnp.zeros((128, 128), F32)
    for h in range(HEADS):
        scores = scores_ref[h]
        peak = jnp.max(scores, axis=1, keepdims=True)
        weights_ref[h] = jnp.exp2(scores - peak).astype(BF16)
        peaks = jnp.where(lane == h, peak, peaks)
    peaks = peaks.T
    tail_row = lax.broadcasted_iota(jnp.int32, (8, 128), 0)
    for h in range(HEADS):
        mixed = lax.dot_general(values_ref[h], weights_ref[h], NT, preferred_element_type=F32)
        acc_ref[h, :HD] = mixed[:HD]
        acc_ref[h, HD:] = jnp.where(tail_row == 1, peaks[h : h + 1], mixed[HD:])


def attend_scratch(count):
    return [
        pltpu.VMEM((HEADS, SLOT, count), BF16),
        pltpu.VMEM((HEADS, SLOT, count), BF16),
        pltpu.VMEM((HEADS, 128, count), F32),
        pltpu.VMEM((HEADS, 128, count), BF16),
    ]


def query_kernel(lengths_ref, block_ref, centered_ref, query_ref, query_gain_ref, queries_ref):
    normed = jnp.dot(block_ref[...], centered_ref[...], preferred_element_type=F32).astype(BF16)
    part = jnp.dot(normed, query_ref[...], preferred_element_type=F32).T
    count = part.shape[1]
    sides = window_sides(lengths_ref, lax.axis_index("seq") // 2, count)
    queries = normed_heads(part, as_column(query_gain_ref[...] * (math.log2(math.e) / math.sqrt(HD))))
    row = lax.broadcasted_iota(jnp.int32, (8, count), 0)
    tail = jnp.where(row == 0, MASK * sides, jnp.where(row == 1, -MASK, 0.0))
    for h in range(HEADS):
        queries_ref[h] = jnp.concatenate([queries[h], tail], axis=0).T.astype(BF16)


def make_queries(lengths, block, centered, query_weight, query_gain):
    return pl.pallas_call(
        query_kernel,
        out_shape=jax.ShapeDtypeStruct((HEADS, 128, SLOT), BF16),
        in_specs=[SMEM] + [VMEM] * 4,
        out_specs=VMEM,
        compiler_params=params(),
        name="queries",
        cost_estimate=pl.CostEstimate(flops=1 << 30, bytes_accessed=4 << 20, transcendentals=0),
    )(lengths, block, centered, query_weight, query_gain)


def step_kernel(offsets, lengths_ref, *refs):
    blocks = refs[: len(offsets)]
    folded_ref, key_gain_ref, queries_ref, acc_ref, *scratch = refs[len(offsets) :]
    place = ring_place()
    tokens = jnp.concatenate([ref[...] for ref in blocks], axis=0)
    sides = jnp.concatenate(
        [window_sides(lengths_ref, chip_at(place + offset), 128) for offset in dict.fromkeys(offsets)], axis=1
    )
    attend(tokens, sides, folded_ref, as_column(key_gain_ref[...]), queries_ref, acc_ref, *scratch)


ACC = jax.ShapeDtypeStruct((HEADS, SLOT, 128), F32)


def step_attention(offsets, lengths, blocks, folded, key_gain, queries):
    count = sum(block.shape[0] for block in blocks)
    flops = 2 * count * 2 * D * 512 + 4 * HEADS * 128 * 128 * count
    return pl.pallas_call(
        functools.partial(step_kernel, offsets),
        out_shape=ACC,
        in_specs=[SMEM] + [VMEM] * (len(blocks) + 3),
        out_specs=VMEM,
        scratch_shapes=attend_scratch(count),
        compiler_params=params(),
        name="step_attention",
        cost_estimate=pl.CostEstimate(flops=2 * flops, bytes_accessed=5 << 20, transcendentals=HEADS * 128 * count),
    )(lengths, *blocks, folded, key_gain, queries)


RING = (0, -1, 1, -2, 2, -3, 3, 4)


def out_kernel(parts, *refs):
    acc_refs = refs[:parts]
    weight_refs = refs[parts:-3]
    keep_ref, send_ref, mixed_ref = refs[-3:]
    for h in range(HEADS):
        peaks = [acc[h, HD + 1 : HD + 2] for acc in acc_refs]
        peak = functools.reduce(jnp.maximum, peaks)
        total = None
        for acc, own in zip(acc_refs, peaks):
            term = acc[h] * jnp.exp2(own - peak)
            total = term if total is None else total + term
        mixed_ref[h] = total[:HD] / total[HD : HD + 1]
    place = ring_place()
    core = lax.axis_index("seq") % 2
    lefts = []
    for side in range(2):
        heads = [2 * chip_at(place + offset) + jnp.where(core == side, 0, 1) for offset in RING]
        lefts.append(jnp.concatenate([mixed_ref[head] for head in heads], axis=0).T.astype(BF16))
    half = keep_ref.shape[0]
    for first in range(0, D, 256):
        columns = slice(first, min(first + 256, D))
        result = jnp.dot(lefts[0], weight_refs[0][:, columns], preferred_element_type=F32)
        result = result + jnp.dot(lefts[1], weight_refs[1][:, columns], preferred_element_type=F32)
        result = result.astype(BF16)
        keep_ref[:, columns] = result[:half]
        send_ref[:, columns] = result[half:]


def project_out(accs, weights):
    out = jax.ShapeDtypeStruct((64, D), BF16)
    return pl.pallas_call(
        functools.partial(out_kernel, len(accs)),
        out_shape=(out, out),
        in_specs=[VMEM] * (len(accs) + len(weights)),
        out_specs=(VMEM, VMEM),
        scratch_shapes=[pltpu.VMEM((HEADS, HD, 128), F32)],
        compiler_params=params(),
        name="project_out",
        cost_estimate=pl.CostEstimate(flops=2 * 128 * 1280 * D, bytes_accessed=4 << 20, transcendentals=0),
    )(*accs, *weights)


def pack_kernel(*refs):
    out_ref = refs[-1]
    for i in range(7):
        out_ref[i] = refs[i][...]
    cut = refs[7].shape[1]
    out_ref[7, :, :cut] = refs[7][...]
    out_ref[7, :, cut:] = refs[8][...]


def pack(pieces):
    rows, columns = pieces[0].shape
    out = pl.pallas_call(
        pack_kernel,
        out_shape=jax.ShapeDtypeStruct((8, rows, columns), BF16),
        in_specs=[VMEM] * 9,
        out_specs=VMEM,
        compiler_params=params(),
        name="pack",
    )(*pieces)
    return out.reshape(8 * rows, columns)


def merge_kernel(lengths_ref, keep_ref, got_ref, out_ref):
    position = lax.axis_index("seq")
    keep = keep_ref[...].astype(F32)
    got = got_ref[...].astype(F32)
    start, _ = long_window(lengths_ref)
    q_cols = 16
    slot = lax.broadcasted_iota(jnp.int32, keep.shape, 0)
    token = (slot // q_cols) * (lax.axis_size("seq") * q_cols) + position * q_cols + slot % q_cols
    inside = jnp.where(token >= start, 1, 0)
    mine = inside == jnp.where(position % 2 == 0, 1, 0)
    half = keep.shape[0]
    out_ref[:half] = jnp.where(mine, keep, got).astype(BF16)
    out_ref[half:] = jnp.where(mine, got, keep).astype(BF16)


def merge(lengths, keep, got):
    return pl.pallas_call(
        merge_kernel,
        out_shape=jax.ShapeDtypeStruct((128, D), BF16),
        in_specs=[SMEM, VMEM, VMEM],
        out_specs=VMEM,
        compiler_params=params(),
        name="merge",
    )(lengths, keep, got)


def shards(
    clip, frame_counts, conv_first, conv_second, patch_weight, qkv_weight, query_gain, key_gain,
    out_weight, window_lengths,
):
    size = lax.axis_size("seq")
    facing = [(i, j) for i in range(1, size - 1, 2) for i, j in ((i, i + 1), (i + 1, i))]
    cores = [(i, i ^ 1) for i in range(size)]
    forward = ring_pairs()
    backward = [(j, i) for i, j in forward]

    def send(array, pairs):
        return lax.ppermute(array, "seq", pairs)

    def tied(*arrays):
        return lax.optimization_barrier(arrays)

    def tied(*arrays):
        return lax.optimization_barrier(arrays)

    def both_ways(ahead, behind):
        return send(ahead, forward), send(behind, backward)

    def tied(*arrays):
        return lax.optimization_barrier(arrays)

    def both_ways(ahead, behind):
        return send(ahead, forward), send(behind, backward)

    sibling_rows = send(clip, cores)
    other_rows = send(clip, facing)
    query_row, key_row = query_gain[None], key_gain[None]
    weight_one = both_ways(out_weight, out_weight)
    folded, query_weight, centered, first, second = fold(
        patch_weight, qkv_weight, conv_first, conv_second
    )
    sibling_rows, other_rows, *weight_one, folded = tied(sibling_rows, other_rows, *weight_one, folded)
    weight_two = both_ways(*weight_one)
    keep, other = convolve(
        frame_counts, window_lengths, clip, sibling_rows, other_rows, first, second, patch_weight
    )
    other, wu_a, wu_b = tied(other, *weight_two)
    weight_two = (wu_a, wu_b)
    got = send(other, cores)
    weight_three = both_ways(*weight_two)
    block = jnp.concatenate([keep, got], axis=0)
    one = both_ways(block, block)
    queries = make_queries(window_lengths, block, centered, query_weight, query_row)
    *one, queries = tied(*one, queries)
    two = both_ways(*one)
    acc_one = step_attention((-1, 1), window_lengths, one, folded, key_row, queries)
    wt_a, wt_b, acc_one = tied(*weight_three, acc_one)
    cut = 640
    weight_four = both_ways(wt_a[:, :cut], wt_b[:, cut:])
    *two, acc_one = tied(*two, acc_one)
    three = both_ways(*two)
    acc_two = step_attention((-2, 2), window_lengths, two, folded, key_row, queries)
    *three, acc_two, wf_a, wf_b = tied(*three, acc_two, *weight_four)
    four = both_ways(three[0][:64], three[1][64:])
    weights = pack([out_weight, *weight_one, *weight_two, wt_a, wt_b, wf_a, wf_b])
    sibling = send(weights, cores)
    acc_three = step_attention((-3, 3), window_lengths, three, folded, key_row, queries)
    *four, acc_three = tied(*four, acc_three)
    acc_four = step_attention((0, 4, 4), window_lengths, [block, *four], folded, key_row, queries)
    keep_rows, send_rows = project_out((acc_one, acc_two, acc_three, acc_four), (weights, sibling))
    return merge(window_lengths, keep_rows, send(send_rows, cores))


def solution(mesh):
    own = mesh.shape["seq"] == HEADS
    return jax.shard_map(
        shards if own else general_shards,
        mesh=mesh,
        in_specs=(
            P("groups", "seq", None, None),
            P("groups"),
            P(),
            P(),
            P(),
            P(),
            P(),
            P(),
            P("seq", None),
            P("groups", None),
        ),
        out_specs=P(("groups", "seq"), None),
        check_vma=False,
    )
```

```python
import functools
import math

import jax
import jax.numpy as jnp
from jax import lax
from jax.experimental import pallas as pl
from jax.experimental.pallas import tpu as pltpu
from jax.sharding import PartitionSpec as P

D = 1152
HEADS = 16


def extended(array, sides, width):
    for axis, dim in sides:
        size, length = (lax.axis_size(axis), array.shape[dim])
        up = [(i, (i + 1) % size) for i in range(size - 1)]
        down = [(j, i) for i, j in up]
        last = lax.slice_in_dim(array, length - width, length, axis=dim)
        first = lax.slice_in_dim(array, 0, width, axis=dim)
        before = lax.ppermute(last, axis, up)
        after = lax.ppermute(first, axis, down)
        array = jnp.concatenate([before, array, after], axis=dim)
    return array


def frame_weights(frame_counts, frames):
    position = jnp.arange(frames, dtype=jnp.int32)
    clip_ends = jnp.cumsum(frame_counts)

    def clip_of(index):
        return jnp.sum((index[:, None] >= clip_ends[None, :]).astype(jnp.int32), axis=1)

    own_clip = clip_of(position)
    columns = []
    for offset in (-1, 0, 1):
        neighbor = position + offset
        inside = (neighbor >= 0) & (neighbor < frames)
        same_clip = clip_of(jnp.clip(neighbor, 0, frames - 1)) == own_clip
        columns.append((inside & same_clip).astype(jnp.float32))
    return jnp.stack(columns, axis=1)


def convolve_rows(activation, kernel, tap_weights):
    empty_frame = jnp.zeros_like(activation[:1])
    shifted = (
        jnp.concatenate([empty_frame, activation[:-1]], 0),
        activation,
        jnp.concatenate([activation[1:], empty_frame], 0),
    )
    summed = None
    for offset in range(3):
        response = lax.conv_general_dilated(
            shifted[offset],
            kernel[offset],
            (1, 1),
            ((0, 0), (1, 1)),
            dimension_numbers=("NHWC", "HWIO", "NHWC"),
            preferred_element_type=jnp.float32,
        )
        tap_term = tap_weights[:, offset][:, None, None, None] * response
        summed = tap_term if offset == 0 else summed + tap_term
    return summed


def rms_scale(part, gain):
    factor = lax.rsqrt(jnp.mean(part * part, axis=-1, keepdims=True) + 1e-06)
    return (part * factor * gain).astype(jnp.bfloat16)


def general_shards(
    clip,
    frame_counts,
    conv_first,
    conv_second,
    patch_weight,
    qkv_weight,
    query_gain,
    key_gain,
    out_weight,
    window_lengths,
):
    frames, tile_rows, tile_cols, channels = clip.shape
    devices = lax.axis_size("seq")
    position = lax.axis_index("seq")
    head_dim = D // HEADS
    score_scale = 1.0 / math.sqrt(head_dim)
    tap_weights = frame_weights(frame_counts, frames)
    source = clip.astype(jnp.float32)
    padded_clip = extended(clip, (("seq", 1),), 2)
    first_in = jax.nn.silu(padded_clip.astype(jnp.float32)).astype(jnp.bfloat16)
    hidden_wide = convolve_rows(first_in, conv_first, tap_weights)
    global_row = position * tile_rows - 1 + jnp.arange(tile_rows + 2, dtype=jnp.int32)
    inside = ((global_row >= 0) & (global_row < tile_rows * devices)).astype(jnp.float32)
    hidden_one = (hidden_wide * inside[None, :, None, None]).astype(jnp.bfloat16)
    padded_second = jax.nn.silu(hidden_one.astype(jnp.float32)).astype(jnp.bfloat16)
    latent = (source + convolve_rows(padded_second, conv_second, tap_weights)).astype(jnp.bfloat16)
    token_rows = tile_rows // 2
    token_cols = tile_cols // 2
    patches = (
        latent.reshape(frames, token_rows, 2, token_cols, 2, channels)
        .transpose(0, 1, 3, 2, 4, 5)
        .reshape(-1, 4 * channels)
    )
    tok_count = patches.shape[0]
    embedded = jnp.dot(patches, patch_weight, preferred_element_type=jnp.float32).astype(
        jnp.bfloat16
    )
    values_f = embedded.astype(jnp.float32)
    row_mean = jnp.mean(values_f, axis=-1, keepdims=True)
    centered = values_f - row_mean
    variance = jnp.mean(centered * centered, axis=-1, keepdims=True)
    normed = (centered / jnp.sqrt(variance + 1e-06)).astype(jnp.bfloat16)
    projected = jnp.dot(normed, qkv_weight, preferred_element_type=jnp.float32).reshape(
        tok_count, 3, HEADS, head_dim
    )
    stacked = jnp.stack(
        [
            rms_scale(projected[:, 0], query_gain),
            rms_scale(projected[:, 1], key_gain),
            projected[:, 2].astype(jnp.bfloat16),
        ],
        axis=1,
    )
    groups = devices // HEADS
    frame_share = frames // groups
    local_share = tok_count // groups
    span_rows = devices * local_share
    outgoing = (
        stacked.reshape(groups, local_share, 3, HEADS, head_dim)
        .transpose(0, 3, 1, 2, 4)
        .reshape(devices, local_share, 3 * head_dim)
    )
    incoming = lax.all_to_all(outgoing, "seq", split_axis=0, concat_axis=0, tiled=True)
    arranged = (
        incoming.reshape(devices, frame_share, token_rows * token_cols, 3, head_dim)
        .transpose(3, 1, 0, 2, 4)
        .reshape(3, span_rows, head_dim)
    )
    my_group = position // HEADS
    lengths = lax.dynamic_index_in_dim(window_lengths, my_group, 0, keepdims=False)
    window_ends = jnp.cumsum(lengths)
    token_index = jnp.arange(span_rows, dtype=jnp.int32)
    segment = jnp.sum((token_index[:, None] >= window_ends[None, :]).astype(jnp.int32), axis=1)
    key_rows = arranged[1]
    value_rows = arranged[2]
    block_rows = min(512, span_rows)
    block_count = span_rows // block_rows

    def attend_block(inputs):
        query_block, segment_block = inputs
        scores = jnp.dot(query_block, key_rows.T, preferred_element_type=jnp.float32) * score_scale
        allowed = segment_block[:, None] == segment[None, :]
        scores = jnp.where(allowed, scores, -1e30)
        row_peak = jnp.max(scores, axis=-1, keepdims=True)
        weights = jnp.exp(scores - row_peak)
        row_mass = jnp.sum(weights, axis=-1, keepdims=True)
        mixed = (
            jnp.dot(weights.astype(jnp.bfloat16), value_rows, preferred_element_type=jnp.float32)
            / row_mass
        )
        return mixed.astype(jnp.bfloat16)

    mixed_rows = lax.map(
        attend_block,
        (
            arranged[0].reshape(block_count, block_rows, head_dim),
            segment.reshape(block_count, block_rows),
        ),
    ).reshape(span_rows, head_dim)
    outgoing_back = (
        mixed_rows.reshape(frame_share, devices, token_rows * token_cols, head_dim)
        .transpose(1, 0, 2, 3)
        .reshape(devices, local_share, head_dim)
    )
    returned = lax.all_to_all(outgoing_back, "seq", split_axis=0, concat_axis=0, tiled=True)
    merged = (
        returned.reshape(groups, HEADS, local_share, head_dim)
        .transpose(0, 2, 1, 3)
        .reshape(tok_count, D)
    )
    projected_out = jnp.dot(
        merged,
        lax.all_gather(out_weight, "seq", axis=0, tiled=True),
        preferred_element_type=jnp.float32,
    )
    return projected_out.astype(jnp.bfloat16)


HD = D // HEADS
SLOT = 80
MASK = 1024.0
F32 = jnp.float32
BF16 = jnp.bfloat16
VMEM = pl.BlockSpec(memory_space=pltpu.VMEM)
SMEM = pl.BlockSpec(memory_space=pltpu.SMEM)
NT = (((1,), (1,)), ((), ()))


def params(mib=40):
    return pltpu.CompilerParams(vmem_limit_bytes=mib << 20)


def silu(v):
    return v / (1.0 + jnp.exp(-v))


def long_window(lengths):
    first, second = lengths[0, 0], lengths[0, 1]
    half = 1024
    start = jnp.where(first == half, 0, jnp.where(second == half, first, first + second))
    bound = jnp.where(first == half, half + second, first)
    return start, bound


ANY = pl.BlockSpec(memory_space=pl.ANY)
TN = (((0,), (1,)), ((), ()))


def pair_weights(weights, o, ch=128):
    blank = jnp.zeros((ch, ch), BF16)
    rows = []
    for four in range(4):
        for j in range(3):
            taps = [weights[o, four - r, j] if 0 <= four - r < 3 else blank for r in range(2)]
            rows.append(jnp.concatenate(taps, axis=1))
    return jnp.concatenate(rows, axis=0)


def fold_kernel(patch_any, qkv_any, folded_ref, query_ref, centered_ref, patch_ref, qkv_ref, sems):
    copies = [
        pltpu.make_async_copy(patch_any, patch_ref, sems.at[0]),
        pltpu.make_async_copy(qkv_any.at[:, pl.ds(D, D)], qkv_ref.at[0], sems.at[1]),
        pltpu.make_async_copy(qkv_any.at[:, pl.ds(2 * D, D)], qkv_ref.at[1], sems.at[2]),
        pltpu.make_async_copy(qkv_any.at[:, pl.ds(0, D)], query_ref, sems.at[3]),
    ]
    for copy in copies:
        copy.start()
    copies[0].wait()
    patch = patch_ref[...].astype(F32)
    centered_ref[...] = (patch - jnp.mean(patch, axis=1, keepdims=True)).astype(BF16)
    for part in range(2):
        copies[part + 1].wait()
        product = lax.dot_general(qkv_ref[part], centered_ref[...], TN, preferred_element_type=F32)
        folded_ref[part * D : (part + 1) * D] = product.astype(BF16)
    copies[3].wait()


def fold(patch_weight, qkv_weight):
    inner = patch_weight.shape[0]
    return pl.pallas_call(
        fold_kernel,
        out_shape=(
            jax.ShapeDtypeStruct((2 * D, inner), BF16),
            jax.ShapeDtypeStruct((D, D), BF16),
            jax.ShapeDtypeStruct((inner, D), BF16),
        ),
        in_specs=[ANY, ANY],
        out_specs=(VMEM, VMEM, VMEM),
        scratch_shapes=[
            pltpu.VMEM((inner, D), BF16),
            pltpu.VMEM((2, D, D), BF16),
            pltpu.SemaphoreType.DMA((4,)),
        ],
        compiler_params=params(),
        name="fold",
        cost_estimate=pl.CostEstimate(flops=2 * inner * D * 2 * D, bytes_accessed=12 << 20, transcendentals=0),
    )(patch_weight, qkv_weight)


def frame_taps(counts_ref, frames):
    def clip_of(frame):
        end = 0
        index = 0
        for c in range(counts_ref.shape[0]):
            end = end + counts_ref[c]
            index = index + jnp.where(frame >= end, 1, 0)
        return index

    own = [clip_of(f) for f in range(frames)]
    joined = [jnp.where(own[f] == own[f + 1], 1.0, 0.0) for f in range(frames - 1)]
    return [0.0] + joined, joined + [0.0]


def conv_kernel(
    counts_any, lengths_any, own_any, patch_any, sibling_ref, other_ref, first_ref, second_ref,
    keep_ref, send_ref, grid_one, grid_two, pixels, own_ref, patch_ref, counts_ref, lengths_ref, sems,
):
    copies = [
        pltpu.make_async_copy(own_any, own_ref, sems.at[0]),
        pltpu.make_async_copy(counts_any, counts_ref, sems.at[1]),
        pltpu.make_async_copy(lengths_any, lengths_ref, sems.at[2]),
        pltpu.make_async_copy(patch_any, patch_ref, sems.at[3]),
    ]
    for copy in copies:
        copy.start()
    frames, _, cols, ch = own_ref.shape
    wide = 12 * ch
    position = lax.axis_index("seq")
    column = lax.broadcasted_iota(jnp.int32, (frames, cols, ch), 1)

    def shifted(row):
        left = jnp.where(column == 0, 0.0, pltpu.roll(row, 1, 1))
        right = jnp.where(column == cols - 1, 0.0, pltpu.roll(row, cols - 1, 1))
        return [part.astype(BF16) for part in (left, row, right)]

    blank = jnp.zeros((cols, wide), BF16)
    for g in range(2):
        grid_one[g, 0] = blank
        grid_one[g, frames + 1] = blank
    grid_two[0] = blank
    grid_two[frames + 1] = blank
    on_first = position % 2 == 0

    def source_row(r):
        if r in (2, 3):
            return own_ref[:, r - 2].astype(F32)
        sibling, other = sibling_ref[:, r % 2].astype(F32), other_ref[:, r % 2].astype(F32)
        return jnp.where(on_first, other, sibling) if r < 2 else jnp.where(on_first, sibling, other)

    for r in (0, 1, 4, 5, 2, 3):
        if r == 2:
            copies[0].wait()
        row = silu(source_row(r))
        parts = shifted(row)
        for g in range(2):
            four = r - 2 * g
            if 0 <= four < 4:
                for j in range(3):
                    grid_one[g, 1 : frames + 1, :, (four * 3 + j) * ch : (four * 3 + j + 1) * ch] = parts[j]

    copies[1].wait()
    copies[2].wait()
    before_tap, after_tap = frame_taps(counts_ref, frames)

    def summed(terms):
        rows = []
        for f in range(frames):
            total = terms[1][f]
            if f > 0:
                total = total + before_tap[f] * terms[0][f]
            if f < frames - 1:
                total = total + after_tap[f] * terms[2][f]
            rows.append(total)
        return jnp.stack(rows)

    for g in range(2):
        terms = []
        for o in range(3):
            left = grid_one[g, o : o + frames].reshape(frames * cols, wide)
            terms.append(
                jnp.dot(left, pair_weights(first_ref, o), preferred_element_type=F32).reshape(frames, cols, 2 * ch)
            )
        hidden = summed(terms)
        for out_row in range(2):
            four = 2 * g + out_row
            row = hidden[:, :, out_row * ch : (out_row + 1) * ch]
            if four == 0:
                row = row * jnp.where(position == 0, 0.0, 1.0)
            if four == 3:
                row = row * jnp.where(position == lax.axis_size("seq") - 1, 0.0, 1.0)
            row = silu(row.astype(BF16).astype(F32))
            parts = shifted(row)
            for j in range(3):
                grid_two[1 : frames + 1, :, (four * 3 + j) * ch : (four * 3 + j + 1) * ch] = parts[j]
    terms = []
    for o in range(3):
        left = grid_two[o : o + frames].reshape(frames * cols, wide)
        terms.append(
            jnp.dot(left, pair_weights(second_ref, o), preferred_element_type=F32).reshape(frames, cols, 2 * ch)
        )
    residual = summed(terms)
    for out_row in range(2):
        block = own_ref[:, out_row].astype(F32) + residual[:, :, out_row * ch : (out_row + 1) * ch]
        pixels[out_row] = block.astype(BF16).astype(F32).reshape(frames * cols, ch)
    tokens = frames * cols // 2
    patches = jnp.concatenate(
        [pixels[a, pl.ds(b, tokens, 2), :] for a in range(2) for b in range(2)], axis=1
    )
    copies[3].wait()
    embedded = jnp.dot(patches.astype(BF16), patch_ref[...], preferred_element_type=F32)
    centered = embedded - jnp.mean(embedded, axis=1, keepdims=True)
    variance = jnp.mean(centered * centered, axis=1, keepdims=True)
    scaled = patches * (1.0 / jnp.sqrt(variance + 1e-06))
    half = tokens // 2
    low, high = scaled[:half], scaled[half:]
    start, _ = long_window(lengths_ref)
    q_cols = cols // 2
    slot = lax.broadcasted_iota(jnp.int32, low.shape, 0)
    token = (slot // q_cols) * (lax.axis_size("seq") * q_cols) + position * q_cols + slot % q_cols
    inside = jnp.where(token >= start, 1, 0)
    mine = inside == jnp.where(position % 2 == 0, 1, 0)
    keep = jnp.where(mine, low, high).astype(BF16)
    send = jnp.where(mine, high, low).astype(BF16)
    keep_ref[...] = keep
    send_ref[...] = send


def convolve(counts, lengths, clip, sibling_rows, other_rows, conv_first, conv_second, patch_weight):
    frames, _, cols, ch = clip.shape
    tokens = frames * cols // 2
    out = jax.ShapeDtypeStruct((tokens // 2, 4 * ch), BF16)
    return pl.pallas_call(
        conv_kernel,
        out_shape=(out, out),
        in_specs=[ANY] * 4 + [VMEM] * 4,
        out_specs=(VMEM, VMEM),
        scratch_shapes=[
            pltpu.VMEM((2, frames + 2, cols, 12 * ch), BF16),
            pltpu.VMEM((frames + 2, cols, 12 * ch), BF16),
            pltpu.VMEM((2, frames * cols, ch), F32),
            pltpu.VMEM(clip.shape, BF16),
            pltpu.VMEM(patch_weight.shape, BF16),
            pltpu.SMEM(counts.shape, jnp.int32),
            pltpu.SMEM(lengths.shape, jnp.int32),
            pltpu.SemaphoreType.DMA((4,)),
        ],
        compiler_params=params(),
        name="convolve",
        cost_estimate=pl.CostEstimate(flops=2 << 30, bytes_accessed=4 << 20, transcendentals=1 << 18),
    )(counts, lengths, clip, patch_weight, sibling_rows, other_rows, conv_first, conv_second)


def chip_at(place):
    chips = lax.axis_size("seq") // 2
    place = lax.rem(place + 2 * chips, chips)
    return jnp.where(place < chips // 2, 2 * place, 2 * (chips - 1 - place) + 1)


def ring_place():
    chips = lax.axis_size("seq") // 2
    chip = lax.axis_index("seq") // 2
    return jnp.where(chip % 2 == 0, chip // 2, chips - 1 - chip // 2)


def ring_pairs():
    size = lax.axis_size("seq")
    chips = size // 2
    order = [2 * i for i in range(chips // 2)] + [2 * i + 1 for i in reversed(range(chips // 2))]
    return [
        (2 * order[i] + core, 2 * order[(i + 1) % chips] + core) for i in range(chips) for core in range(2)
    ]


def window_sides(lengths_ref, chip, count):
    size = lax.axis_size("seq")
    core = lax.axis_index("seq") % 2
    start, bound = long_window(lengths_ref)
    lane = lax.broadcasted_iota(jnp.int32, (8, count), 1)
    half = count // 2
    slot = lane % half
    row = 2 * chip + jnp.where(lane < half, core, 1 - core)
    q_cols = 16
    token = (slot // q_cols) * (size * q_cols) + row * q_cols + slot % q_cols
    inside = jnp.where(token >= start, 1, 0)
    upper = inside != jnp.where(core == 0, 1, 0)
    token = jnp.where(upper, token + 4 * size * q_cols, token)
    return jnp.where(token < bound, 1.0, -1.0)


def normed_heads(part, gain):
    count = part.shape[1]
    heads = part.reshape(-1, HD, count)
    factor = lax.rsqrt(jnp.mean(heads * heads, axis=1, keepdims=True) + 1e-06)
    return heads * factor * gain[None]


def as_column(row):
    size = row.shape[1]
    square = (size, size)
    same = lax.broadcasted_iota(jnp.int32, square, 0) == lax.broadcasted_iota(jnp.int32, square, 1)
    return jnp.sum(jnp.where(same, jnp.broadcast_to(row, square), 0.0), axis=1, keepdims=True)


def attend(tokens, sides, folded, key_gain, queries, acc_ref, keys_ref, values_ref, scores_ref, weights_ref):
    count = tokens.shape[0]
    row = lax.broadcasted_iota(jnp.int32, (8, count), 0)
    key_tail = jnp.where(row == 0, sides, jnp.where(row == 1, 1.0, 0.0))
    value_tail = jnp.where(row == 0, 1.0, 0.0)
    heads_at_once = 4
    for first in range(0, HEADS, heads_at_once):
        rows = slice(first * HD, (first + heads_at_once) * HD)
        part = lax.dot_general(folded[rows], tokens, NT, preferred_element_type=F32)
        keys = normed_heads(part, key_gain)
        for h in range(heads_at_once):
            keys_ref[first + h] = jnp.concatenate([keys[h], key_tail], axis=0).astype(BF16)
            scores_ref[first + h] = jnp.dot(queries[first + h], keys_ref[first + h], preferred_element_type=F32)
    for first in range(0, HEADS, heads_at_once):
        rows = slice(D + first * HD, D + (first + heads_at_once) * HD)
        part = lax.dot_general(folded[rows], tokens, NT, preferred_element_type=F32)
        values = part.reshape(heads_at_once, HD, count)
        for h in range(heads_at_once):
            values_ref[first + h] = jnp.concatenate([values[h], value_tail], axis=0).astype(BF16)
    lane = lax.broadcasted_iota(jnp.int32, (128, 128), 1)
    peaks = jnp.zeros((128, 128), F32)
    for h in range(HEADS):
        scores = scores_ref[h]
        peak = jnp.max(scores, axis=1, keepdims=True)
        weights_ref[h] = jnp.exp2(scores - peak).astype(BF16)
        peaks = jnp.where(lane == h, peak, peaks)
    peaks = peaks.T
    tail_row = lax.broadcasted_iota(jnp.int32, (8, 128), 0)
    for h in range(HEADS):
        mixed = lax.dot_general(values_ref[h], weights_ref[h], NT, preferred_element_type=F32)
        acc_ref[h, :HD] = mixed[:HD]
        acc_ref[h, HD:] = jnp.where(tail_row == 1, peaks[h : h + 1], mixed[HD:])


def attend_scratch(count):
    return [
        pltpu.VMEM((HEADS, SLOT, count), BF16),
        pltpu.VMEM((HEADS, SLOT, count), BF16),
        pltpu.VMEM((HEADS, 128, count), F32),
        pltpu.VMEM((HEADS, 128, count), BF16),
    ]


def query_kernel(lengths_ref, block_ref, centered_ref, query_ref, query_gain_ref, queries_ref):
    normed = jnp.dot(block_ref[...], centered_ref[...], preferred_element_type=F32).astype(BF16)
    part = jnp.dot(normed, query_ref[...], preferred_element_type=F32).T
    count = part.shape[1]
    sides = window_sides(lengths_ref, lax.axis_index("seq") // 2, count)
    queries = normed_heads(part, as_column(query_gain_ref[...] * (math.log2(math.e) / math.sqrt(HD))))
    row = lax.broadcasted_iota(jnp.int32, (8, count), 0)
    tail = jnp.where(row == 0, MASK * sides, jnp.where(row == 1, -MASK, 0.0))
    for h in range(HEADS):
        queries_ref[h] = jnp.concatenate([queries[h], tail], axis=0).T.astype(BF16)


def make_queries(lengths, block, centered, query_weight, query_gain):
    return pl.pallas_call(
        query_kernel,
        out_shape=jax.ShapeDtypeStruct((HEADS, 128, SLOT), BF16),
        in_specs=[SMEM] + [VMEM] * 4,
        out_specs=VMEM,
        compiler_params=params(),
        name="queries",
        cost_estimate=pl.CostEstimate(flops=1 << 30, bytes_accessed=4 << 20, transcendentals=0),
    )(lengths, block, centered, query_weight, query_gain)


def step_kernel(offsets, lengths_ref, *refs):
    blocks = refs[: len(offsets)]
    folded_ref, key_gain_ref, queries_ref, acc_ref, *scratch = refs[len(offsets) :]
    place = ring_place()
    tokens = jnp.concatenate([ref[...] for ref in blocks], axis=0)
    sides = jnp.concatenate(
        [window_sides(lengths_ref, chip_at(place + offset), 128) for offset in dict.fromkeys(offsets)], axis=1
    )
    attend(tokens, sides, folded_ref, as_column(key_gain_ref[...]), queries_ref, acc_ref, *scratch)


ACC = jax.ShapeDtypeStruct((HEADS, SLOT, 128), F32)


def step_attention(offsets, lengths, blocks, folded, key_gain, queries):
    count = sum(block.shape[0] for block in blocks)
    flops = 2 * count * 2 * D * 512 + 4 * HEADS * 128 * 128 * count
    return pl.pallas_call(
        functools.partial(step_kernel, offsets),
        out_shape=ACC,
        in_specs=[SMEM] + [VMEM] * (len(blocks) + 3),
        out_specs=VMEM,
        scratch_shapes=attend_scratch(count),
        compiler_params=params(),
        name="step_attention",
        cost_estimate=pl.CostEstimate(flops=2 * flops, bytes_accessed=5 << 20, transcendentals=HEADS * 128 * count),
    )(lengths, *blocks, folded, key_gain, queries)


RING = (0, -1, 1, -2, 2, -3, 3, 4)


def out_kernel(parts, *refs):
    acc_refs = refs[:parts]
    weight_refs = refs[parts:-3]
    keep_ref, send_ref, mixed_ref = refs[-3:]
    for h in range(HEADS):
        peaks = [acc[h, HD + 1 : HD + 2] for acc in acc_refs]
        peak = functools.reduce(jnp.maximum, peaks)
        total = None
        for acc, own in zip(acc_refs, peaks):
            term = acc[h] * jnp.exp2(own - peak)
            total = term if total is None else total + term
        mixed_ref[h] = total[:HD] / total[HD : HD + 1]
    place = ring_place()
    core = lax.axis_index("seq") % 2
    lefts = []
    for side in range(2):
        heads = [2 * chip_at(place + offset) + jnp.where(core == side, 0, 1) for offset in RING]
        lefts.append(jnp.concatenate([mixed_ref[head] for head in heads], axis=0).T.astype(BF16))
    half = keep_ref.shape[0]
    for first in range(0, D, 256):
        columns = slice(first, min(first + 256, D))
        result = jnp.dot(lefts[0], weight_refs[0][:, columns], preferred_element_type=F32)
        result = result + jnp.dot(lefts[1], weight_refs[1][:, columns], preferred_element_type=F32)
        result = result.astype(BF16)
        keep_ref[:, columns] = result[:half]
        send_ref[:, columns] = result[half:]


def project_out(accs, weights):
    out = jax.ShapeDtypeStruct((64, D), BF16)
    return pl.pallas_call(
        functools.partial(out_kernel, len(accs)),
        out_shape=(out, out),
        in_specs=[VMEM] * (len(accs) + len(weights)),
        out_specs=(VMEM, VMEM),
        scratch_shapes=[pltpu.VMEM((HEADS, HD, 128), F32)],
        compiler_params=params(),
        name="project_out",
        cost_estimate=pl.CostEstimate(flops=2 * 128 * 1280 * D, bytes_accessed=4 << 20, transcendentals=0),
    )(*accs, *weights)


def pack_kernel(*refs):
    out_ref = refs[-1]
    for i in range(7):
        out_ref[i] = refs[i][...]
    cut = refs[7].shape[1]
    out_ref[7, :, :cut] = refs[7][...]
    out_ref[7, :, cut:] = refs[8][...]


def pack(pieces):
    rows, columns = pieces[0].shape
    out = pl.pallas_call(
        pack_kernel,
        out_shape=jax.ShapeDtypeStruct((8, rows, columns), BF16),
        in_specs=[VMEM] * 9,
        out_specs=VMEM,
        compiler_params=params(),
        name="pack",
    )(*pieces)
    return out.reshape(8 * rows, columns)


def merge_kernel(lengths_ref, keep_ref, got_ref, out_ref):
    position = lax.axis_index("seq")
    keep = keep_ref[...].astype(F32)
    got = got_ref[...].astype(F32)
    start, _ = long_window(lengths_ref)
    q_cols = 16
    slot = lax.broadcasted_iota(jnp.int32, keep.shape, 0)
    token = (slot // q_cols) * (lax.axis_size("seq") * q_cols) + position * q_cols + slot % q_cols
    inside = jnp.where(token >= start, 1, 0)
    mine = inside == jnp.where(position % 2 == 0, 1, 0)
    half = keep.shape[0]
    out_ref[:half] = jnp.where(mine, keep, got).astype(BF16)
    out_ref[half:] = jnp.where(mine, got, keep).astype(BF16)


def merge(lengths, keep, got):
    return pl.pallas_call(
        merge_kernel,
        out_shape=jax.ShapeDtypeStruct((128, D), BF16),
        in_specs=[SMEM, VMEM, VMEM],
        out_specs=VMEM,
        compiler_params=params(),
        name="merge",
    )(lengths, keep, got)


def shards(
    clip, frame_counts, conv_first, conv_second, patch_weight, qkv_weight, query_gain, key_gain,
    out_weight, window_lengths,
):
    size = lax.axis_size("seq")
    facing = [(i, j) for i in range(1, size - 1, 2) for i, j in ((i, i + 1), (i + 1, i))]
    cores = [(i, i ^ 1) for i in range(size)]
    forward = ring_pairs()
    backward = [(j, i) for i, j in forward]

    def send(array, pairs):
        return lax.ppermute(array, "seq", pairs)

    def tied(*arrays):
        return lax.optimization_barrier(arrays)

    def tied(*arrays):
        return lax.optimization_barrier(arrays)

    def both_ways(ahead, behind):
        return send(ahead, forward), send(behind, backward)

    def tied(*arrays):
        return lax.optimization_barrier(arrays)

    def both_ways(ahead, behind):
        return send(ahead, forward), send(behind, backward)

    sibling_rows = send(clip, cores)
    other_rows = send(clip, facing)
    query_row, key_row = query_gain[None], key_gain[None]
    weight_one = both_ways(out_weight, out_weight)
    folded, query_weight, centered = fold(patch_weight, qkv_weight)
    sibling_rows, other_rows, *weight_one, folded = tied(sibling_rows, other_rows, *weight_one, folded)
    weight_two = both_ways(*weight_one)
    keep, other = convolve(
        frame_counts, window_lengths, clip, sibling_rows, other_rows, conv_first, conv_second, patch_weight
    )
    got = send(other, cores)
    got, wu_a, wu_b = tied(got, *weight_two)
    weight_two = (wu_a, wu_b)
    weight_three = both_ways(*weight_two)
    block = jnp.concatenate([keep, got], axis=0)
    one = both_ways(block, block)
    queries = make_queries(window_lengths, block, centered, query_weight, query_row)
    *one, queries = tied(*one, queries)
    two = both_ways(*one)
    acc_one = step_attention((-1, 1), window_lengths, one, folded, key_row, queries)
    wt_a, wt_b, acc_one = tied(*weight_three, acc_one)
    cut = 640
    weight_four = both_ways(wt_a[:, :cut], wt_b[:, cut:])
    *two, acc_one = tied(*two, acc_one)
    three = both_ways(*two)
    acc_two = step_attention((-2, 2), window_lengths, two, folded, key_row, queries)
    *three, acc_two, wf_a, wf_b = tied(*three, acc_two, *weight_four)
    four = both_ways(three[0][:64], three[1][64:])
    weights = pack([out_weight, *weight_one, *weight_two, wt_a, wt_b, wf_a, wf_b])
    sibling = send(weights, cores)
    acc_three = step_attention((-3, 3), window_lengths, three, folded, key_row, queries)
    *four, acc_three = tied(*four, acc_three)
    acc_four = step_attention((0, 4, 4), window_lengths, [block, *four], folded, key_row, queries)
    keep_rows, send_rows = project_out((acc_one, acc_two, acc_three, acc_four), (weights, sibling))
    return merge(window_lengths, keep_rows, send(send_rows, cores))


def solution(mesh):
    own = mesh.shape["seq"] == HEADS
    return jax.shard_map(
        shards if own else general_shards,
        mesh=mesh,
        in_specs=(
            P("groups", "seq", None, None),
            P("groups"),
            P(),
            P(),
            P(),
            P(),
            P(),
            P(),
            P("seq", None),
            P("groups", None),
        ),
        out_specs=P(("groups", "seq"), None),
        check_vma=False,
    )
```

```python
import functools
import math

import jax
import jax.numpy as jnp
from jax import lax
from jax.experimental import pallas as pl
from jax.experimental.pallas import tpu as pltpu
from jax.sharding import PartitionSpec as P

D = 1152
HEADS = 16


def extended(array, sides, width):
    for axis, dim in sides:
        size, length = (lax.axis_size(axis), array.shape[dim])
        up = [(i, (i + 1) % size) for i in range(size - 1)]
        down = [(j, i) for i, j in up]
        last = lax.slice_in_dim(array, length - width, length, axis=dim)
        first = lax.slice_in_dim(array, 0, width, axis=dim)
        before = lax.ppermute(last, axis, up)
        after = lax.ppermute(first, axis, down)
        array = jnp.concatenate([before, array, after], axis=dim)
    return array


def frame_weights(frame_counts, frames):
    position = jnp.arange(frames, dtype=jnp.int32)
    clip_ends = jnp.cumsum(frame_counts)

    def clip_of(index):
        return jnp.sum((index[:, None] >= clip_ends[None, :]).astype(jnp.int32), axis=1)

    own_clip = clip_of(position)
    columns = []
    for offset in (-1, 0, 1):
        neighbor = position + offset
        inside = (neighbor >= 0) & (neighbor < frames)
        same_clip = clip_of(jnp.clip(neighbor, 0, frames - 1)) == own_clip
        columns.append((inside & same_clip).astype(jnp.float32))
    return jnp.stack(columns, axis=1)


def convolve_rows(activation, kernel, tap_weights):
    empty_frame = jnp.zeros_like(activation[:1])
    shifted = (
        jnp.concatenate([empty_frame, activation[:-1]], 0),
        activation,
        jnp.concatenate([activation[1:], empty_frame], 0),
    )
    summed = None
    for offset in range(3):
        response = lax.conv_general_dilated(
            shifted[offset],
            kernel[offset],
            (1, 1),
            ((0, 0), (1, 1)),
            dimension_numbers=("NHWC", "HWIO", "NHWC"),
            preferred_element_type=jnp.float32,
        )
        tap_term = tap_weights[:, offset][:, None, None, None] * response
        summed = tap_term if offset == 0 else summed + tap_term
    return summed


def rms_scale(part, gain):
    factor = lax.rsqrt(jnp.mean(part * part, axis=-1, keepdims=True) + 1e-06)
    return (part * factor * gain).astype(jnp.bfloat16)


def general_shards(
    clip,
    frame_counts,
    conv_first,
    conv_second,
    patch_weight,
    qkv_weight,
    query_gain,
    key_gain,
    out_weight,
    window_lengths,
):
    frames, tile_rows, tile_cols, channels = clip.shape
    devices = lax.axis_size("seq")
    position = lax.axis_index("seq")
    head_dim = D // HEADS
    score_scale = 1.0 / math.sqrt(head_dim)
    tap_weights = frame_weights(frame_counts, frames)
    source = clip.astype(jnp.float32)
    padded_clip = extended(clip, (("seq", 1),), 2)
    first_in = jax.nn.silu(padded_clip.astype(jnp.float32)).astype(jnp.bfloat16)
    hidden_wide = convolve_rows(first_in, conv_first, tap_weights)
    global_row = position * tile_rows - 1 + jnp.arange(tile_rows + 2, dtype=jnp.int32)
    inside = ((global_row >= 0) & (global_row < tile_rows * devices)).astype(jnp.float32)
    hidden_one = (hidden_wide * inside[None, :, None, None]).astype(jnp.bfloat16)
    padded_second = jax.nn.silu(hidden_one.astype(jnp.float32)).astype(jnp.bfloat16)
    latent = (source + convolve_rows(padded_second, conv_second, tap_weights)).astype(jnp.bfloat16)
    token_rows = tile_rows // 2
    token_cols = tile_cols // 2
    patches = (
        latent.reshape(frames, token_rows, 2, token_cols, 2, channels)
        .transpose(0, 1, 3, 2, 4, 5)
        .reshape(-1, 4 * channels)
    )
    tok_count = patches.shape[0]
    embedded = jnp.dot(patches, patch_weight, preferred_element_type=jnp.float32).astype(
        jnp.bfloat16
    )
    values_f = embedded.astype(jnp.float32)
    row_mean = jnp.mean(values_f, axis=-1, keepdims=True)
    centered = values_f - row_mean
    variance = jnp.mean(centered * centered, axis=-1, keepdims=True)
    normed = (centered / jnp.sqrt(variance + 1e-06)).astype(jnp.bfloat16)
    projected = jnp.dot(normed, qkv_weight, preferred_element_type=jnp.float32).reshape(
        tok_count, 3, HEADS, head_dim
    )
    stacked = jnp.stack(
        [
            rms_scale(projected[:, 0], query_gain),
            rms_scale(projected[:, 1], key_gain),
            projected[:, 2].astype(jnp.bfloat16),
        ],
        axis=1,
    )
    groups = devices // HEADS
    frame_share = frames // groups
    local_share = tok_count // groups
    span_rows = devices * local_share
    outgoing = (
        stacked.reshape(groups, local_share, 3, HEADS, head_dim)
        .transpose(0, 3, 1, 2, 4)
        .reshape(devices, local_share, 3 * head_dim)
    )
    incoming = lax.all_to_all(outgoing, "seq", split_axis=0, concat_axis=0, tiled=True)
    arranged = (
        incoming.reshape(devices, frame_share, token_rows * token_cols, 3, head_dim)
        .transpose(3, 1, 0, 2, 4)
        .reshape(3, span_rows, head_dim)
    )
    my_group = position // HEADS
    lengths = lax.dynamic_index_in_dim(window_lengths, my_group, 0, keepdims=False)
    window_ends = jnp.cumsum(lengths)
    token_index = jnp.arange(span_rows, dtype=jnp.int32)
    segment = jnp.sum((token_index[:, None] >= window_ends[None, :]).astype(jnp.int32), axis=1)
    key_rows = arranged[1]
    value_rows = arranged[2]
    block_rows = min(512, span_rows)
    block_count = span_rows // block_rows

    def attend_block(inputs):
        query_block, segment_block = inputs
        scores = jnp.dot(query_block, key_rows.T, preferred_element_type=jnp.float32) * score_scale
        allowed = segment_block[:, None] == segment[None, :]
        scores = jnp.where(allowed, scores, -1e30)
        row_peak = jnp.max(scores, axis=-1, keepdims=True)
        weights = jnp.exp(scores - row_peak)
        row_mass = jnp.sum(weights, axis=-1, keepdims=True)
        mixed = (
            jnp.dot(weights.astype(jnp.bfloat16), value_rows, preferred_element_type=jnp.float32)
            / row_mass
        )
        return mixed.astype(jnp.bfloat16)

    mixed_rows = lax.map(
        attend_block,
        (
            arranged[0].reshape(block_count, block_rows, head_dim),
            segment.reshape(block_count, block_rows),
        ),
    ).reshape(span_rows, head_dim)
    outgoing_back = (
        mixed_rows.reshape(frame_share, devices, token_rows * token_cols, head_dim)
        .transpose(1, 0, 2, 3)
        .reshape(devices, local_share, head_dim)
    )
    returned = lax.all_to_all(outgoing_back, "seq", split_axis=0, concat_axis=0, tiled=True)
    merged = (
        returned.reshape(groups, HEADS, local_share, head_dim)
        .transpose(0, 2, 1, 3)
        .reshape(tok_count, D)
    )
    projected_out = jnp.dot(
        merged,
        lax.all_gather(out_weight, "seq", axis=0, tiled=True),
        preferred_element_type=jnp.float32,
    )
    return projected_out.astype(jnp.bfloat16)


HD = D // HEADS
SLOT = 80
MASK = 1024.0
F32 = jnp.float32
BF16 = jnp.bfloat16
VMEM = pl.BlockSpec(memory_space=pltpu.VMEM)
SMEM = pl.BlockSpec(memory_space=pltpu.SMEM)
NT = (((1,), (1,)), ((), ()))


def params(mib=40):
    return pltpu.CompilerParams(vmem_limit_bytes=mib << 20)


def silu(v):
    return v / (1.0 + jnp.exp(-v))


def long_window(lengths):
    first, second = lengths[0, 0], lengths[0, 1]
    half = 1024
    start = jnp.where(first == half, 0, jnp.where(second == half, first, first + second))
    bound = jnp.where(first == half, half + second, first)
    return start, bound


ANY = pl.BlockSpec(memory_space=pl.ANY)
TN = (((0,), (1,)), ((), ()))


def pair_weights(weights, o, ch=128):
    blank = jnp.zeros((ch, ch), BF16)
    rows = []
    for four in range(4):
        for j in range(3):
            taps = [weights[o, four - r, j] if 0 <= four - r < 3 else blank for r in range(2)]
            rows.append(jnp.concatenate(taps, axis=1))
    return jnp.concatenate(rows, axis=0)


def fold_kernel(patch_any, qkv_any, folded_ref, query_ref, centered_ref, patch_ref, qkv_ref, sems):
    copies = [
        pltpu.make_async_copy(patch_any, patch_ref, sems.at[0]),
        pltpu.make_async_copy(qkv_any.at[:, pl.ds(D, D)], qkv_ref.at[0], sems.at[1]),
        pltpu.make_async_copy(qkv_any.at[:, pl.ds(2 * D, D)], qkv_ref.at[1], sems.at[2]),
        pltpu.make_async_copy(qkv_any.at[:, pl.ds(0, D)], query_ref, sems.at[3]),
    ]
    for copy in copies:
        copy.start()
    copies[0].wait()
    patch = patch_ref[...].astype(F32)
    centered_ref[...] = (patch - jnp.mean(patch, axis=1, keepdims=True)).astype(BF16)
    for part in range(2):
        copies[part + 1].wait()
        product = lax.dot_general(qkv_ref[part], centered_ref[...], TN, preferred_element_type=F32)
        folded_ref[part * D : (part + 1) * D] = product.astype(BF16)
    copies[3].wait()


def fold(patch_weight, qkv_weight):
    inner = patch_weight.shape[0]
    return pl.pallas_call(
        fold_kernel,
        out_shape=(
            jax.ShapeDtypeStruct((2 * D, inner), BF16),
            jax.ShapeDtypeStruct((D, D), BF16),
            jax.ShapeDtypeStruct((inner, D), BF16),
        ),
        in_specs=[ANY, ANY],
        out_specs=(VMEM, VMEM, VMEM),
        scratch_shapes=[
            pltpu.VMEM((inner, D), BF16),
            pltpu.VMEM((2, D, D), BF16),
            pltpu.SemaphoreType.DMA((4,)),
        ],
        compiler_params=params(),
        name="fold",
        cost_estimate=pl.CostEstimate(flops=2 * inner * D * 2 * D, bytes_accessed=12 << 20, transcendentals=0),
    )(patch_weight, qkv_weight)


def frame_taps(counts_ref, frames):
    def clip_of(frame):
        end = 0
        index = 0
        for c in range(counts_ref.shape[0]):
            end = end + counts_ref[c]
            index = index + jnp.where(frame >= end, 1, 0)
        return index

    own = [clip_of(f) for f in range(frames)]
    joined = [jnp.where(own[f] == own[f + 1], 1.0, 0.0) for f in range(frames - 1)]
    return [0.0] + joined, joined + [0.0]


def conv_kernel(
    counts_any, lengths_any, own_any, patch_any, sibling_ref, other_ref, first_ref, second_ref,
    keep_ref, send_ref, grid_one, grid_two, pixels, own_ref, patch_ref, counts_ref, lengths_ref, sems,
):
    copies = [
        pltpu.make_async_copy(own_any, own_ref, sems.at[0]),
        pltpu.make_async_copy(counts_any, counts_ref, sems.at[1]),
        pltpu.make_async_copy(lengths_any, lengths_ref, sems.at[2]),
        pltpu.make_async_copy(patch_any, patch_ref, sems.at[3]),
    ]
    for copy in copies:
        copy.start()
    frames, _, cols, ch = own_ref.shape
    wide = 12 * ch
    position = lax.axis_index("seq")
    column = lax.broadcasted_iota(jnp.int32, (frames, cols, ch), 1)

    def shifted(row):
        left = jnp.where(column == 0, 0.0, pltpu.roll(row, 1, 1))
        right = jnp.where(column == cols - 1, 0.0, pltpu.roll(row, cols - 1, 1))
        return [part.astype(BF16) for part in (left, row, right)]

    blank = jnp.zeros((cols, wide), BF16)
    for g in range(2):
        grid_one[g, 0] = blank
        grid_one[g, frames + 1] = blank
    grid_two[0] = blank
    grid_two[frames + 1] = blank
    on_first = position % 2 == 0

    def source_row(r):
        if r in (2, 3):
            return own_ref[:, r - 2].astype(F32)
        sibling, other = sibling_ref[:, r % 2].astype(F32), other_ref[:, r % 2].astype(F32)
        return jnp.where(on_first, other, sibling) if r < 2 else jnp.where(on_first, sibling, other)

    for r in (0, 1, 4, 5, 2, 3):
        if r == 2:
            copies[0].wait()
        row = silu(source_row(r))
        parts = shifted(row)
        for g in range(2):
            four = r - 2 * g
            if 0 <= four < 4:
                for j in range(3):
                    grid_one[g, 1 : frames + 1, :, (four * 3 + j) * ch : (four * 3 + j + 1) * ch] = parts[j]

    copies[1].wait()
    copies[2].wait()
    before_tap, after_tap = frame_taps(counts_ref, frames)

    def summed(terms):
        rows = []
        for f in range(frames):
            total = terms[1][f]
            if f > 0:
                total = total + before_tap[f] * terms[0][f]
            if f < frames - 1:
                total = total + after_tap[f] * terms[2][f]
            rows.append(total)
        return jnp.stack(rows)

    for g in range(2):
        terms = []
        for o in range(3):
            left = grid_one[g, o : o + frames].reshape(frames * cols, wide)
            terms.append(
                jnp.dot(left, pair_weights(first_ref, o), preferred_element_type=F32).reshape(frames, cols, 2 * ch)
            )
        hidden = summed(terms)
        for out_row in range(2):
            four = 2 * g + out_row
            row = hidden[:, :, out_row * ch : (out_row + 1) * ch]
            if four == 0:
                row = row * jnp.where(position == 0, 0.0, 1.0)
            if four == 3:
                row = row * jnp.where(position == lax.axis_size("seq") - 1, 0.0, 1.0)
            row = silu(row.astype(BF16).astype(F32))
            parts = shifted(row)
            for j in range(3):
                grid_two[1 : frames + 1, :, (four * 3 + j) * ch : (four * 3 + j + 1) * ch] = parts[j]
    terms = []
    for o in range(3):
        left = grid_two[o : o + frames].reshape(frames * cols, wide)
        terms.append(
            jnp.dot(left, pair_weights(second_ref, o), preferred_element_type=F32).reshape(frames, cols, 2 * ch)
        )
    residual = summed(terms)
    for out_row in range(2):
        block = own_ref[:, out_row].astype(F32) + residual[:, :, out_row * ch : (out_row + 1) * ch]
        pixels[out_row] = block.astype(BF16).astype(F32).reshape(frames * cols, ch)
    tokens = frames * cols // 2
    patches = jnp.concatenate(
        [pixels[a, pl.ds(b, tokens, 2), :] for a in range(2) for b in range(2)], axis=1
    )
    copies[3].wait()
    embedded = jnp.dot(patches.astype(BF16), patch_ref[...], preferred_element_type=F32)
    centered = embedded - jnp.mean(embedded, axis=1, keepdims=True)
    variance = jnp.mean(centered * centered, axis=1, keepdims=True)
    scaled = patches * (1.0 / jnp.sqrt(variance + 1e-06))
    half = tokens // 2
    low, high = scaled[:half], scaled[half:]
    start, _ = long_window(lengths_ref)
    q_cols = cols // 2
    slot = lax.broadcasted_iota(jnp.int32, low.shape, 0)
    token = (slot // q_cols) * (lax.axis_size("seq") * q_cols) + position * q_cols + slot % q_cols
    inside = jnp.where(token >= start, 1, 0)
    mine = inside == jnp.where(position % 2 == 0, 1, 0)
    keep = jnp.where(mine, low, high).astype(BF16)
    send = jnp.where(mine, high, low).astype(BF16)
    keep_ref[...] = keep
    send_ref[...] = send


def convolve(counts, lengths, clip, sibling_rows, other_rows, conv_first, conv_second, patch_weight):
    frames, _, cols, ch = clip.shape
    tokens = frames * cols // 2
    out = jax.ShapeDtypeStruct((tokens // 2, 4 * ch), BF16)
    return pl.pallas_call(
        conv_kernel,
        out_shape=(out, out),
        in_specs=[ANY] * 4 + [VMEM] * 4,
        out_specs=(VMEM, VMEM),
        scratch_shapes=[
            pltpu.VMEM((2, frames + 2, cols, 12 * ch), BF16),
            pltpu.VMEM((frames + 2, cols, 12 * ch), BF16),
            pltpu.VMEM((2, frames * cols, ch), F32),
            pltpu.VMEM(clip.shape, BF16),
            pltpu.VMEM(patch_weight.shape, BF16),
            pltpu.SMEM(counts.shape, jnp.int32),
            pltpu.SMEM(lengths.shape, jnp.int32),
            pltpu.SemaphoreType.DMA((4,)),
        ],
        compiler_params=params(),
        name="convolve",
        cost_estimate=pl.CostEstimate(flops=2 << 30, bytes_accessed=4 << 20, transcendentals=1 << 18),
    )(counts, lengths, clip, patch_weight, sibling_rows, other_rows, conv_first, conv_second)


def chip_at(place):
    chips = lax.axis_size("seq") // 2
    place = lax.rem(place + 2 * chips, chips)
    return jnp.where(place < chips // 2, 2 * place, 2 * (chips - 1 - place) + 1)


def ring_place():
    chips = lax.axis_size("seq") // 2
    chip = lax.axis_index("seq") // 2
    return jnp.where(chip % 2 == 0, chip // 2, chips - 1 - chip // 2)


def ring_pairs():
    size = lax.axis_size("seq")
    chips = size // 2
    order = [2 * i for i in range(chips // 2)] + [2 * i + 1 for i in reversed(range(chips // 2))]
    return [
        (2 * order[i] + core, 2 * order[(i + 1) % chips] + core) for i in range(chips) for core in range(2)
    ]


def window_sides(lengths_ref, chip, count):
    size = lax.axis_size("seq")
    core = lax.axis_index("seq") % 2
    start, bound = long_window(lengths_ref)
    lane = lax.broadcasted_iota(jnp.int32, (8, count), 1)
    half = count // 2
    slot = lane % half
    row = 2 * chip + jnp.where(lane < half, core, 1 - core)
    q_cols = 16
    token = (slot // q_cols) * (size * q_cols) + row * q_cols + slot % q_cols
    inside = jnp.where(token >= start, 1, 0)
    upper = inside != jnp.where(core == 0, 1, 0)
    token = jnp.where(upper, token + 4 * size * q_cols, token)
    return jnp.where(token < bound, 1.0, -1.0)


def normed_heads(part, gain):
    count = part.shape[1]
    heads = part.reshape(-1, HD, count)
    factor = lax.rsqrt(jnp.mean(heads * heads, axis=1, keepdims=True) + 1e-06)
    return heads * factor * gain[None]


def as_column(row):
    size = row.shape[1]
    square = (size, size)
    same = lax.broadcasted_iota(jnp.int32, square, 0) == lax.broadcasted_iota(jnp.int32, square, 1)
    return jnp.sum(jnp.where(same, jnp.broadcast_to(row, square), 0.0), axis=1, keepdims=True)


def attend(tokens, sides, folded, key_gain, queries, acc_ref, keys_ref, values_ref, scores_ref, weights_ref):
    count = tokens.shape[0]
    row = lax.broadcasted_iota(jnp.int32, (8, count), 0)
    key_tail = jnp.where(row == 0, sides, jnp.where(row == 1, 1.0, 0.0))
    value_tail = jnp.where(row == 0, 1.0, 0.0)
    heads_at_once = 4
    for first in range(0, HEADS, heads_at_once):
        rows = slice(first * HD, (first + heads_at_once) * HD)
        part = lax.dot_general(folded[rows], tokens, NT, preferred_element_type=F32)
        keys = normed_heads(part, key_gain)
        for h in range(heads_at_once):
            keys_ref[first + h] = jnp.concatenate([keys[h], key_tail], axis=0).astype(BF16)
    for first in range(0, HEADS, heads_at_once):
        rows = slice(D + first * HD, D + (first + heads_at_once) * HD)
        part = lax.dot_general(folded[rows], tokens, NT, preferred_element_type=F32)
        values = part.reshape(heads_at_once, HD, count)
        for h in range(heads_at_once):
            values_ref[first + h] = jnp.concatenate([values[h], value_tail], axis=0).astype(BF16)
    for h in range(HEADS):
        scores_ref[h] = jnp.dot(queries[h], keys_ref[h], preferred_element_type=F32)
    lane = lax.broadcasted_iota(jnp.int32, (128, 128), 1)
    peaks = jnp.zeros((128, 128), F32)
    for h in range(HEADS):
        scores = scores_ref[h]
        peak = jnp.max(scores, axis=1, keepdims=True)
        weights_ref[h] = jnp.exp2(scores - peak).astype(BF16)
        peaks = jnp.where(lane == h, peak, peaks)
    peaks = peaks.T
    tail_row = lax.broadcasted_iota(jnp.int32, (8, 128), 0)
    for h in range(HEADS):
        mixed = lax.dot_general(values_ref[h], weights_ref[h], NT, preferred_element_type=F32)
        acc_ref[h, :HD] = mixed[:HD]
        acc_ref[h, HD:] = jnp.where(tail_row == 1, peaks[h : h + 1], mixed[HD:])


def attend_scratch(count):
    return [
        pltpu.VMEM((HEADS, SLOT, count), BF16),
        pltpu.VMEM((HEADS, SLOT, count), BF16),
        pltpu.VMEM((HEADS, 128, count), F32),
        pltpu.VMEM((HEADS, 128, count), BF16),
    ]


def query_kernel(lengths_ref, block_ref, centered_ref, query_ref, query_gain_ref, queries_ref):
    normed = jnp.dot(block_ref[...], centered_ref[...], preferred_element_type=F32).astype(BF16)
    part = jnp.dot(normed, query_ref[...], preferred_element_type=F32).T
    count = part.shape[1]
    sides = window_sides(lengths_ref, lax.axis_index("seq") // 2, count)
    queries = normed_heads(part, as_column(query_gain_ref[...] * (math.log2(math.e) / math.sqrt(HD))))
    row = lax.broadcasted_iota(jnp.int32, (8, count), 0)
    tail = jnp.where(row == 0, MASK * sides, jnp.where(row == 1, -MASK, 0.0))
    for h in range(HEADS):
        queries_ref[h] = jnp.concatenate([queries[h], tail], axis=0).T.astype(BF16)


def make_queries(lengths, block, centered, query_weight, query_gain):
    return pl.pallas_call(
        query_kernel,
        out_shape=jax.ShapeDtypeStruct((HEADS, 128, SLOT), BF16),
        in_specs=[SMEM] + [VMEM] * 4,
        out_specs=VMEM,
        compiler_params=params(),
        name="queries",
        cost_estimate=pl.CostEstimate(flops=1 << 30, bytes_accessed=4 << 20, transcendentals=0),
    )(lengths, block, centered, query_weight, query_gain)


def step_kernel(offsets, lengths_ref, *refs):
    blocks = refs[: len(offsets)]
    folded_ref, key_gain_ref, queries_ref, acc_ref, *scratch = refs[len(offsets) :]
    place = ring_place()
    tokens = jnp.concatenate([ref[...] for ref in blocks], axis=0)
    sides = jnp.concatenate(
        [window_sides(lengths_ref, chip_at(place + offset), 128) for offset in dict.fromkeys(offsets)], axis=1
    )
    attend(tokens, sides, folded_ref, as_column(key_gain_ref[...]), queries_ref, acc_ref, *scratch)


ACC = jax.ShapeDtypeStruct((HEADS, SLOT, 128), F32)


def step_attention(offsets, lengths, blocks, folded, key_gain, queries):
    count = sum(block.shape[0] for block in blocks)
    flops = 2 * count * 2 * D * 512 + 4 * HEADS * 128 * 128 * count
    return pl.pallas_call(
        functools.partial(step_kernel, offsets),
        out_shape=ACC,
        in_specs=[SMEM] + [VMEM] * (len(blocks) + 3),
        out_specs=VMEM,
        scratch_shapes=attend_scratch(count),
        compiler_params=params(),
        name="step_attention",
        cost_estimate=pl.CostEstimate(flops=2 * flops, bytes_accessed=5 << 20, transcendentals=HEADS * 128 * count),
    )(lengths, *blocks, folded, key_gain, queries)


RING = (0, -1, 1, -2, 2, -3, 3, 4)


def out_kernel(parts, *refs):
    acc_refs = refs[:parts]
    weight_refs = refs[parts:-3]
    keep_ref, send_ref, mixed_ref = refs[-3:]
    for h in range(HEADS):
        peaks = [acc[h, HD + 1 : HD + 2] for acc in acc_refs]
        peak = functools.reduce(jnp.maximum, peaks)
        total = None
        for acc, own in zip(acc_refs, peaks):
            term = acc[h] * jnp.exp2(own - peak)
            total = term if total is None else total + term
        mixed_ref[h] = total[:HD] / total[HD : HD + 1]
    place = ring_place()
    core = lax.axis_index("seq") % 2
    lefts = []
    for side in range(2):
        heads = [2 * chip_at(place + offset) + jnp.where(core == side, 0, 1) for offset in RING]
        lefts.append(jnp.concatenate([mixed_ref[head] for head in heads], axis=0).T.astype(BF16))
    half = keep_ref.shape[0]
    for first in range(0, D, 256):
        columns = slice(first, min(first + 256, D))
        result = jnp.dot(lefts[0], weight_refs[0][:, columns], preferred_element_type=F32)
        result = result + jnp.dot(lefts[1], weight_refs[1][:, columns], preferred_element_type=F32)
        result = result.astype(BF16)
        keep_ref[:, columns] = result[:half]
        send_ref[:, columns] = result[half:]


def project_out(accs, weights):
    out = jax.ShapeDtypeStruct((64, D), BF16)
    return pl.pallas_call(
        functools.partial(out_kernel, len(accs)),
        out_shape=(out, out),
        in_specs=[VMEM] * (len(accs) + len(weights)),
        out_specs=(VMEM, VMEM),
        scratch_shapes=[pltpu.VMEM((HEADS, HD, 128), F32)],
        compiler_params=params(),
        name="project_out",
        cost_estimate=pl.CostEstimate(flops=2 * 128 * 1280 * D, bytes_accessed=4 << 20, transcendentals=0),
    )(*accs, *weights)


def pack_kernel(*refs):
    out_ref = refs[-1]
    for i in range(7):
        out_ref[i] = refs[i][...]
    cut = refs[7].shape[1]
    out_ref[7, :, :cut] = refs[7][...]
    out_ref[7, :, cut:] = refs[8][...]


def pack(pieces):
    rows, columns = pieces[0].shape
    out = pl.pallas_call(
        pack_kernel,
        out_shape=jax.ShapeDtypeStruct((8, rows, columns), BF16),
        in_specs=[VMEM] * 9,
        out_specs=VMEM,
        compiler_params=params(),
        name="pack",
    )(*pieces)
    return out.reshape(8 * rows, columns)


def merge_kernel(lengths_ref, keep_ref, got_ref, out_ref):
    position = lax.axis_index("seq")
    keep = keep_ref[...].astype(F32)
    got = got_ref[...].astype(F32)
    start, _ = long_window(lengths_ref)
    q_cols = 16
    slot = lax.broadcasted_iota(jnp.int32, keep.shape, 0)
    token = (slot // q_cols) * (lax.axis_size("seq") * q_cols) + position * q_cols + slot % q_cols
    inside = jnp.where(token >= start, 1, 0)
    mine = inside == jnp.where(position % 2 == 0, 1, 0)
    half = keep.shape[0]
    out_ref[:half] = jnp.where(mine, keep, got).astype(BF16)
    out_ref[half:] = jnp.where(mine, got, keep).astype(BF16)


def merge(lengths, keep, got):
    return pl.pallas_call(
        merge_kernel,
        out_shape=jax.ShapeDtypeStruct((128, D), BF16),
        in_specs=[SMEM, VMEM, VMEM],
        out_specs=VMEM,
        compiler_params=params(),
        name="merge",
    )(lengths, keep, got)


def shards(
    clip, frame_counts, conv_first, conv_second, patch_weight, qkv_weight, query_gain, key_gain,
    out_weight, window_lengths,
):
    size = lax.axis_size("seq")
    facing = [(i, j) for i in range(1, size - 1, 2) for i, j in ((i, i + 1), (i + 1, i))]
    cores = [(i, i ^ 1) for i in range(size)]
    forward = ring_pairs()
    backward = [(j, i) for i, j in forward]

    def send(array, pairs):
        return lax.ppermute(array, "seq", pairs)

    def tied(*arrays):
        return lax.optimization_barrier(arrays)

    def tied(*arrays):
        return lax.optimization_barrier(arrays)

    def both_ways(ahead, behind):
        return send(ahead, forward), send(behind, backward)

    def tied(*arrays):
        return lax.optimization_barrier(arrays)

    def both_ways(ahead, behind):
        return send(ahead, forward), send(behind, backward)

    sibling_rows = send(clip, cores)
    other_rows = send(clip, facing)
    query_row, key_row = query_gain[None], key_gain[None]
    weight_one = both_ways(out_weight, out_weight)
    folded, query_weight, centered = fold(patch_weight, qkv_weight)
    sibling_rows, other_rows, *weight_one, folded = tied(sibling_rows, other_rows, *weight_one, folded)
    weight_two = both_ways(*weight_one)
    keep, other = convolve(
        frame_counts, window_lengths, clip, sibling_rows, other_rows, conv_first, conv_second, patch_weight
    )
    got = send(other, cores)
    got, wu_a, wu_b = tied(got, *weight_two)
    weight_two = (wu_a, wu_b)
    weight_three = both_ways(*weight_two)
    block = jnp.concatenate([keep, got], axis=0)
    one = both_ways(block, block)
    queries = make_queries(window_lengths, block, centered, query_weight, query_row)
    *one, queries = tied(*one, queries)
    two = both_ways(*one)
    acc_one = step_attention((-1, 1), window_lengths, one, folded, key_row, queries)
    wt_a, wt_b, acc_one = tied(*weight_three, acc_one)
    cut = 640
    weight_four = both_ways(wt_a[:, :cut], wt_b[:, cut:])
    *two, acc_one = tied(*two, acc_one)
    three = both_ways(*two)
    acc_two = step_attention((-2, 2), window_lengths, two, folded, key_row, queries)
    *three, acc_two, wf_a, wf_b = tied(*three, acc_two, *weight_four)
    four = both_ways(three[0][:64], three[1][64:])
    weights = pack([out_weight, *weight_one, *weight_two, wt_a, wt_b, wf_a, wf_b])
    sibling = send(weights, cores)
    acc_three = step_attention((-3, 3), window_lengths, three, folded, key_row, queries)
    *four, acc_three = tied(*four, acc_three)
    acc_four = step_attention((0, 4, 4), window_lengths, [block, *four], folded, key_row, queries)
    keep_rows, send_rows = project_out((acc_one, acc_two, acc_three, acc_four), (weights, sibling))
    return merge(window_lengths, keep_rows, send(send_rows, cores))


def solution(mesh):
    own = mesh.shape["seq"] == HEADS
    return jax.shard_map(
        shards if own else general_shards,
        mesh=mesh,
        in_specs=(
            P("groups", "seq", None, None),
            P("groups"),
            P(),
            P(),
            P(),
            P(),
            P(),
            P(),
            P("seq", None),
            P("groups", None),
        ),
        out_specs=P(("groups", "seq"), None),
        check_vma=False,
    )
```

```python
import functools
import math

import jax
import jax.numpy as jnp
from jax import lax
from jax.experimental import pallas as pl
from jax.experimental.pallas import tpu as pltpu
from jax.sharding import PartitionSpec as P

D = 1152
HEADS = 16


def extended(array, sides, width):
    for axis, dim in sides:
        size, length = (lax.axis_size(axis), array.shape[dim])
        up = [(i, (i + 1) % size) for i in range(size - 1)]
        down = [(j, i) for i, j in up]
        last = lax.slice_in_dim(array, length - width, length, axis=dim)
        first = lax.slice_in_dim(array, 0, width, axis=dim)
        before = lax.ppermute(last, axis, up)
        after = lax.ppermute(first, axis, down)
        array = jnp.concatenate([before, array, after], axis=dim)
    return array


def frame_weights(frame_counts, frames):
    position = jnp.arange(frames, dtype=jnp.int32)
    clip_ends = jnp.cumsum(frame_counts)

    def clip_of(index):
        return jnp.sum((index[:, None] >= clip_ends[None, :]).astype(jnp.int32), axis=1)

    own_clip = clip_of(position)
    columns = []
    for offset in (-1, 0, 1):
        neighbor = position + offset
        inside = (neighbor >= 0) & (neighbor < frames)
        same_clip = clip_of(jnp.clip(neighbor, 0, frames - 1)) == own_clip
        columns.append((inside & same_clip).astype(jnp.float32))
    return jnp.stack(columns, axis=1)


def convolve_rows(activation, kernel, tap_weights):
    empty_frame = jnp.zeros_like(activation[:1])
    shifted = (
        jnp.concatenate([empty_frame, activation[:-1]], 0),
        activation,
        jnp.concatenate([activation[1:], empty_frame], 0),
    )
    summed = None
    for offset in range(3):
        response = lax.conv_general_dilated(
            shifted[offset],
            kernel[offset],
            (1, 1),
            ((0, 0), (1, 1)),
            dimension_numbers=("NHWC", "HWIO", "NHWC"),
            preferred_element_type=jnp.float32,
        )
        tap_term = tap_weights[:, offset][:, None, None, None] * response
        summed = tap_term if offset == 0 else summed + tap_term
    return summed


def rms_scale(part, gain):
    factor = lax.rsqrt(jnp.mean(part * part, axis=-1, keepdims=True) + 1e-06)
    return (part * factor * gain).astype(jnp.bfloat16)


def general_shards(
    clip,
    frame_counts,
    conv_first,
    conv_second,
    patch_weight,
    qkv_weight,
    query_gain,
    key_gain,
    out_weight,
    window_lengths,
):
    frames, tile_rows, tile_cols, channels = clip.shape
    devices = lax.axis_size("seq")
    position = lax.axis_index("seq")
    head_dim = D // HEADS
    score_scale = 1.0 / math.sqrt(head_dim)
    tap_weights = frame_weights(frame_counts, frames)
    source = clip.astype(jnp.float32)
    padded_clip = extended(clip, (("seq", 1),), 2)
    first_in = jax.nn.silu(padded_clip.astype(jnp.float32)).astype(jnp.bfloat16)
    hidden_wide = convolve_rows(first_in, conv_first, tap_weights)
    global_row = position * tile_rows - 1 + jnp.arange(tile_rows + 2, dtype=jnp.int32)
    inside = ((global_row >= 0) & (global_row < tile_rows * devices)).astype(jnp.float32)
    hidden_one = (hidden_wide * inside[None, :, None, None]).astype(jnp.bfloat16)
    padded_second = jax.nn.silu(hidden_one.astype(jnp.float32)).astype(jnp.bfloat16)
    latent = (source + convolve_rows(padded_second, conv_second, tap_weights)).astype(jnp.bfloat16)
    token_rows = tile_rows // 2
    token_cols = tile_cols // 2
    patches = (
        latent.reshape(frames, token_rows, 2, token_cols, 2, channels)
        .transpose(0, 1, 3, 2, 4, 5)
        .reshape(-1, 4 * channels)
    )
    tok_count = patches.shape[0]
    embedded = jnp.dot(patches, patch_weight, preferred_element_type=jnp.float32).astype(
        jnp.bfloat16
    )
    values_f = embedded.astype(jnp.float32)
    row_mean = jnp.mean(values_f, axis=-1, keepdims=True)
    centered = values_f - row_mean
    variance = jnp.mean(centered * centered, axis=-1, keepdims=True)
    normed = (centered / jnp.sqrt(variance + 1e-06)).astype(jnp.bfloat16)
    projected = jnp.dot(normed, qkv_weight, preferred_element_type=jnp.float32).reshape(
        tok_count, 3, HEADS, head_dim
    )
    stacked = jnp.stack(
        [
            rms_scale(projected[:, 0], query_gain),
            rms_scale(projected[:, 1], key_gain),
            projected[:, 2].astype(jnp.bfloat16),
        ],
        axis=1,
    )
    groups = devices // HEADS
    frame_share = frames // groups
    local_share = tok_count // groups
    span_rows = devices * local_share
    outgoing = (
        stacked.reshape(groups, local_share, 3, HEADS, head_dim)
        .transpose(0, 3, 1, 2, 4)
        .reshape(devices, local_share, 3 * head_dim)
    )
    incoming = lax.all_to_all(outgoing, "seq", split_axis=0, concat_axis=0, tiled=True)
    arranged = (
        incoming.reshape(devices, frame_share, token_rows * token_cols, 3, head_dim)
        .transpose(3, 1, 0, 2, 4)
        .reshape(3, span_rows, head_dim)
    )
    my_group = position // HEADS
    lengths = lax.dynamic_index_in_dim(window_lengths, my_group, 0, keepdims=False)
    window_ends = jnp.cumsum(lengths)
    token_index = jnp.arange(span_rows, dtype=jnp.int32)
    segment = jnp.sum((token_index[:, None] >= window_ends[None, :]).astype(jnp.int32), axis=1)
    key_rows = arranged[1]
    value_rows = arranged[2]
    block_rows = min(512, span_rows)
    block_count = span_rows // block_rows

    def attend_block(inputs):
        query_block, segment_block = inputs
        scores = jnp.dot(query_block, key_rows.T, preferred_element_type=jnp.float32) * score_scale
        allowed = segment_block[:, None] == segment[None, :]
        scores = jnp.where(allowed, scores, -1e30)
        row_peak = jnp.max(scores, axis=-1, keepdims=True)
        weights = jnp.exp(scores - row_peak)
        row_mass = jnp.sum(weights, axis=-1, keepdims=True)
        mixed = (
            jnp.dot(weights.astype(jnp.bfloat16), value_rows, preferred_element_type=jnp.float32)
            / row_mass
        )
        return mixed.astype(jnp.bfloat16)

    mixed_rows = lax.map(
        attend_block,
        (
            arranged[0].reshape(block_count, block_rows, head_dim),
            segment.reshape(block_count, block_rows),
        ),
    ).reshape(span_rows, head_dim)
    outgoing_back = (
        mixed_rows.reshape(frame_share, devices, token_rows * token_cols, head_dim)
        .transpose(1, 0, 2, 3)
        .reshape(devices, local_share, head_dim)
    )
    returned = lax.all_to_all(outgoing_back, "seq", split_axis=0, concat_axis=0, tiled=True)
    merged = (
        returned.reshape(groups, HEADS, local_share, head_dim)
        .transpose(0, 2, 1, 3)
        .reshape(tok_count, D)
    )
    projected_out = jnp.dot(
        merged,
        lax.all_gather(out_weight, "seq", axis=0, tiled=True),
        preferred_element_type=jnp.float32,
    )
    return projected_out.astype(jnp.bfloat16)


HD = D // HEADS
SLOT = 80
MASK = 1024.0
F32 = jnp.float32
BF16 = jnp.bfloat16
VMEM = pl.BlockSpec(memory_space=pltpu.VMEM)
SMEM = pl.BlockSpec(memory_space=pltpu.SMEM)
NT = (((1,), (1,)), ((), ()))


def params(mib=40):
    return pltpu.CompilerParams(vmem_limit_bytes=mib << 20)


def silu(v):
    return v / (1.0 + jnp.exp(-v))


def long_window(lengths):
    first, second = lengths[0, 0], lengths[0, 1]
    half = 1024
    start = jnp.where(first == half, 0, jnp.where(second == half, first, first + second))
    bound = jnp.where(first == half, half + second, first)
    return start, bound


ANY = pl.BlockSpec(memory_space=pl.ANY)
TN = (((0,), (1,)), ((), ()))


def pair_weights(weights, o, ch=128):
    blank = jnp.zeros((ch, ch), BF16)
    rows = []
    for four in range(4):
        for j in range(3):
            taps = [weights[o, four - r, j] if 0 <= four - r < 3 else blank for r in range(2)]
            rows.append(jnp.concatenate(taps, axis=1))
    return jnp.concatenate(rows, axis=0)


def fold_kernel(patch_any, qkv_any, folded_ref, query_ref, centered_ref, patch_ref, qkv_ref, sems):
    copies = [
        pltpu.make_async_copy(patch_any, patch_ref, sems.at[0]),
        pltpu.make_async_copy(qkv_any.at[:, pl.ds(D, D)], qkv_ref.at[0], sems.at[1]),
        pltpu.make_async_copy(qkv_any.at[:, pl.ds(2 * D, D)], qkv_ref.at[1], sems.at[2]),
        pltpu.make_async_copy(qkv_any.at[:, pl.ds(0, D)], query_ref, sems.at[3]),
    ]
    for copy in copies:
        copy.start()
    copies[0].wait()
    patch = patch_ref[...].astype(F32)
    centered_ref[...] = (patch - jnp.mean(patch, axis=1, keepdims=True)).astype(BF16)
    for part in range(2):
        copies[part + 1].wait()
        product = lax.dot_general(qkv_ref[part], centered_ref[...], TN, preferred_element_type=F32)
        folded_ref[part * D : (part + 1) * D] = product.astype(BF16)
    copies[3].wait()


def fold(patch_weight, qkv_weight):
    inner = patch_weight.shape[0]
    return pl.pallas_call(
        fold_kernel,
        out_shape=(
            jax.ShapeDtypeStruct((2 * D, inner), BF16),
            jax.ShapeDtypeStruct((D, D), BF16),
            jax.ShapeDtypeStruct((inner, D), BF16),
        ),
        in_specs=[ANY, ANY],
        out_specs=(VMEM, VMEM, VMEM),
        scratch_shapes=[
            pltpu.VMEM((inner, D), BF16),
            pltpu.VMEM((2, D, D), BF16),
            pltpu.SemaphoreType.DMA((4,)),
        ],
        compiler_params=params(),
        name="fold",
        cost_estimate=pl.CostEstimate(flops=2 * inner * D * 2 * D, bytes_accessed=12 << 20, transcendentals=0),
    )(patch_weight, qkv_weight)


def frame_taps(counts_ref, frames):
    def clip_of(frame):
        end = 0
        index = 0
        for c in range(counts_ref.shape[0]):
            end = end + counts_ref[c]
            index = index + jnp.where(frame >= end, 1, 0)
        return index

    own = [clip_of(f) for f in range(frames)]
    joined = [jnp.where(own[f] == own[f + 1], 1.0, 0.0) for f in range(frames - 1)]
    return [0.0] + joined, joined + [0.0]


def conv_kernel(
    counts_any, lengths_any, own_any, patch_any, sibling_ref, other_ref, first_ref, second_ref,
    keep_ref, send_ref, grid_one, grid_two, pixels, own_ref, patch_ref, counts_ref, lengths_ref, sems,
):
    copies = [
        pltpu.make_async_copy(own_any, own_ref, sems.at[0]),
        pltpu.make_async_copy(counts_any, counts_ref, sems.at[1]),
        pltpu.make_async_copy(lengths_any, lengths_ref, sems.at[2]),
        pltpu.make_async_copy(patch_any, patch_ref, sems.at[3]),
    ]
    for copy in copies:
        copy.start()
    frames, _, cols, ch = own_ref.shape
    wide = 12 * ch
    position = lax.axis_index("seq")
    column = lax.broadcasted_iota(jnp.int32, (frames, cols, ch), 1)

    def shifted(row):
        left = jnp.where(column == 0, 0.0, pltpu.roll(row, 1, 1))
        right = jnp.where(column == cols - 1, 0.0, pltpu.roll(row, cols - 1, 1))
        return [part.astype(BF16) for part in (left, row, right)]

    blank = jnp.zeros((cols, wide), BF16)
    for g in range(2):
        grid_one[g, 0] = blank
        grid_one[g, frames + 1] = blank
    grid_two[0] = blank
    grid_two[frames + 1] = blank
    on_first = position % 2 == 0

    def source_row(r):
        if r in (2, 3):
            return own_ref[:, r - 2].astype(F32)
        sibling, other = sibling_ref[:, r % 2].astype(F32), other_ref[:, r % 2].astype(F32)
        return jnp.where(on_first, other, sibling) if r < 2 else jnp.where(on_first, sibling, other)

    for r in (0, 1, 4, 5, 2, 3):
        if r == 2:
            copies[0].wait()
        row = silu(source_row(r))
        parts = shifted(row)
        for g in range(2):
            four = r - 2 * g
            if 0 <= four < 4:
                for j in range(3):
                    grid_one[g, 1 : frames + 1, :, (four * 3 + j) * ch : (four * 3 + j + 1) * ch] = parts[j]

    copies[1].wait()
    copies[2].wait()
    before_tap, after_tap = frame_taps(counts_ref, frames)

    def summed(terms):
        rows = []
        for f in range(frames):
            total = terms[1][f]
            if f > 0:
                total = total + before_tap[f] * terms[0][f]
            if f < frames - 1:
                total = total + after_tap[f] * terms[2][f]
            rows.append(total)
        return jnp.stack(rows)

    for g in range(2):
        terms = []
        for o in range(3):
            left = grid_one[g, o : o + frames].reshape(frames * cols, wide)
            terms.append(
                jnp.dot(left, pair_weights(first_ref, o), preferred_element_type=F32).reshape(frames, cols, 2 * ch)
            )
        hidden = summed(terms)
        for out_row in range(2):
            four = 2 * g + out_row
            row = hidden[:, :, out_row * ch : (out_row + 1) * ch]
            if four == 0:
                row = row * jnp.where(position == 0, 0.0, 1.0)
            if four == 3:
                row = row * jnp.where(position == lax.axis_size("seq") - 1, 0.0, 1.0)
            row = silu(row.astype(BF16).astype(F32))
            parts = shifted(row)
            for j in range(3):
                grid_two[1 : frames + 1, :, (four * 3 + j) * ch : (four * 3 + j + 1) * ch] = parts[j]
    terms = []
    for o in range(3):
        left = grid_two[o : o + frames].reshape(frames * cols, wide)
        terms.append(
            jnp.dot(left, pair_weights(second_ref, o), preferred_element_type=F32).reshape(frames, cols, 2 * ch)
        )
    residual = summed(terms)
    for out_row in range(2):
        block = own_ref[:, out_row].astype(F32) + residual[:, :, out_row * ch : (out_row + 1) * ch]
        pixels[out_row] = block.astype(BF16).astype(F32).reshape(frames * cols, ch)
    tokens = frames * cols // 2
    patches = jnp.concatenate(
        [pixels[a, pl.ds(b, tokens, 2), :] for a in range(2) for b in range(2)], axis=1
    )
    copies[3].wait()
    embedded = jnp.dot(patches.astype(BF16), patch_ref[...], preferred_element_type=F32)
    centered = embedded - jnp.mean(embedded, axis=1, keepdims=True)
    variance = jnp.mean(centered * centered, axis=1, keepdims=True)
    scaled = patches * (1.0 / jnp.sqrt(variance + 1e-06))
    half = tokens // 2
    low, high = scaled[:half], scaled[half:]
    start, _ = long_window(lengths_ref)
    q_cols = cols // 2
    slot = lax.broadcasted_iota(jnp.int32, low.shape, 0)
    token = (slot // q_cols) * (lax.axis_size("seq") * q_cols) + position * q_cols + slot % q_cols
    inside = jnp.where(token >= start, 1, 0)
    mine = inside == jnp.where(position % 2 == 0, 1, 0)
    keep = jnp.where(mine, low, high).astype(BF16)
    send = jnp.where(mine, high, low).astype(BF16)
    keep_ref[...] = keep
    send_ref[...] = send


def convolve(counts, lengths, clip, sibling_rows, other_rows, conv_first, conv_second, patch_weight):
    frames, _, cols, ch = clip.shape
    tokens = frames * cols // 2
    out = jax.ShapeDtypeStruct((tokens // 2, 4 * ch), BF16)
    return pl.pallas_call(
        conv_kernel,
        out_shape=(out, out),
        in_specs=[ANY] * 4 + [VMEM] * 4,
        out_specs=(VMEM, VMEM),
        scratch_shapes=[
            pltpu.VMEM((2, frames + 2, cols, 12 * ch), BF16),
            pltpu.VMEM((frames + 2, cols, 12 * ch), BF16),
            pltpu.VMEM((2, frames * cols, ch), F32),
            pltpu.VMEM(clip.shape, BF16),
            pltpu.VMEM(patch_weight.shape, BF16),
            pltpu.SMEM(counts.shape, jnp.int32),
            pltpu.SMEM(lengths.shape, jnp.int32),
            pltpu.SemaphoreType.DMA((4,)),
        ],
        compiler_params=params(),
        name="convolve",
        cost_estimate=pl.CostEstimate(flops=2 << 30, bytes_accessed=4 << 20, transcendentals=1 << 18),
    )(counts, lengths, clip, patch_weight, sibling_rows, other_rows, conv_first, conv_second)


def chip_at(place):
    chips = lax.axis_size("seq") // 2
    place = lax.rem(place + 2 * chips, chips)
    return jnp.where(place < chips // 2, 2 * place, 2 * (chips - 1 - place) + 1)


def ring_place():
    chips = lax.axis_size("seq") // 2
    chip = lax.axis_index("seq") // 2
    return jnp.where(chip % 2 == 0, chip // 2, chips - 1 - chip // 2)


def ring_pairs():
    size = lax.axis_size("seq")
    chips = size // 2
    order = [2 * i for i in range(chips // 2)] + [2 * i + 1 for i in reversed(range(chips // 2))]
    return [
        (2 * order[i] + core, 2 * order[(i + 1) % chips] + core) for i in range(chips) for core in range(2)
    ]


def window_sides(lengths_ref, chip, count):
    size = lax.axis_size("seq")
    core = lax.axis_index("seq") % 2
    start, bound = long_window(lengths_ref)
    lane = lax.broadcasted_iota(jnp.int32, (8, count), 1)
    half = count // 2
    slot = lane % half
    row = 2 * chip + jnp.where(lane < half, core, 1 - core)
    q_cols = 16
    token = (slot // q_cols) * (size * q_cols) + row * q_cols + slot % q_cols
    inside = jnp.where(token >= start, 1, 0)
    upper = inside != jnp.where(core == 0, 1, 0)
    token = jnp.where(upper, token + 4 * size * q_cols, token)
    return jnp.where(token < bound, 1.0, -1.0)


def normed_heads(part, gain):
    count = part.shape[1]
    heads = part.reshape(-1, HD, count)
    factor = lax.rsqrt(jnp.mean(heads * heads, axis=1, keepdims=True) + 1e-06)
    return heads * factor * gain[None]


def as_column(row):
    size = row.shape[1]
    square = (size, size)
    same = lax.broadcasted_iota(jnp.int32, square, 0) == lax.broadcasted_iota(jnp.int32, square, 1)
    return jnp.sum(jnp.where(same, jnp.broadcast_to(row, square), 0.0), axis=1, keepdims=True)


def attend(tokens, sides, folded, key_gain, queries, acc_ref, keys_ref, values_ref, scores_ref, weights_ref):
    count = tokens.shape[0]
    row = lax.broadcasted_iota(jnp.int32, (8, count), 0)
    key_tail = jnp.where(row == 0, sides, jnp.where(row == 1, 1.0, 0.0))
    value_tail = jnp.where(row == 0, 1.0, 0.0)
    heads_at_once = 4
    for first in range(0, HEADS, heads_at_once):
        rows = slice(first * HD, (first + heads_at_once) * HD)
        part = lax.dot_general(folded[rows], tokens, NT, preferred_element_type=F32)
        keys = normed_heads(part, key_gain)
        for h in range(heads_at_once):
            keys_ref[first + h] = jnp.concatenate([keys[h], key_tail], axis=0).astype(BF16)
    for first in range(0, HEADS, heads_at_once):
        rows = slice(D + first * HD, D + (first + heads_at_once) * HD)
        part = lax.dot_general(folded[rows], tokens, NT, preferred_element_type=F32)
        values = part.reshape(heads_at_once, HD, count)
        for h in range(heads_at_once):
            values_ref[first + h] = jnp.concatenate([values[h], value_tail], axis=0).astype(BF16)
    for h in range(HEADS):
        scores_ref[h] = jnp.dot(queries[h], keys_ref[h], preferred_element_type=F32)
    lane = lax.broadcasted_iota(jnp.int32, (128, 128), 1)
    peaks = jnp.zeros((128, 128), F32)
    for h in range(HEADS):
        scores = scores_ref[h]
        peak = jnp.max(scores, axis=1, keepdims=True)
        weights_ref[h] = jnp.exp2(scores - peak).astype(BF16)
        peaks = jnp.where(lane == h, peak, peaks)
    peaks = peaks.T
    tail_row = lax.broadcasted_iota(jnp.int32, (8, 128), 0)
    for h in range(HEADS):
        mixed = lax.dot_general(values_ref[h], weights_ref[h], NT, preferred_element_type=F32)
        acc_ref[h, :HD] = mixed[:HD]
        acc_ref[h, HD:] = jnp.where(tail_row == 1, peaks[h : h + 1], mixed[HD:])


def attend_scratch(count):
    return [
        pltpu.VMEM((HEADS, SLOT, count), BF16),
        pltpu.VMEM((HEADS, SLOT, count), BF16),
        pltpu.VMEM((HEADS, 128, count), F32),
        pltpu.VMEM((HEADS, 128, count), BF16),
    ]


def query_kernel(lengths_ref, block_ref, centered_ref, query_ref, query_gain_ref, queries_ref):
    normed = jnp.dot(block_ref[...], centered_ref[...], preferred_element_type=F32).astype(BF16)
    part = jnp.dot(normed, query_ref[...], preferred_element_type=F32).T
    count = part.shape[1]
    sides = window_sides(lengths_ref, lax.axis_index("seq") // 2, count)
    queries = normed_heads(part, as_column(query_gain_ref[...] * (math.log2(math.e) / math.sqrt(HD))))
    row = lax.broadcasted_iota(jnp.int32, (8, count), 0)
    tail = jnp.where(row == 0, MASK * sides, jnp.where(row == 1, -MASK, 0.0))
    for h in range(HEADS):
        queries_ref[h] = jnp.concatenate([queries[h], tail], axis=0).T.astype(BF16)


def make_queries(lengths, block, centered, query_weight, query_gain):
    return pl.pallas_call(
        query_kernel,
        out_shape=jax.ShapeDtypeStruct((HEADS, 128, SLOT), BF16),
        in_specs=[SMEM] + [VMEM] * 4,
        out_specs=VMEM,
        compiler_params=params(),
        name="queries",
        cost_estimate=pl.CostEstimate(flops=1 << 30, bytes_accessed=4 << 20, transcendentals=0),
    )(lengths, block, centered, query_weight, query_gain)


def step_kernel(offsets, lengths_ref, *refs):
    blocks = refs[: len(offsets)]
    folded_ref, key_gain_ref, queries_ref, acc_ref, *scratch = refs[len(offsets) :]
    place = ring_place()
    tokens = jnp.concatenate([ref[...] for ref in blocks], axis=0)
    sides = jnp.concatenate(
        [window_sides(lengths_ref, chip_at(place + offset), 128) for offset in dict.fromkeys(offsets)], axis=1
    )
    attend(tokens, sides, folded_ref, as_column(key_gain_ref[...]), queries_ref, acc_ref, *scratch)


ACC = jax.ShapeDtypeStruct((HEADS, SLOT, 128), F32)


def step_attention(offsets, lengths, blocks, folded, key_gain, queries):
    count = sum(block.shape[0] for block in blocks)
    flops = 2 * count * 2 * D * 512 + 4 * HEADS * 128 * 128 * count
    return pl.pallas_call(
        functools.partial(step_kernel, offsets),
        out_shape=ACC,
        in_specs=[SMEM] + [VMEM] * (len(blocks) + 3),
        out_specs=VMEM,
        scratch_shapes=attend_scratch(count),
        compiler_params=params(),
        name="step_attention",
        cost_estimate=pl.CostEstimate(flops=2 * flops, bytes_accessed=5 << 20, transcendentals=HEADS * 128 * count),
    )(lengths, *blocks, folded, key_gain, queries)


RING = (0, -1, 1, -2, 2, -3, 3, 4)


def out_kernel(parts, *refs):
    acc_refs = refs[:parts]
    weight_refs = refs[parts:-3]
    keep_ref, send_ref, mixed_ref = refs[-3:]
    for h in range(HEADS):
        peaks = [acc[h, HD + 1 : HD + 2] for acc in acc_refs]
        peak = functools.reduce(jnp.maximum, peaks)
        total = None
        for acc, own in zip(acc_refs, peaks):
            term = acc[h] * jnp.exp2(own - peak)
            total = term if total is None else total + term
        mixed_ref[h] = total[:HD] / total[HD : HD + 1]
    place = ring_place()
    core = lax.axis_index("seq") % 2
    lefts = []
    for side in range(2):
        heads = [2 * chip_at(place + offset) + jnp.where(core == side, 0, 1) for offset in RING]
        lefts.append(jnp.concatenate([mixed_ref[head] for head in heads], axis=0).T.astype(BF16))
    half = keep_ref.shape[0]
    for first in range(0, D, 256):
        columns = slice(first, min(first + 256, D))
        result = jnp.dot(lefts[0], weight_refs[0][:, columns], preferred_element_type=F32)
        result = result + jnp.dot(lefts[1], weight_refs[1][:, columns], preferred_element_type=F32)
        result = result.astype(BF16)
        keep_ref[:, columns] = result[:half]
        send_ref[:, columns] = result[half:]


def project_out(accs, weights):
    out = jax.ShapeDtypeStruct((64, D), BF16)
    return pl.pallas_call(
        functools.partial(out_kernel, len(accs)),
        out_shape=(out, out),
        in_specs=[VMEM] * (len(accs) + len(weights)),
        out_specs=(VMEM, VMEM),
        scratch_shapes=[pltpu.VMEM((HEADS, HD, 128), F32)],
        compiler_params=params(),
        name="project_out",
        cost_estimate=pl.CostEstimate(flops=2 * 128 * 1280 * D, bytes_accessed=4 << 20, transcendentals=0),
    )(*accs, *weights)


def pack_kernel(*refs):
    out_ref = refs[-1]
    for i in range(7):
        out_ref[i] = refs[i][...]
    cut = refs[7].shape[1]
    out_ref[7, :, :cut] = refs[7][...]
    out_ref[7, :, cut:] = refs[8][...]


def pack(pieces):
    rows, columns = pieces[0].shape
    out = pl.pallas_call(
        pack_kernel,
        out_shape=jax.ShapeDtypeStruct((8, rows, columns), BF16),
        in_specs=[VMEM] * 9,
        out_specs=VMEM,
        compiler_params=params(),
        name="pack",
    )(*pieces)
    return out.reshape(8 * rows, columns)


def merge_kernel(lengths_ref, keep_ref, got_ref, out_ref):
    position = lax.axis_index("seq")
    keep = keep_ref[...].astype(F32)
    got = got_ref[...].astype(F32)
    start, _ = long_window(lengths_ref)
    q_cols = 16
    slot = lax.broadcasted_iota(jnp.int32, keep.shape, 0)
    token = (slot // q_cols) * (lax.axis_size("seq") * q_cols) + position * q_cols + slot % q_cols
    inside = jnp.where(token >= start, 1, 0)
    mine = inside == jnp.where(position % 2 == 0, 1, 0)
    half = keep.shape[0]
    out_ref[:half] = jnp.where(mine, keep, got).astype(BF16)
    out_ref[half:] = jnp.where(mine, got, keep).astype(BF16)


def merge(lengths, keep, got):
    return pl.pallas_call(
        merge_kernel,
        out_shape=jax.ShapeDtypeStruct((128, D), BF16),
        in_specs=[SMEM, VMEM, VMEM],
        out_specs=VMEM,
        compiler_params=params(),
        name="merge",
    )(lengths, keep, got)


def shards(
    clip, frame_counts, conv_first, conv_second, patch_weight, qkv_weight, query_gain, key_gain,
    out_weight, window_lengths,
):
    size = lax.axis_size("seq")
    facing = [(i, j) for i in range(1, size - 1, 2) for i, j in ((i, i + 1), (i + 1, i))]
    cores = [(i, i ^ 1) for i in range(size)]
    forward = ring_pairs()
    backward = [(j, i) for i, j in forward]

    def send(array, pairs):
        return lax.ppermute(array, "seq", pairs)

    def tied(*arrays):
        return lax.optimization_barrier(arrays)

    def tied(*arrays):
        return lax.optimization_barrier(arrays)

    def both_ways(ahead, behind):
        return send(ahead, forward), send(behind, backward)

    def tied(*arrays):
        return lax.optimization_barrier(arrays)

    def both_ways(ahead, behind):
        return send(ahead, forward), send(behind, backward)

    sibling_rows = send(clip, cores)
    other_rows = send(clip, facing)
    query_row, key_row = query_gain[None], key_gain[None]
    weight_one = both_ways(out_weight, out_weight)
    folded, query_weight, centered = fold(patch_weight, qkv_weight)
    sibling_rows, other_rows, *weight_one, folded = tied(sibling_rows, other_rows, *weight_one, folded)
    weight_two = both_ways(*weight_one)
    keep, other = convolve(
        frame_counts, window_lengths, clip, sibling_rows, other_rows, conv_first, conv_second, patch_weight
    )
    got = send(other, cores)
    got, wu_a, wu_b = tied(got, *weight_two)
    weight_two = (wu_a, wu_b)
    weight_three = both_ways(*weight_two)
    block = jnp.concatenate([keep, got], axis=0)
    one = both_ways(block, block)
    wt_a, wt_b, query_block = tied(*weight_three, block)
    cut = 640
    weight_four = both_ways(wt_a[:, :cut], wt_b[:, cut:])
    queries = make_queries(window_lengths, query_block, centered, query_weight, query_row)
    *one, queries = tied(*one, queries)
    two = both_ways(*one)
    acc_one = step_attention((-1, 1), window_lengths, one, folded, key_row, queries)
    wf_a, wf_b, *two, acc_one = tied(*weight_four, *two, acc_one)
    three = both_ways(*two)
    weights = pack([out_weight, *weight_one, *weight_two, wt_a, wt_b, wf_a, wf_b])
    acc_two = step_attention((-2, 2), window_lengths, two, folded, key_row, queries)
    *three, acc_two, weights = tied(*three, acc_two, weights)
    four = both_ways(three[0][:64], three[1][64:])
    sibling = send(weights, cores)
    acc_three = step_attention((-3, 3), window_lengths, three, folded, key_row, queries)
    *four, acc_three = tied(*four, acc_three)
    acc_four = step_attention((0, 4, 4), window_lengths, [block, *four], folded, key_row, queries)
    keep_rows, send_rows = project_out((acc_one, acc_two, acc_three, acc_four), (weights, sibling))
    return merge(window_lengths, keep_rows, send(send_rows, cores))


def solution(mesh):
    own = mesh.shape["seq"] == HEADS
    return jax.shard_map(
        shards if own else general_shards,
        mesh=mesh,
        in_specs=(
            P("groups", "seq", None, None),
            P("groups"),
            P(),
            P(),
            P(),
            P(),
            P(),
            P(),
            P("seq", None),
            P("groups", None),
        ),
        out_specs=P(("groups", "seq"), None),
        check_vma=False,
    )
```

```python
import functools
import math

import jax
import jax.numpy as jnp
from jax import lax
from jax.experimental import pallas as pl
from jax.experimental.pallas import tpu as pltpu
from jax.sharding import PartitionSpec as P

D = 1152
HEADS = 16


def extended(array, sides, width):
    for axis, dim in sides:
        size, length = (lax.axis_size(axis), array.shape[dim])
        up = [(i, (i + 1) % size) for i in range(size - 1)]
        down = [(j, i) for i, j in up]
        last = lax.slice_in_dim(array, length - width, length, axis=dim)
        first = lax.slice_in_dim(array, 0, width, axis=dim)
        before = lax.ppermute(last, axis, up)
        after = lax.ppermute(first, axis, down)
        array = jnp.concatenate([before, array, after], axis=dim)
    return array


def frame_weights(frame_counts, frames):
    position = jnp.arange(frames, dtype=jnp.int32)
    clip_ends = jnp.cumsum(frame_counts)

    def clip_of(index):
        return jnp.sum((index[:, None] >= clip_ends[None, :]).astype(jnp.int32), axis=1)

    own_clip = clip_of(position)
    columns = []
    for offset in (-1, 0, 1):
        neighbor = position + offset
        inside = (neighbor >= 0) & (neighbor < frames)
        same_clip = clip_of(jnp.clip(neighbor, 0, frames - 1)) == own_clip
        columns.append((inside & same_clip).astype(jnp.float32))
    return jnp.stack(columns, axis=1)


def convolve_rows(activation, kernel, tap_weights):
    empty_frame = jnp.zeros_like(activation[:1])
    shifted = (
        jnp.concatenate([empty_frame, activation[:-1]], 0),
        activation,
        jnp.concatenate([activation[1:], empty_frame], 0),
    )
    summed = None
    for offset in range(3):
        response = lax.conv_general_dilated(
            shifted[offset],
            kernel[offset],
            (1, 1),
            ((0, 0), (1, 1)),
            dimension_numbers=("NHWC", "HWIO", "NHWC"),
            preferred_element_type=jnp.float32,
        )
        tap_term = tap_weights[:, offset][:, None, None, None] * response
        summed = tap_term if offset == 0 else summed + tap_term
    return summed


def rms_scale(part, gain):
    factor = lax.rsqrt(jnp.mean(part * part, axis=-1, keepdims=True) + 1e-06)
    return (part * factor * gain).astype(jnp.bfloat16)


def general_shards(
    clip,
    frame_counts,
    conv_first,
    conv_second,
    patch_weight,
    qkv_weight,
    query_gain,
    key_gain,
    out_weight,
    window_lengths,
):
    frames, tile_rows, tile_cols, channels = clip.shape
    devices = lax.axis_size("seq")
    position = lax.axis_index("seq")
    head_dim = D // HEADS
    score_scale = 1.0 / math.sqrt(head_dim)
    tap_weights = frame_weights(frame_counts, frames)
    source = clip.astype(jnp.float32)
    padded_clip = extended(clip, (("seq", 1),), 2)
    first_in = jax.nn.silu(padded_clip.astype(jnp.float32)).astype(jnp.bfloat16)
    hidden_wide = convolve_rows(first_in, conv_first, tap_weights)
    global_row = position * tile_rows - 1 + jnp.arange(tile_rows + 2, dtype=jnp.int32)
    inside = ((global_row >= 0) & (global_row < tile_rows * devices)).astype(jnp.float32)
    hidden_one = (hidden_wide * inside[None, :, None, None]).astype(jnp.bfloat16)
    padded_second = jax.nn.silu(hidden_one.astype(jnp.float32)).astype(jnp.bfloat16)
    latent = (source + convolve_rows(padded_second, conv_second, tap_weights)).astype(jnp.bfloat16)
    token_rows = tile_rows // 2
    token_cols = tile_cols // 2
    patches = (
        latent.reshape(frames, token_rows, 2, token_cols, 2, channels)
        .transpose(0, 1, 3, 2, 4, 5)
        .reshape(-1, 4 * channels)
    )
    tok_count = patches.shape[0]
    embedded = jnp.dot(patches, patch_weight, preferred_element_type=jnp.float32).astype(
        jnp.bfloat16
    )
    values_f = embedded.astype(jnp.float32)
    row_mean = jnp.mean(values_f, axis=-1, keepdims=True)
    centered = values_f - row_mean
    variance = jnp.mean(centered * centered, axis=-1, keepdims=True)
    normed = (centered / jnp.sqrt(variance + 1e-06)).astype(jnp.bfloat16)
    projected = jnp.dot(normed, qkv_weight, preferred_element_type=jnp.float32).reshape(
        tok_count, 3, HEADS, head_dim
    )
    stacked = jnp.stack(
        [
            rms_scale(projected[:, 0], query_gain),
            rms_scale(projected[:, 1], key_gain),
            projected[:, 2].astype(jnp.bfloat16),
        ],
        axis=1,
    )
    groups = devices // HEADS
    frame_share = frames // groups
    local_share = tok_count // groups
    span_rows = devices * local_share
    outgoing = (
        stacked.reshape(groups, local_share, 3, HEADS, head_dim)
        .transpose(0, 3, 1, 2, 4)
        .reshape(devices, local_share, 3 * head_dim)
    )
    incoming = lax.all_to_all(outgoing, "seq", split_axis=0, concat_axis=0, tiled=True)
    arranged = (
        incoming.reshape(devices, frame_share, token_rows * token_cols, 3, head_dim)
        .transpose(3, 1, 0, 2, 4)
        .reshape(3, span_rows, head_dim)
    )
    my_group = position // HEADS
    lengths = lax.dynamic_index_in_dim(window_lengths, my_group, 0, keepdims=False)
    window_ends = jnp.cumsum(lengths)
    token_index = jnp.arange(span_rows, dtype=jnp.int32)
    segment = jnp.sum((token_index[:, None] >= window_ends[None, :]).astype(jnp.int32), axis=1)
    key_rows = arranged[1]
    value_rows = arranged[2]
    block_rows = min(512, span_rows)
    block_count = span_rows // block_rows

    def attend_block(inputs):
        query_block, segment_block = inputs
        scores = jnp.dot(query_block, key_rows.T, preferred_element_type=jnp.float32) * score_scale
        allowed = segment_block[:, None] == segment[None, :]
        scores = jnp.where(allowed, scores, -1e30)
        row_peak = jnp.max(scores, axis=-1, keepdims=True)
        weights = jnp.exp(scores - row_peak)
        row_mass = jnp.sum(weights, axis=-1, keepdims=True)
        mixed = (
            jnp.dot(weights.astype(jnp.bfloat16), value_rows, preferred_element_type=jnp.float32)
            / row_mass
        )
        return mixed.astype(jnp.bfloat16)

    mixed_rows = lax.map(
        attend_block,
        (
            arranged[0].reshape(block_count, block_rows, head_dim),
            segment.reshape(block_count, block_rows),
        ),
    ).reshape(span_rows, head_dim)
    outgoing_back = (
        mixed_rows.reshape(frame_share, devices, token_rows * token_cols, head_dim)
        .transpose(1, 0, 2, 3)
        .reshape(devices, local_share, head_dim)
    )
    returned = lax.all_to_all(outgoing_back, "seq", split_axis=0, concat_axis=0, tiled=True)
    merged = (
        returned.reshape(groups, HEADS, local_share, head_dim)
        .transpose(0, 2, 1, 3)
        .reshape(tok_count, D)
    )
    projected_out = jnp.dot(
        merged,
        lax.all_gather(out_weight, "seq", axis=0, tiled=True),
        preferred_element_type=jnp.float32,
    )
    return projected_out.astype(jnp.bfloat16)


HD = D // HEADS
SLOT = 80
MASK = 1024.0
F32 = jnp.float32
BF16 = jnp.bfloat16
VMEM = pl.BlockSpec(memory_space=pltpu.VMEM)
SMEM = pl.BlockSpec(memory_space=pltpu.SMEM)
NT = (((1,), (1,)), ((), ()))


def params(mib=40):
    return pltpu.CompilerParams(vmem_limit_bytes=mib << 20)


def silu(v):
    return 0.5 * v * (1.0 + jnp.tanh(0.5 * v))


def long_window(lengths):
    first, second = lengths[0, 0], lengths[0, 1]
    half = 1024
    start = jnp.where(first == half, 0, jnp.where(second == half, first, first + second))
    bound = jnp.where(first == half, half + second, first)
    return start, bound


ANY = pl.BlockSpec(memory_space=pl.ANY)
TN = (((0,), (1,)), ((), ()))


def pair_weights(weights, o, ch=128):
    blank = jnp.zeros((ch, ch), BF16)
    rows = []
    for four in range(4):
        for j in range(3):
            taps = [weights[o, four - r, j] if 0 <= four - r < 3 else blank for r in range(2)]
            rows.append(jnp.concatenate(taps, axis=1))
    return jnp.concatenate(rows, axis=0)


def fold_kernel(patch_any, qkv_any, folded_ref, query_ref, centered_ref, patch_ref, qkv_ref, sems):
    copies = [
        pltpu.make_async_copy(patch_any, patch_ref, sems.at[0]),
        pltpu.make_async_copy(qkv_any.at[:, pl.ds(D, D)], qkv_ref.at[0], sems.at[1]),
        pltpu.make_async_copy(qkv_any.at[:, pl.ds(2 * D, D)], qkv_ref.at[1], sems.at[2]),
        pltpu.make_async_copy(qkv_any.at[:, pl.ds(0, D)], query_ref, sems.at[3]),
    ]
    for copy in copies:
        copy.start()
    copies[0].wait()
    patch = patch_ref[...].astype(F32)
    centered_ref[...] = (patch - jnp.mean(patch, axis=1, keepdims=True)).astype(BF16)
    for part in range(2):
        copies[part + 1].wait()
        product = lax.dot_general(qkv_ref[part], centered_ref[...], TN, preferred_element_type=F32)
        folded_ref[part * D : (part + 1) * D] = product.astype(BF16)
    copies[3].wait()


def fold(patch_weight, qkv_weight):
    inner = patch_weight.shape[0]
    return pl.pallas_call(
        fold_kernel,
        out_shape=(
            jax.ShapeDtypeStruct((2 * D, inner), BF16),
            jax.ShapeDtypeStruct((D, D), BF16),
            jax.ShapeDtypeStruct((inner, D), BF16),
        ),
        in_specs=[ANY, ANY],
        out_specs=(VMEM, VMEM, VMEM),
        scratch_shapes=[
            pltpu.VMEM((inner, D), BF16),
            pltpu.VMEM((2, D, D), BF16),
            pltpu.SemaphoreType.DMA((4,)),
        ],
        compiler_params=params(),
        name="fold",
        cost_estimate=pl.CostEstimate(flops=2 * inner * D * 2 * D, bytes_accessed=12 << 20, transcendentals=0),
    )(patch_weight, qkv_weight)


def frame_taps(counts_ref, frames):
    def clip_of(frame):
        end = 0
        index = 0
        for c in range(counts_ref.shape[0]):
            end = end + counts_ref[c]
            index = index + jnp.where(frame >= end, 1, 0)
        return index

    own = [clip_of(f) for f in range(frames)]
    joined = [jnp.where(own[f] == own[f + 1], 1.0, 0.0) for f in range(frames - 1)]
    return [0.0] + joined, joined + [0.0]


def conv_kernel(
    counts_any, lengths_any, own_any, patch_any, sibling_ref, other_ref, first_ref, second_ref,
    keep_ref, send_ref, grid_one, grid_two, pixels, own_ref, patch_ref, counts_ref, lengths_ref, sems,
):
    copies = [
        pltpu.make_async_copy(own_any, own_ref, sems.at[0]),
        pltpu.make_async_copy(counts_any, counts_ref, sems.at[1]),
        pltpu.make_async_copy(lengths_any, lengths_ref, sems.at[2]),
        pltpu.make_async_copy(patch_any, patch_ref, sems.at[3]),
    ]
    for copy in copies:
        copy.start()
    frames, _, cols, ch = own_ref.shape
    wide = 12 * ch
    position = lax.axis_index("seq")
    column = lax.broadcasted_iota(jnp.int32, (frames, cols, ch), 1)

    def shifted(row):
        left = jnp.where(column == 0, 0.0, pltpu.roll(row, 1, 1))
        right = jnp.where(column == cols - 1, 0.0, pltpu.roll(row, cols - 1, 1))
        return [part.astype(BF16) for part in (left, row, right)]

    blank = jnp.zeros((cols, wide), BF16)
    for g in range(2):
        grid_one[g, 0] = blank
        grid_one[g, frames + 1] = blank
    grid_two[0] = blank
    grid_two[frames + 1] = blank
    on_first = position % 2 == 0

    def source_row(r):
        if r in (2, 3):
            return own_ref[:, r - 2].astype(F32)
        sibling, other = sibling_ref[:, r % 2].astype(F32), other_ref[:, r % 2].astype(F32)
        return jnp.where(on_first, other, sibling) if r < 2 else jnp.where(on_first, sibling, other)

    for r in (0, 1, 4, 5, 2, 3):
        if r == 2:
            copies[0].wait()
        row = silu(source_row(r))
        parts = shifted(row)
        for g in range(2):
            four = r - 2 * g
            if 0 <= four < 4:
                for j in range(3):
                    grid_one[g, 1 : frames + 1, :, (four * 3 + j) * ch : (four * 3 + j + 1) * ch] = parts[j]

    copies[1].wait()
    copies[2].wait()
    before_tap, after_tap = frame_taps(counts_ref, frames)

    def summed(terms):
        rows = []
        for f in range(frames):
            total = terms[1][f]
            if f > 0:
                total = total + before_tap[f] * terms[0][f]
            if f < frames - 1:
                total = total + after_tap[f] * terms[2][f]
            rows.append(total)
        return jnp.stack(rows)

    for g in range(2):
        terms = []
        for o in range(3):
            left = grid_one[g, o : o + frames].reshape(frames * cols, wide)
            terms.append(
                jnp.dot(left, pair_weights(first_ref, o), preferred_element_type=F32).reshape(frames, cols, 2 * ch)
            )
        hidden = summed(terms)
        for out_row in range(2):
            four = 2 * g + out_row
            row = hidden[:, :, out_row * ch : (out_row + 1) * ch]
            if four == 0:
                row = row * jnp.where(position == 0, 0.0, 1.0)
            if four == 3:
                row = row * jnp.where(position == lax.axis_size("seq") - 1, 0.0, 1.0)
            row = silu(row.astype(BF16).astype(F32))
            parts = shifted(row)
            for j in range(3):
                grid_two[1 : frames + 1, :, (four * 3 + j) * ch : (four * 3 + j + 1) * ch] = parts[j]
    terms = []
    for o in range(3):
        left = grid_two[o : o + frames].reshape(frames * cols, wide)
        terms.append(
            jnp.dot(left, pair_weights(second_ref, o), preferred_element_type=F32).reshape(frames, cols, 2 * ch)
        )
    residual = summed(terms)
    for out_row in range(2):
        block = own_ref[:, out_row].astype(F32) + residual[:, :, out_row * ch : (out_row + 1) * ch]
        pixels[out_row] = block.astype(BF16).astype(F32).reshape(frames * cols, ch)
    tokens = frames * cols // 2
    patches = jnp.concatenate(
        [pixels[a, pl.ds(b, tokens, 2), :] for a in range(2) for b in range(2)], axis=1
    )
    copies[3].wait()
    embedded = jnp.dot(patches.astype(BF16), patch_ref[...], preferred_element_type=F32)
    centered = embedded - jnp.mean(embedded, axis=1, keepdims=True)
    variance = jnp.mean(centered * centered, axis=1, keepdims=True)
    scaled = patches * (1.0 / jnp.sqrt(variance + 1e-06))
    half = tokens // 2
    low, high = scaled[:half], scaled[half:]
    start, _ = long_window(lengths_ref)
    q_cols = cols // 2
    slot = lax.broadcasted_iota(jnp.int32, low.shape, 0)
    token = (slot // q_cols) * (lax.axis_size("seq") * q_cols) + position * q_cols + slot % q_cols
    inside = jnp.where(token >= start, 1, 0)
    mine = inside == jnp.where(position % 2 == 0, 1, 0)
    keep = jnp.where(mine, low, high).astype(BF16)
    send = jnp.where(mine, high, low).astype(BF16)
    keep_ref[...] = keep
    send_ref[...] = send


def convolve(counts, lengths, clip, sibling_rows, other_rows, conv_first, conv_second, patch_weight):
    frames, _, cols, ch = clip.shape
    tokens = frames * cols // 2
    out = jax.ShapeDtypeStruct((tokens // 2, 4 * ch), BF16)
    return pl.pallas_call(
        conv_kernel,
        out_shape=(out, out),
        in_specs=[ANY] * 4 + [VMEM] * 4,
        out_specs=(VMEM, VMEM),
        scratch_shapes=[
            pltpu.VMEM((2, frames + 2, cols, 12 * ch), BF16),
            pltpu.VMEM((frames + 2, cols, 12 * ch), BF16),
            pltpu.VMEM((2, frames * cols, ch), F32),
            pltpu.VMEM(clip.shape, BF16),
            pltpu.VMEM(patch_weight.shape, BF16),
            pltpu.SMEM(counts.shape, jnp.int32),
            pltpu.SMEM(lengths.shape, jnp.int32),
            pltpu.SemaphoreType.DMA((4,)),
        ],
        compiler_params=params(),
        name="convolve",
        cost_estimate=pl.CostEstimate(flops=2 << 30, bytes_accessed=4 << 20, transcendentals=1 << 18),
    )(counts, lengths, clip, patch_weight, sibling_rows, other_rows, conv_first, conv_second)


def chip_at(place):
    chips = lax.axis_size("seq") // 2
    place = lax.rem(place + 2 * chips, chips)
    return jnp.where(place < chips // 2, 2 * place, 2 * (chips - 1 - place) + 1)


def ring_place():
    chips = lax.axis_size("seq") // 2
    chip = lax.axis_index("seq") // 2
    return jnp.where(chip % 2 == 0, chip // 2, chips - 1 - chip // 2)


def ring_pairs():
    size = lax.axis_size("seq")
    chips = size // 2
    order = [2 * i for i in range(chips // 2)] + [2 * i + 1 for i in reversed(range(chips // 2))]
    return [
        (2 * order[i] + core, 2 * order[(i + 1) % chips] + core) for i in range(chips) for core in range(2)
    ]


def window_sides(lengths_ref, chip, count):
    size = lax.axis_size("seq")
    core = lax.axis_index("seq") % 2
    start, bound = long_window(lengths_ref)
    lane = lax.broadcasted_iota(jnp.int32, (8, count), 1)
    half = count // 2
    slot = lane % half
    row = 2 * chip + jnp.where(lane < half, core, 1 - core)
    q_cols = 16
    token = (slot // q_cols) * (size * q_cols) + row * q_cols + slot % q_cols
    inside = jnp.where(token >= start, 1, 0)
    upper = inside != jnp.where(core == 0, 1, 0)
    token = jnp.where(upper, token + 4 * size * q_cols, token)
    return jnp.where(token < bound, 1.0, -1.0)


def normed_heads(part, gain):
    count = part.shape[1]
    heads = part.reshape(-1, HD, count)
    factor = lax.rsqrt(jnp.mean(heads * heads, axis=1, keepdims=True) + 1e-06)
    return heads * factor * gain[None]


def as_column(row):
    size = row.shape[1]
    square = (size, size)
    same = lax.broadcasted_iota(jnp.int32, square, 0) == lax.broadcasted_iota(jnp.int32, square, 1)
    return jnp.sum(jnp.where(same, jnp.broadcast_to(row, square), 0.0), axis=1, keepdims=True)


def attend(tokens, sides, folded, key_gain, queries, acc_ref, keys_ref, values_ref, scores_ref, weights_ref):
    count = tokens.shape[0]
    row = lax.broadcasted_iota(jnp.int32, (8, count), 0)
    key_tail = jnp.where(row == 0, sides, jnp.where(row == 1, 1.0, 0.0))
    value_tail = jnp.where(row == 0, 1.0, 0.0)
    heads_at_once = 4
    for first in range(0, HEADS, heads_at_once):
        rows = slice(first * HD, (first + heads_at_once) * HD)
        part = lax.dot_general(folded[rows], tokens, NT, preferred_element_type=F32)
        keys = normed_heads(part, key_gain)
        for h in range(heads_at_once):
            keys_ref[first + h] = jnp.concatenate([keys[h], key_tail], axis=0).astype(BF16)
    for first in range(0, HEADS, heads_at_once):
        rows = slice(D + first * HD, D + (first + heads_at_once) * HD)
        part = lax.dot_general(folded[rows], tokens, NT, preferred_element_type=F32)
        values = part.reshape(heads_at_once, HD, count)
        for h in range(heads_at_once):
            values_ref[first + h] = jnp.concatenate([values[h], value_tail], axis=0).astype(BF16)
    for h in range(HEADS):
        scores_ref[h] = jnp.dot(queries[h], keys_ref[h], preferred_element_type=F32)
    lane = lax.broadcasted_iota(jnp.int32, (128, 128), 1)
    peaks = jnp.zeros((128, 128), F32)
    for h in range(HEADS):
        scores = scores_ref[h]
        peak = jnp.max(scores, axis=1, keepdims=True)
        weights_ref[h] = jnp.exp2(scores - peak).astype(BF16)
        peaks = jnp.where(lane == h, peak, peaks)
    peaks = peaks.T
    tail_row = lax.broadcasted_iota(jnp.int32, (8, 128), 0)
    for h in range(HEADS):
        mixed = lax.dot_general(values_ref[h], weights_ref[h], NT, preferred_element_type=F32)
        acc_ref[h, :HD] = mixed[:HD]
        acc_ref[h, HD:] = jnp.where(tail_row == 1, peaks[h : h + 1], mixed[HD:])


def attend_scratch(count):
    return [
        pltpu.VMEM((HEADS, SLOT, count), BF16),
        pltpu.VMEM((HEADS, SLOT, count), BF16),
        pltpu.VMEM((HEADS, 128, count), F32),
        pltpu.VMEM((HEADS, 128, count), BF16),
    ]


def query_kernel(lengths_ref, block_ref, centered_ref, query_ref, query_gain_ref, queries_ref):
    normed = jnp.dot(block_ref[...], centered_ref[...], preferred_element_type=F32).astype(BF16)
    part = jnp.dot(normed, query_ref[...], preferred_element_type=F32).T
    count = part.shape[1]
    sides = window_sides(lengths_ref, lax.axis_index("seq") // 2, count)
    queries = normed_heads(part, as_column(query_gain_ref[...] * (math.log2(math.e) / math.sqrt(HD))))
    row = lax.broadcasted_iota(jnp.int32, (8, count), 0)
    tail = jnp.where(row == 0, MASK * sides, jnp.where(row == 1, -MASK, 0.0))
    for h in range(HEADS):
        queries_ref[h] = jnp.concatenate([queries[h], tail], axis=0).T.astype(BF16)


def make_queries(lengths, block, centered, query_weight, query_gain):
    return pl.pallas_call(
        query_kernel,
        out_shape=jax.ShapeDtypeStruct((HEADS, 128, SLOT), BF16),
        in_specs=[SMEM] + [VMEM] * 4,
        out_specs=VMEM,
        compiler_params=params(),
        name="queries",
        cost_estimate=pl.CostEstimate(flops=1 << 30, bytes_accessed=4 << 20, transcendentals=0),
    )(lengths, block, centered, query_weight, query_gain)


def step_kernel(offsets, lengths_ref, *refs):
    blocks = refs[: len(offsets)]
    folded_ref, key_gain_ref, queries_ref, acc_ref, *scratch = refs[len(offsets) :]
    place = ring_place()
    tokens = jnp.concatenate([ref[...] for ref in blocks], axis=0)
    sides = jnp.concatenate(
        [window_sides(lengths_ref, chip_at(place + offset), 128) for offset in dict.fromkeys(offsets)], axis=1
    )
    attend(tokens, sides, folded_ref, as_column(key_gain_ref[...]), queries_ref, acc_ref, *scratch)


ACC = jax.ShapeDtypeStruct((HEADS, SLOT, 128), F32)


def step_attention(offsets, lengths, blocks, folded, key_gain, queries):
    count = sum(block.shape[0] for block in blocks)
    flops = 2 * count * 2 * D * 512 + 4 * HEADS * 128 * 128 * count
    return pl.pallas_call(
        functools.partial(step_kernel, offsets),
        out_shape=ACC,
        in_specs=[SMEM] + [VMEM] * (len(blocks) + 3),
        out_specs=VMEM,
        scratch_shapes=attend_scratch(count),
        compiler_params=params(),
        name="step_attention",
        cost_estimate=pl.CostEstimate(flops=2 * flops, bytes_accessed=5 << 20, transcendentals=HEADS * 128 * count),
    )(lengths, *blocks, folded, key_gain, queries)


RING = (0, -1, 1, -2, 2, -3, 3, 4)


def out_kernel(parts, *refs):
    acc_refs = refs[:parts]
    weight_refs = refs[parts:-3]
    keep_ref, send_ref, mixed_ref = refs[-3:]
    for h in range(HEADS):
        peaks = [acc[h, HD + 1 : HD + 2] for acc in acc_refs]
        peak = functools.reduce(jnp.maximum, peaks)
        total = None
        for acc, own in zip(acc_refs, peaks):
            term = acc[h] * jnp.exp2(own - peak)
            total = term if total is None else total + term
        mixed_ref[h] = total[:HD] / total[HD : HD + 1]
    place = ring_place()
    core = lax.axis_index("seq") % 2
    lefts = []
    for side in range(2):
        heads = [2 * chip_at(place + offset) + jnp.where(core == side, 0, 1) for offset in RING]
        lefts.append(jnp.concatenate([mixed_ref[head] for head in heads], axis=0).T.astype(BF16))
    half = keep_ref.shape[0]
    for first in range(0, D, 256):
        columns = slice(first, min(first + 256, D))
        result = jnp.dot(lefts[0], weight_refs[0][:, columns], preferred_element_type=F32)
        result = result + jnp.dot(lefts[1], weight_refs[1][:, columns], preferred_element_type=F32)
        result = result.astype(BF16)
        keep_ref[:, columns] = result[:half]
        send_ref[:, columns] = result[half:]


def project_out(accs, weights):
    out = jax.ShapeDtypeStruct((64, D), BF16)
    return pl.pallas_call(
        functools.partial(out_kernel, len(accs)),
        out_shape=(out, out),
        in_specs=[VMEM] * (len(accs) + len(weights)),
        out_specs=(VMEM, VMEM),
        scratch_shapes=[pltpu.VMEM((HEADS, HD, 128), F32)],
        compiler_params=params(),
        name="project_out",
        cost_estimate=pl.CostEstimate(flops=2 * 128 * 1280 * D, bytes_accessed=4 << 20, transcendentals=0),
    )(*accs, *weights)


def pack_kernel(*refs):
    out_ref = refs[-1]
    for i in range(7):
        out_ref[i] = refs[i][...]
    cut = refs[7].shape[1]
    out_ref[7, :, :cut] = refs[7][...]
    out_ref[7, :, cut:] = refs[8][...]


def pack(pieces):
    rows, columns = pieces[0].shape
    out = pl.pallas_call(
        pack_kernel,
        out_shape=jax.ShapeDtypeStruct((8, rows, columns), BF16),
        in_specs=[VMEM] * 9,
        out_specs=VMEM,
        compiler_params=params(),
        name="pack",
    )(*pieces)
    return out.reshape(8 * rows, columns)


def merge(lengths, keep, got):
    start, _ = long_window(lengths)
    position = lax.axis_index("seq")
    q_cols = 16
    slot = jnp.arange(keep.shape[0], dtype=jnp.int32)
    token = (slot // q_cols) * (lax.axis_size("seq") * q_cols) + position * q_cols + slot % q_cols
    mine = ((token >= start) == (position % 2 == 0))[:, None]
    return jnp.concatenate([jnp.where(mine, keep, got), jnp.where(mine, got, keep)], axis=0)


def shards(
    clip, frame_counts, conv_first, conv_second, patch_weight, qkv_weight, query_gain, key_gain,
    out_weight, window_lengths,
):
    size = lax.axis_size("seq")
    facing = [(i, j) for i in range(1, size - 1, 2) for i, j in ((i, i + 1), (i + 1, i))]
    cores = [(i, i ^ 1) for i in range(size)]
    forward = ring_pairs()
    backward = [(j, i) for i, j in forward]

    def send(array, pairs):
        return lax.ppermute(array, "seq", pairs)

    def tied(*arrays):
        return lax.optimization_barrier(arrays)

    def tied(*arrays):
        return lax.optimization_barrier(arrays)

    def both_ways(ahead, behind):
        return send(ahead, forward), send(behind, backward)

    def tied(*arrays):
        return lax.optimization_barrier(arrays)

    def both_ways(ahead, behind):
        return send(ahead, forward), send(behind, backward)

    sibling_rows = send(clip, cores)
    other_rows = send(clip, facing)
    query_row, key_row = query_gain[None], key_gain[None]
    weight_one = both_ways(out_weight, out_weight)
    folded, query_weight, centered = fold(patch_weight, qkv_weight)
    sibling_rows, other_rows, *weight_one, folded = tied(sibling_rows, other_rows, *weight_one, folded)
    weight_two = both_ways(*weight_one)
    keep, other = convolve(
        frame_counts, window_lengths, clip, sibling_rows, other_rows, conv_first, conv_second, patch_weight
    )
    got = send(other, cores)
    got, wu_a, wu_b = tied(got, *weight_two)
    weight_two = (wu_a, wu_b)
    weight_three = both_ways(*weight_two)
    block = jnp.concatenate([keep, got], axis=0)
    one = both_ways(block, block)
    queries = make_queries(window_lengths, block, centered, query_weight, query_row)
    *one, queries = tied(*one, queries)
    two = both_ways(*one)
    acc_one = step_attention((-1, 1), window_lengths, one, folded, key_row, queries)
    wt_a, wt_b, acc_one = tied(*weight_three, acc_one)
    cut = 640
    weight_four = both_ways(wt_a[:, :cut], wt_b[:, cut:])
    *two, acc_one = tied(*two, acc_one)
    three = both_ways(*two)
    acc_two = step_attention((-2, 2), window_lengths, two, folded, key_row, queries)
    *three, acc_two, wf_a, wf_b = tied(*three, acc_two, *weight_four)
    four = both_ways(three[0][:64], three[1][64:])
    weights = pack([out_weight, *weight_one, *weight_two, wt_a, wt_b, wf_a, wf_b])
    sibling = send(weights, cores)
    acc_three = step_attention((-3, 3), window_lengths, three, folded, key_row, queries)
    *four, acc_three = tied(*four, acc_three)
    acc_four = step_attention((0, 4, 4), window_lengths, [block, *four], folded, key_row, queries)
    keep_rows, send_rows = project_out((acc_one, acc_two, acc_three, acc_four), (weights, sibling))
    return merge(window_lengths, keep_rows, send(send_rows, cores))


def solution(mesh):
    own = mesh.shape["seq"] == HEADS
    return jax.shard_map(
        shards if own else general_shards,
        mesh=mesh,
        in_specs=(
            P("groups", "seq", None, None),
            P("groups"),
            P(),
            P(),
            P(),
            P(),
            P(),
            P(),
            P("seq", None),
            P("groups", None),
        ),
        out_specs=P(("groups", "seq"), None),
        check_vma=False,
    )
```

```python
import functools
import math

import jax
import jax.numpy as jnp
from jax import lax
from jax.experimental import pallas as pl
from jax.experimental.pallas import tpu as pltpu
from jax.sharding import PartitionSpec as P

D = 1152
HEADS = 16


def extended(array, sides, width):
    for axis, dim in sides:
        size, length = (lax.axis_size(axis), array.shape[dim])
        up = [(i, (i + 1) % size) for i in range(size - 1)]
        down = [(j, i) for i, j in up]
        last = lax.slice_in_dim(array, length - width, length, axis=dim)
        first = lax.slice_in_dim(array, 0, width, axis=dim)
        before = lax.ppermute(last, axis, up)
        after = lax.ppermute(first, axis, down)
        array = jnp.concatenate([before, array, after], axis=dim)
    return array


def frame_weights(frame_counts, frames):
    position = jnp.arange(frames, dtype=jnp.int32)
    clip_ends = jnp.cumsum(frame_counts)

    def clip_of(index):
        return jnp.sum((index[:, None] >= clip_ends[None, :]).astype(jnp.int32), axis=1)

    own_clip = clip_of(position)
    columns = []
    for offset in (-1, 0, 1):
        neighbor = position + offset
        inside = (neighbor >= 0) & (neighbor < frames)
        same_clip = clip_of(jnp.clip(neighbor, 0, frames - 1)) == own_clip
        columns.append((inside & same_clip).astype(jnp.float32))
    return jnp.stack(columns, axis=1)


def convolve_rows(activation, kernel, tap_weights):
    empty_frame = jnp.zeros_like(activation[:1])
    shifted = (
        jnp.concatenate([empty_frame, activation[:-1]], 0),
        activation,
        jnp.concatenate([activation[1:], empty_frame], 0),
    )
    summed = None
    for offset in range(3):
        response = lax.conv_general_dilated(
            shifted[offset],
            kernel[offset],
            (1, 1),
            ((0, 0), (1, 1)),
            dimension_numbers=("NHWC", "HWIO", "NHWC"),
            preferred_element_type=jnp.float32,
        )
        tap_term = tap_weights[:, offset][:, None, None, None] * response
        summed = tap_term if offset == 0 else summed + tap_term
    return summed


def rms_scale(part, gain):
    factor = lax.rsqrt(jnp.mean(part * part, axis=-1, keepdims=True) + 1e-06)
    return (part * factor * gain).astype(jnp.bfloat16)


def general_shards(
    clip,
    frame_counts,
    conv_first,
    conv_second,
    patch_weight,
    qkv_weight,
    query_gain,
    key_gain,
    out_weight,
    window_lengths,
):
    frames, tile_rows, tile_cols, channels = clip.shape
    devices = lax.axis_size("seq")
    position = lax.axis_index("seq")
    head_dim = D // HEADS
    score_scale = 1.0 / math.sqrt(head_dim)
    tap_weights = frame_weights(frame_counts, frames)
    source = clip.astype(jnp.float32)
    padded_clip = extended(clip, (("seq", 1),), 2)
    first_in = jax.nn.silu(padded_clip.astype(jnp.float32)).astype(jnp.bfloat16)
    hidden_wide = convolve_rows(first_in, conv_first, tap_weights)
    global_row = position * tile_rows - 1 + jnp.arange(tile_rows + 2, dtype=jnp.int32)
    inside = ((global_row >= 0) & (global_row < tile_rows * devices)).astype(jnp.float32)
    hidden_one = (hidden_wide * inside[None, :, None, None]).astype(jnp.bfloat16)
    padded_second = jax.nn.silu(hidden_one.astype(jnp.float32)).astype(jnp.bfloat16)
    latent = (source + convolve_rows(padded_second, conv_second, tap_weights)).astype(jnp.bfloat16)
    token_rows = tile_rows // 2
    token_cols = tile_cols // 2
    patches = (
        latent.reshape(frames, token_rows, 2, token_cols, 2, channels)
        .transpose(0, 1, 3, 2, 4, 5)
        .reshape(-1, 4 * channels)
    )
    tok_count = patches.shape[0]
    embedded = jnp.dot(patches, patch_weight, preferred_element_type=jnp.float32).astype(
        jnp.bfloat16
    )
    values_f = embedded.astype(jnp.float32)
    row_mean = jnp.mean(values_f, axis=-1, keepdims=True)
    centered = values_f - row_mean
    variance = jnp.mean(centered * centered, axis=-1, keepdims=True)
    normed = (centered / jnp.sqrt(variance + 1e-06)).astype(jnp.bfloat16)
    projected = jnp.dot(normed, qkv_weight, preferred_element_type=jnp.float32).reshape(
        tok_count, 3, HEADS, head_dim
    )
    stacked = jnp.stack(
        [
            rms_scale(projected[:, 0], query_gain),
            rms_scale(projected[:, 1], key_gain),
            projected[:, 2].astype(jnp.bfloat16),
        ],
        axis=1,
    )
    groups = devices // HEADS
    frame_share = frames // groups
    local_share = tok_count // groups
    span_rows = devices * local_share
    outgoing = (
        stacked.reshape(groups, local_share, 3, HEADS, head_dim)
        .transpose(0, 3, 1, 2, 4)
        .reshape(devices, local_share, 3 * head_dim)
    )
    incoming = lax.all_to_all(outgoing, "seq", split_axis=0, concat_axis=0, tiled=True)
    arranged = (
        incoming.reshape(devices, frame_share, token_rows * token_cols, 3, head_dim)
        .transpose(3, 1, 0, 2, 4)
        .reshape(3, span_rows, head_dim)
    )
    my_group = position // HEADS
    lengths = lax.dynamic_index_in_dim(window_lengths, my_group, 0, keepdims=False)
    window_ends = jnp.cumsum(lengths)
    token_index = jnp.arange(span_rows, dtype=jnp.int32)
    segment = jnp.sum((token_index[:, None] >= window_ends[None, :]).astype(jnp.int32), axis=1)
    key_rows = arranged[1]
    value_rows = arranged[2]
    block_rows = min(512, span_rows)
    block_count = span_rows // block_rows

    def attend_block(inputs):
        query_block, segment_block = inputs
        scores = jnp.dot(query_block, key_rows.T, preferred_element_type=jnp.float32) * score_scale
        allowed = segment_block[:, None] == segment[None, :]
        scores = jnp.where(allowed, scores, -1e30)
        row_peak = jnp.max(scores, axis=-1, keepdims=True)
        weights = jnp.exp(scores - row_peak)
        row_mass = jnp.sum(weights, axis=-1, keepdims=True)
        mixed = (
            jnp.dot(weights.astype(jnp.bfloat16), value_rows, preferred_element_type=jnp.float32)
            / row_mass
        )
        return mixed.astype(jnp.bfloat16)

    mixed_rows = lax.map(
        attend_block,
        (
            arranged[0].reshape(block_count, block_rows, head_dim),
            segment.reshape(block_count, block_rows),
        ),
    ).reshape(span_rows, head_dim)
    outgoing_back = (
        mixed_rows.reshape(frame_share, devices, token_rows * token_cols, head_dim)
        .transpose(1, 0, 2, 3)
        .reshape(devices, local_share, head_dim)
    )
    returned = lax.all_to_all(outgoing_back, "seq", split_axis=0, concat_axis=0, tiled=True)
    merged = (
        returned.reshape(groups, HEADS, local_share, head_dim)
        .transpose(0, 2, 1, 3)
        .reshape(tok_count, D)
    )
    projected_out = jnp.dot(
        merged,
        lax.all_gather(out_weight, "seq", axis=0, tiled=True),
        preferred_element_type=jnp.float32,
    )
    return projected_out.astype(jnp.bfloat16)


HD = D // HEADS
SLOT = 80
MASK = 1024.0
F32 = jnp.float32
BF16 = jnp.bfloat16
VMEM = pl.BlockSpec(memory_space=pltpu.VMEM)
SMEM = pl.BlockSpec(memory_space=pltpu.SMEM)
NT = (((1,), (1,)), ((), ()))


def params(mib=40):
    return pltpu.CompilerParams(vmem_limit_bytes=mib << 20)


def silu(v):
    return v / (1.0 + jnp.exp(-v))


def long_window(lengths):
    first, second = lengths[0, 0], lengths[0, 1]
    half = 1024
    start = jnp.where(first == half, 0, jnp.where(second == half, first, first + second))
    bound = jnp.where(first == half, half + second, first)
    return start, bound


ANY = pl.BlockSpec(memory_space=pl.ANY)
TN = (((0,), (1,)), ((), ()))


def pair_weights(weights, o, ch=128):
    blank = jnp.zeros((ch, ch), BF16)
    rows = []
    for four in range(4):
        for j in range(3):
            taps = [weights[o, four - r, j] if 0 <= four - r < 3 else blank for r in range(2)]
            rows.append(jnp.concatenate(taps, axis=1))
    return jnp.concatenate(rows, axis=0)


def fold_kernel(patch_any, qkv_any, folded_ref, query_ref, centered_ref, patch_ref, qkv_ref, sems):
    copies = [
        pltpu.make_async_copy(patch_any, patch_ref, sems.at[0]),
        pltpu.make_async_copy(qkv_any.at[:, pl.ds(D, D)], qkv_ref.at[0], sems.at[1]),
        pltpu.make_async_copy(qkv_any.at[:, pl.ds(2 * D, D)], qkv_ref.at[1], sems.at[2]),
        pltpu.make_async_copy(qkv_any.at[:, pl.ds(0, D)], query_ref, sems.at[3]),
    ]
    for copy in copies:
        copy.start()
    copies[0].wait()
    patch = patch_ref[...].astype(F32)
    centered_ref[...] = (patch - jnp.mean(patch, axis=1, keepdims=True)).astype(BF16)
    for part in range(2):
        copies[part + 1].wait()
        product = lax.dot_general(qkv_ref[part], centered_ref[...], TN, preferred_element_type=F32)
        folded_ref[part * D : (part + 1) * D] = product.astype(BF16)
    copies[3].wait()


def fold(patch_weight, qkv_weight):
    inner = patch_weight.shape[0]
    return pl.pallas_call(
        fold_kernel,
        out_shape=(
            jax.ShapeDtypeStruct((2 * D, inner), BF16),
            jax.ShapeDtypeStruct((D, D), BF16),
            jax.ShapeDtypeStruct((inner, D), BF16),
        ),
        in_specs=[ANY, ANY],
        out_specs=(VMEM, VMEM, VMEM),
        scratch_shapes=[
            pltpu.VMEM((inner, D), BF16),
            pltpu.VMEM((2, D, D), BF16),
            pltpu.SemaphoreType.DMA((4,)),
        ],
        compiler_params=params(),
        name="fold",
        cost_estimate=pl.CostEstimate(flops=2 * inner * D * 2 * D, bytes_accessed=12 << 20, transcendentals=0),
    )(patch_weight, qkv_weight)


def frame_taps(counts_ref, frames):
    def clip_of(frame):
        end = 0
        index = 0
        for c in range(counts_ref.shape[0]):
            end = end + counts_ref[c]
            index = index + jnp.where(frame >= end, 1, 0)
        return index

    own = [clip_of(f) for f in range(frames)]
    joined = [jnp.where(own[f] == own[f + 1], 1.0, 0.0) for f in range(frames - 1)]
    return [0.0] + joined, joined + [0.0]


def conv_kernel(
    counts_any, lengths_any, own_any, patch_any, sibling_ref, other_ref, first_ref, second_ref,
    keep_ref, send_ref, grid_one, grid_two, pixels, own_ref, patch_ref, counts_ref, lengths_ref, sems,
):
    copies = [
        pltpu.make_async_copy(own_any, own_ref, sems.at[0]),
        pltpu.make_async_copy(counts_any, counts_ref, sems.at[1]),
        pltpu.make_async_copy(lengths_any, lengths_ref, sems.at[2]),
        pltpu.make_async_copy(patch_any, patch_ref, sems.at[3]),
    ]
    for copy in copies:
        copy.start()
    frames, _, cols, ch = own_ref.shape
    wide = 12 * ch
    position = lax.axis_index("seq")
    column = lax.broadcasted_iota(jnp.int32, (frames, cols, ch), 1)

    def shifted(row):
        left = jnp.where(column == 0, 0.0, pltpu.roll(row, 1, 1))
        right = jnp.where(column == cols - 1, 0.0, pltpu.roll(row, cols - 1, 1))
        return [part.astype(BF16) for part in (left, row, right)]

    blank = jnp.zeros((cols, wide), BF16)
    for g in range(2):
        grid_one[g, 0] = blank
        grid_one[g, frames + 1] = blank
    grid_two[0] = blank
    grid_two[frames + 1] = blank
    on_first = position % 2 == 0

    def source_row(r):
        if r in (2, 3):
            return own_ref[:, r - 2].astype(F32)
        sibling, other = sibling_ref[:, r % 2].astype(F32), other_ref[:, r % 2].astype(F32)
        return jnp.where(on_first, other, sibling) if r < 2 else jnp.where(on_first, sibling, other)

    for r in (0, 1, 4, 5, 2, 3):
        if r == 2:
            copies[0].wait()
        row = silu(source_row(r))
        parts = shifted(row)
        for g in range(2):
            four = r - 2 * g
            if 0 <= four < 4:
                for j in range(3):
                    grid_one[g, 1 : frames + 1, :, (four * 3 + j) * ch : (four * 3 + j + 1) * ch] = parts[j]

    copies[1].wait()
    copies[2].wait()
    before_tap, after_tap = frame_taps(counts_ref, frames)

    def summed(terms):
        rows = []
        for f in range(frames):
            total = terms[1][f]
            if f > 0:
                total = total + before_tap[f] * terms[0][f]
            if f < frames - 1:
                total = total + after_tap[f] * terms[2][f]
            rows.append(total)
        return jnp.stack(rows)

    for g in range(2):
        terms = []
        for o in range(3):
            left = grid_one[g, o : o + frames].reshape(frames * cols, wide)
            terms.append(
                jnp.dot(left, pair_weights(first_ref, o), preferred_element_type=F32).reshape(frames, cols, 2 * ch)
            )
        hidden = summed(terms)
        for out_row in range(2):
            four = 2 * g + out_row
            row = hidden[:, :, out_row * ch : (out_row + 1) * ch]
            if four == 0:
                row = row * jnp.where(position == 0, 0.0, 1.0)
            if four == 3:
                row = row * jnp.where(position == lax.axis_size("seq") - 1, 0.0, 1.0)
            row = silu(row.astype(BF16).astype(F32))
            parts = shifted(row)
            for j in range(3):
                grid_two[1 : frames + 1, :, (four * 3 + j) * ch : (four * 3 + j + 1) * ch] = parts[j]
    terms = []
    for o in range(3):
        left = grid_two[o : o + frames].reshape(frames * cols, wide)
        terms.append(
            jnp.dot(left, pair_weights(second_ref, o), preferred_element_type=F32).reshape(frames, cols, 2 * ch)
        )
    residual = summed(terms)
    for out_row in range(2):
        block = own_ref[:, out_row].astype(F32) + residual[:, :, out_row * ch : (out_row + 1) * ch]
        pixels[out_row] = block.astype(BF16).astype(F32).reshape(frames * cols, ch)
    tokens = frames * cols // 2
    patches = jnp.concatenate(
        [pixels[a, pl.ds(b, tokens, 2), :] for a in range(2) for b in range(2)], axis=1
    )
    copies[3].wait()
    embedded = jnp.dot(patches.astype(BF16), patch_ref[...], preferred_element_type=F32)
    centered = embedded - jnp.mean(embedded, axis=1, keepdims=True)
    variance = jnp.mean(centered * centered, axis=1, keepdims=True)
    scaled = patches * (1.0 / jnp.sqrt(variance + 1e-06))
    half = tokens // 2
    low, high = scaled[:half], scaled[half:]
    start, _ = long_window(lengths_ref)
    q_cols = cols // 2
    slot = lax.broadcasted_iota(jnp.int32, low.shape, 0)
    token = (slot // q_cols) * (lax.axis_size("seq") * q_cols) + position * q_cols + slot % q_cols
    inside = jnp.where(token >= start, 1, 0)
    mine = inside == jnp.where(position % 2 == 0, 1, 0)
    keep = jnp.where(mine, low, high).astype(BF16)
    send = jnp.where(mine, high, low).astype(BF16)
    keep_ref[...] = keep
    send_ref[...] = send


def convolve(counts, lengths, clip, sibling_rows, other_rows, conv_first, conv_second, patch_weight):
    frames, _, cols, ch = clip.shape
    tokens = frames * cols // 2
    out = jax.ShapeDtypeStruct((tokens // 2, 4 * ch), BF16)
    return pl.pallas_call(
        conv_kernel,
        out_shape=(out, out),
        in_specs=[ANY] * 4 + [VMEM] * 4,
        out_specs=(VMEM, VMEM),
        scratch_shapes=[
            pltpu.VMEM((2, frames + 2, cols, 12 * ch), BF16),
            pltpu.VMEM((frames + 2, cols, 12 * ch), BF16),
            pltpu.VMEM((2, frames * cols, ch), F32),
            pltpu.VMEM(clip.shape, BF16),
            pltpu.VMEM(patch_weight.shape, BF16),
            pltpu.SMEM(counts.shape, jnp.int32),
            pltpu.SMEM(lengths.shape, jnp.int32),
            pltpu.SemaphoreType.DMA((4,)),
        ],
        compiler_params=params(),
        name="convolve",
        cost_estimate=pl.CostEstimate(flops=2 << 30, bytes_accessed=4 << 20, transcendentals=1 << 18),
    )(counts, lengths, clip, patch_weight, sibling_rows, other_rows, conv_first, conv_second)


def chip_at(place):
    chips = lax.axis_size("seq") // 2
    place = lax.rem(place + 2 * chips, chips)
    return jnp.where(place < chips // 2, 2 * place, 2 * (chips - 1 - place) + 1)


def ring_place():
    chips = lax.axis_size("seq") // 2
    chip = lax.axis_index("seq") // 2
    return jnp.where(chip % 2 == 0, chip // 2, chips - 1 - chip // 2)


def ring_pairs():
    size = lax.axis_size("seq")
    chips = size // 2
    order = [2 * i for i in range(chips // 2)] + [2 * i + 1 for i in reversed(range(chips // 2))]
    return [
        (2 * order[i] + core, 2 * order[(i + 1) % chips] + core) for i in range(chips) for core in range(2)
    ]


def window_sides(lengths_ref, chip, count):
    size = lax.axis_size("seq")
    core = lax.axis_index("seq") % 2
    start, bound = long_window(lengths_ref)
    lane = lax.broadcasted_iota(jnp.int32, (8, count), 1)
    half = count // 2
    slot = lane % half
    row = 2 * chip + jnp.where(lane < half, core, 1 - core)
    q_cols = 16
    token = (slot // q_cols) * (size * q_cols) + row * q_cols + slot % q_cols
    inside = jnp.where(token >= start, 1, 0)
    upper = inside != jnp.where(core == 0, 1, 0)
    token = jnp.where(upper, token + 4 * size * q_cols, token)
    return jnp.where(token < bound, 1.0, -1.0)


def normed_heads(part, gain):
    count = part.shape[1]
    heads = part.reshape(-1, HD, count)
    factor = lax.rsqrt(jnp.mean(heads * heads, axis=1, keepdims=True) + 1e-06)
    return heads * factor * gain[None]


def as_column(row):
    size = row.shape[1]
    square = (size, size)
    same = lax.broadcasted_iota(jnp.int32, square, 0) == lax.broadcasted_iota(jnp.int32, square, 1)
    return jnp.sum(jnp.where(same, jnp.broadcast_to(row, square), 0.0), axis=1, keepdims=True)


def attend(tokens, sides, folded, key_gain, queries, acc_ref, keys_ref, values_ref, scores_ref, weights_ref):
    count = tokens.shape[0]
    row = lax.broadcasted_iota(jnp.int32, (8, count), 0)
    key_tail = jnp.where(row == 0, sides, jnp.where(row == 1, 1.0, 0.0))
    value_tail = jnp.where(row == 0, 1.0, 0.0)
    heads_at_once = 4
    for first in range(0, HEADS, heads_at_once):
        rows = slice(first * HD, (first + heads_at_once) * HD)
        part = lax.dot_general(folded[rows], tokens, NT, preferred_element_type=F32)
        keys = normed_heads(part, key_gain)
        for h in range(heads_at_once):
            keys_ref[first + h] = jnp.concatenate([keys[h], key_tail], axis=0).astype(BF16)
    for first in range(0, HEADS, heads_at_once):
        rows = slice(D + first * HD, D + (first + heads_at_once) * HD)
        part = lax.dot_general(folded[rows], tokens, NT, preferred_element_type=F32)
        values = part.reshape(heads_at_once, HD, count)
        for h in range(heads_at_once):
            values_ref[first + h] = jnp.concatenate([values[h], value_tail], axis=0).astype(BF16)
    for h in range(HEADS):
        scores_ref[h] = jnp.dot(queries[h], keys_ref[h], preferred_element_type=F32)
    lane = lax.broadcasted_iota(jnp.int32, (128, 128), 1)
    peaks = jnp.zeros((128, 128), F32)
    for h in range(HEADS):
        scores = scores_ref[h]
        peak = jnp.max(scores, axis=1, keepdims=True)
        weights_ref[h] = jnp.exp2(scores - peak).astype(BF16)
        peaks = jnp.where(lane == h, peak, peaks)
    peaks = peaks.T
    tail_row = lax.broadcasted_iota(jnp.int32, (8, 128), 0)
    for h in range(HEADS):
        mixed = lax.dot_general(values_ref[h], weights_ref[h], NT, preferred_element_type=F32)
        acc_ref[h, :HD] = mixed[:HD]
        acc_ref[h, HD:] = jnp.where(tail_row == 1, peaks[h : h + 1], mixed[HD:])


def attend_scratch(count):
    return [
        pltpu.VMEM((HEADS, SLOT, count), BF16),
        pltpu.VMEM((HEADS, SLOT, count), BF16),
        pltpu.VMEM((HEADS, 128, count), F32),
        pltpu.VMEM((HEADS, 128, count), BF16),
    ]


def query_kernel(lengths_ref, block_ref, centered_ref, query_ref, query_gain_ref, queries_ref):
    normed = jnp.dot(block_ref[...], centered_ref[...], preferred_element_type=F32).astype(BF16)
    part = jnp.dot(normed, query_ref[...], preferred_element_type=F32).T
    count = part.shape[1]
    sides = window_sides(lengths_ref, lax.axis_index("seq") // 2, count)
    queries = normed_heads(part, as_column(query_gain_ref[...] * (math.log2(math.e) / math.sqrt(HD))))
    row = lax.broadcasted_iota(jnp.int32, (8, count), 0)
    tail = jnp.where(row == 0, MASK * sides, jnp.where(row == 1, -MASK, 0.0))
    for h in range(HEADS):
        queries_ref[h] = jnp.concatenate([queries[h], tail], axis=0).T.astype(BF16)


def make_queries(lengths, block, centered, query_weight, query_gain):
    return pl.pallas_call(
        query_kernel,
        out_shape=jax.ShapeDtypeStruct((HEADS, 128, SLOT), BF16),
        in_specs=[SMEM] + [VMEM] * 4,
        out_specs=VMEM,
        compiler_params=params(),
        name="queries",
        cost_estimate=pl.CostEstimate(flops=1 << 30, bytes_accessed=4 << 20, transcendentals=0),
    )(lengths, block, centered, query_weight, query_gain)


def step_kernel(offsets, lengths_ref, *refs):
    blocks = refs[: len(offsets)]
    folded_ref, key_gain_ref, queries_ref, acc_ref, *scratch = refs[len(offsets) :]
    place = ring_place()
    tokens = jnp.concatenate([ref[...] for ref in blocks], axis=0)
    sides = jnp.concatenate(
        [window_sides(lengths_ref, chip_at(place + offset), 128) for offset in dict.fromkeys(offsets)], axis=1
    )
    attend(tokens, sides, folded_ref, as_column(key_gain_ref[...]), queries_ref, acc_ref, *scratch)


ACC = jax.ShapeDtypeStruct((HEADS, SLOT, 128), F32)


def step_attention(offsets, lengths, blocks, folded, key_gain, queries):
    count = sum(block.shape[0] for block in blocks)
    flops = 2 * count * 2 * D * 512 + 4 * HEADS * 128 * 128 * count
    return pl.pallas_call(
        functools.partial(step_kernel, offsets),
        out_shape=ACC,
        in_specs=[SMEM] + [VMEM] * (len(blocks) + 3),
        out_specs=VMEM,
        scratch_shapes=attend_scratch(count),
        compiler_params=params(),
        name="step_attention",
        cost_estimate=pl.CostEstimate(flops=2 * flops, bytes_accessed=5 << 20, transcendentals=HEADS * 128 * count),
    )(lengths, *blocks, folded, key_gain, queries)


RING = (0, -1, 1, -2, 2, -3, 3, 4)


def out_kernel(parts, *refs):
    acc_refs = refs[:parts]
    weight_refs = refs[parts:-3]
    keep_ref, send_ref, mixed_ref = refs[-3:]
    for h in range(HEADS):
        peaks = [acc[h, HD + 1 : HD + 2] for acc in acc_refs]
        peak = functools.reduce(jnp.maximum, peaks)
        total = None
        for acc, own in zip(acc_refs, peaks):
            term = acc[h] * jnp.exp2(own - peak)
            total = term if total is None else total + term
        mixed_ref[h] = total[:HD] / total[HD : HD + 1]
    place = ring_place()
    core = lax.axis_index("seq") % 2
    lefts = []
    for side in range(2):
        heads = [2 * chip_at(place + offset) + jnp.where(core == side, 0, 1) for offset in RING]
        lefts.append(jnp.concatenate([mixed_ref[head] for head in heads], axis=0).T.astype(BF16))
    half = keep_ref.shape[0]
    for first in range(0, D, 256):
        columns = slice(first, min(first + 256, D))
        result = jnp.dot(lefts[0], weight_refs[0][:, columns], preferred_element_type=F32)
        result = result + jnp.dot(lefts[1], weight_refs[1][:, columns], preferred_element_type=F32)
        result = result.astype(BF16)
        keep_ref[:, columns] = result[:half]
        send_ref[:, columns] = result[half:]


def project_out(accs, weights):
    out = jax.ShapeDtypeStruct((64, D), BF16)
    return pl.pallas_call(
        functools.partial(out_kernel, len(accs)),
        out_shape=(out, out),
        in_specs=[VMEM] * (len(accs) + len(weights)),
        out_specs=(VMEM, VMEM),
        scratch_shapes=[pltpu.VMEM((HEADS, HD, 128), F32)],
        compiler_params=params(),
        name="project_out",
        cost_estimate=pl.CostEstimate(flops=2 * 128 * 1280 * D, bytes_accessed=4 << 20, transcendentals=0),
    )(*accs, *weights)


def pack_kernel(*refs):
    out_ref = refs[-1]
    for i in range(7):
        out_ref[i] = refs[i][...]
    cut = refs[7].shape[1]
    out_ref[7, :, :cut] = refs[7][...]
    out_ref[7, :, cut:] = refs[8][...]


def pack(pieces):
    rows, columns = pieces[0].shape
    out = pl.pallas_call(
        pack_kernel,
        out_shape=jax.ShapeDtypeStruct((8, rows, columns), BF16),
        in_specs=[VMEM] * 9,
        out_specs=VMEM,
        compiler_params=params(),
        name="pack",
    )(*pieces)
    return out.reshape(8 * rows, columns)


def merge_kernel(lengths_ref, keep_ref, got_ref, out_ref):
    position = lax.axis_index("seq")
    keep = keep_ref[...].astype(F32)
    got = got_ref[...].astype(F32)
    start, _ = long_window(lengths_ref)
    q_cols = 16
    slot = lax.broadcasted_iota(jnp.int32, keep.shape, 0)
    token = (slot // q_cols) * (lax.axis_size("seq") * q_cols) + position * q_cols + slot % q_cols
    inside = jnp.where(token >= start, 1, 0)
    mine = inside == jnp.where(position % 2 == 0, 1, 0)
    half = keep.shape[0]
    out_ref[:half] = jnp.where(mine, keep, got).astype(BF16)
    out_ref[half:] = jnp.where(mine, got, keep).astype(BF16)


def merge(lengths, keep, got):
    return pl.pallas_call(
        merge_kernel,
        out_shape=jax.ShapeDtypeStruct((128, D), BF16),
        in_specs=[SMEM, VMEM, VMEM],
        out_specs=VMEM,
        compiler_params=params(),
        name="merge",
    )(lengths, keep, got)


def shards(
    clip, frame_counts, conv_first, conv_second, patch_weight, qkv_weight, query_gain, key_gain,
    out_weight, window_lengths,
):
    size = lax.axis_size("seq")
    facing = [(i, j) for i in range(1, size - 1, 2) for i, j in ((i, i + 1), (i + 1, i))]
    cores = [(i, i ^ 1) for i in range(size)]
    forward = ring_pairs()
    backward = [(j, i) for i, j in forward]

    def send(array, pairs):
        return lax.ppermute(array, "seq", pairs)

    def tied(*arrays):
        return lax.optimization_barrier(arrays)

    def tied(*arrays):
        return lax.optimization_barrier(arrays)

    def both_ways(ahead, behind):
        return send(ahead, forward), send(behind, backward)

    def tied(*arrays):
        return lax.optimization_barrier(arrays)

    def both_ways(ahead, behind):
        return send(ahead, forward), send(behind, backward)

    sibling_rows = send(clip, cores)
    other_rows = send(clip, facing)
    query_row, key_row = query_gain[None], key_gain[None]
    weight_one = both_ways(out_weight, out_weight)
    folded, query_weight, centered = fold(patch_weight, qkv_weight)
    sibling_rows, other_rows, *weight_one, folded = tied(sibling_rows, other_rows, *weight_one, folded)
    weight_two = both_ways(*weight_one)
    keep, other = convolve(
        frame_counts, window_lengths, clip, sibling_rows, other_rows, conv_first, conv_second, patch_weight
    )
    got = send(other, cores)
    got, wu_a, wu_b = tied(got, *weight_two)
    weight_two = (wu_a, wu_b)
    weight_three = both_ways(*weight_two)
    block = jnp.concatenate([keep, got], axis=0)
    one = both_ways(block, block)
    queries = make_queries(window_lengths, block, centered, query_weight, query_row)
    *one, queries = tied(*one, queries)
    two = both_ways(*one)
    acc_one = step_attention((-1, 1), window_lengths, one, folded, key_row, queries)
    *two, acc_one = tied(*two, acc_one)
    three = both_ways(*two)
    acc_two = step_attention((-2, 2), window_lengths, two, folded, key_row, queries)
    wt_a, wt_b, acc_two = tied(*weight_three, acc_two)
    cut = 640
    weight_four = both_ways(wt_a[:, :cut], wt_b[:, cut:])
    *three, acc_two = tied(*three, acc_two)
    four = both_ways(three[0][:64], three[1][64:])
    *three, wf_a, wf_b = tied(*three, *weight_four)
    weights = pack([out_weight, *weight_one, *weight_two, wt_a, wt_b, wf_a, wf_b])
    sibling = send(weights, cores)
    acc_three = step_attention((-3, 3), window_lengths, three, folded, key_row, queries)
    *four, acc_three = tied(*four, acc_three)
    acc_four = step_attention((0, 4, 4), window_lengths, [block, *four], folded, key_row, queries)
    keep_rows, send_rows = project_out((acc_one, acc_two, acc_three, acc_four), (weights, sibling))
    return merge(window_lengths, keep_rows, send(send_rows, cores))


def solution(mesh):
    own = mesh.shape["seq"] == HEADS
    return jax.shard_map(
        shards if own else general_shards,
        mesh=mesh,
        in_specs=(
            P("groups", "seq", None, None),
            P("groups"),
            P(),
            P(),
            P(),
            P(),
            P(),
            P(),
            P("seq", None),
            P("groups", None),
        ),
        out_specs=P(("groups", "seq"), None),
        check_vma=False,
    )
```

```python
import functools
import math

import jax
import jax.numpy as jnp
from jax import lax
from jax.experimental import pallas as pl
from jax.experimental.pallas import tpu as pltpu
from jax.sharding import PartitionSpec as P

D = 1152
HEADS = 16


def extended(array, sides, width):
    for axis, dim in sides:
        size, length = (lax.axis_size(axis), array.shape[dim])
        up = [(i, (i + 1) % size) for i in range(size - 1)]
        down = [(j, i) for i, j in up]
        last = lax.slice_in_dim(array, length - width, length, axis=dim)
        first = lax.slice_in_dim(array, 0, width, axis=dim)
        before = lax.ppermute(last, axis, up)
        after = lax.ppermute(first, axis, down)
        array = jnp.concatenate([before, array, after], axis=dim)
    return array


def frame_weights(frame_counts, frames):
    position = jnp.arange(frames, dtype=jnp.int32)
    clip_ends = jnp.cumsum(frame_counts)

    def clip_of(index):
        return jnp.sum((index[:, None] >= clip_ends[None, :]).astype(jnp.int32), axis=1)

    own_clip = clip_of(position)
    columns = []
    for offset in (-1, 0, 1):
        neighbor = position + offset
        inside = (neighbor >= 0) & (neighbor < frames)
        same_clip = clip_of(jnp.clip(neighbor, 0, frames - 1)) == own_clip
        columns.append((inside & same_clip).astype(jnp.float32))
    return jnp.stack(columns, axis=1)


def convolve_rows(activation, kernel, tap_weights):
    empty_frame = jnp.zeros_like(activation[:1])
    shifted = (
        jnp.concatenate([empty_frame, activation[:-1]], 0),
        activation,
        jnp.concatenate([activation[1:], empty_frame], 0),
    )
    summed = None
    for offset in range(3):
        response = lax.conv_general_dilated(
            shifted[offset],
            kernel[offset],
            (1, 1),
            ((0, 0), (1, 1)),
            dimension_numbers=("NHWC", "HWIO", "NHWC"),
            preferred_element_type=jnp.float32,
        )
        tap_term = tap_weights[:, offset][:, None, None, None] * response
        summed = tap_term if offset == 0 else summed + tap_term
    return summed


def rms_scale(part, gain):
    factor = lax.rsqrt(jnp.mean(part * part, axis=-1, keepdims=True) + 1e-06)
    return (part * factor * gain).astype(jnp.bfloat16)


def general_shards(
    clip,
    frame_counts,
    conv_first,
    conv_second,
    patch_weight,
    qkv_weight,
    query_gain,
    key_gain,
    out_weight,
    window_lengths,
):
    frames, tile_rows, tile_cols, channels = clip.shape
    devices = lax.axis_size("seq")
    position = lax.axis_index("seq")
    head_dim = D // HEADS
    score_scale = 1.0 / math.sqrt(head_dim)
    tap_weights = frame_weights(frame_counts, frames)
    source = clip.astype(jnp.float32)
    padded_clip = extended(clip, (("seq", 1),), 2)
    first_in = jax.nn.silu(padded_clip.astype(jnp.float32)).astype(jnp.bfloat16)
    hidden_wide = convolve_rows(first_in, conv_first, tap_weights)
    global_row = position * tile_rows - 1 + jnp.arange(tile_rows + 2, dtype=jnp.int32)
    inside = ((global_row >= 0) & (global_row < tile_rows * devices)).astype(jnp.float32)
    hidden_one = (hidden_wide * inside[None, :, None, None]).astype(jnp.bfloat16)
    padded_second = jax.nn.silu(hidden_one.astype(jnp.float32)).astype(jnp.bfloat16)
    latent = (source + convolve_rows(padded_second, conv_second, tap_weights)).astype(jnp.bfloat16)
    token_rows = tile_rows // 2
    token_cols = tile_cols // 2
    patches = (
        latent.reshape(frames, token_rows, 2, token_cols, 2, channels)
        .transpose(0, 1, 3, 2, 4, 5)
        .reshape(-1, 4 * channels)
    )
    tok_count = patches.shape[0]
    embedded = jnp.dot(patches, patch_weight, preferred_element_type=jnp.float32).astype(
        jnp.bfloat16
    )
    values_f = embedded.astype(jnp.float32)
    row_mean = jnp.mean(values_f, axis=-1, keepdims=True)
    centered = values_f - row_mean
    variance = jnp.mean(centered * centered, axis=-1, keepdims=True)
    normed = (centered / jnp.sqrt(variance + 1e-06)).astype(jnp.bfloat16)
    projected = jnp.dot(normed, qkv_weight, preferred_element_type=jnp.float32).reshape(
        tok_count, 3, HEADS, head_dim
    )
    stacked = jnp.stack(
        [
            rms_scale(projected[:, 0], query_gain),
            rms_scale(projected[:, 1], key_gain),
            projected[:, 2].astype(jnp.bfloat16),
        ],
        axis=1,
    )
    groups = devices // HEADS
    frame_share = frames // groups
    local_share = tok_count // groups
    span_rows = devices * local_share
    outgoing = (
        stacked.reshape(groups, local_share, 3, HEADS, head_dim)
        .transpose(0, 3, 1, 2, 4)
        .reshape(devices, local_share, 3 * head_dim)
    )
    incoming = lax.all_to_all(outgoing, "seq", split_axis=0, concat_axis=0, tiled=True)
    arranged = (
        incoming.reshape(devices, frame_share, token_rows * token_cols, 3, head_dim)
        .transpose(3, 1, 0, 2, 4)
        .reshape(3, span_rows, head_dim)
    )
    my_group = position // HEADS
    lengths = lax.dynamic_index_in_dim(window_lengths, my_group, 0, keepdims=False)
    window_ends = jnp.cumsum(lengths)
    token_index = jnp.arange(span_rows, dtype=jnp.int32)
    segment = jnp.sum((token_index[:, None] >= window_ends[None, :]).astype(jnp.int32), axis=1)
    key_rows = arranged[1]
    value_rows = arranged[2]
    block_rows = min(512, span_rows)
    block_count = span_rows // block_rows

    def attend_block(inputs):
        query_block, segment_block = inputs
        scores = jnp.dot(query_block, key_rows.T, preferred_element_type=jnp.float32) * score_scale
        allowed = segment_block[:, None] == segment[None, :]
        scores = jnp.where(allowed, scores, -1e30)
        row_peak = jnp.max(scores, axis=-1, keepdims=True)
        weights = jnp.exp(scores - row_peak)
        row_mass = jnp.sum(weights, axis=-1, keepdims=True)
        mixed = (
            jnp.dot(weights.astype(jnp.bfloat16), value_rows, preferred_element_type=jnp.float32)
            / row_mass
        )
        return mixed.astype(jnp.bfloat16)

    mixed_rows = lax.map(
        attend_block,
        (
            arranged[0].reshape(block_count, block_rows, head_dim),
            segment.reshape(block_count, block_rows),
        ),
    ).reshape(span_rows, head_dim)
    outgoing_back = (
        mixed_rows.reshape(frame_share, devices, token_rows * token_cols, head_dim)
        .transpose(1, 0, 2, 3)
        .reshape(devices, local_share, head_dim)
    )
    returned = lax.all_to_all(outgoing_back, "seq", split_axis=0, concat_axis=0, tiled=True)
    merged = (
        returned.reshape(groups, HEADS, local_share, head_dim)
        .transpose(0, 2, 1, 3)
        .reshape(tok_count, D)
    )
    projected_out = jnp.dot(
        merged,
        lax.all_gather(out_weight, "seq", axis=0, tiled=True),
        preferred_element_type=jnp.float32,
    )
    return projected_out.astype(jnp.bfloat16)


HD = D // HEADS
SLOT = 80
MASK = 1024.0
F32 = jnp.float32
BF16 = jnp.bfloat16
VMEM = pl.BlockSpec(memory_space=pltpu.VMEM)
SMEM = pl.BlockSpec(memory_space=pltpu.SMEM)
NT = (((1,), (1,)), ((), ()))


def params(mib=40):
    return pltpu.CompilerParams(vmem_limit_bytes=mib << 20)


def silu(v):
    return v / (1.0 + jnp.exp(-v))


def long_window(lengths):
    first, second = lengths[0, 0], lengths[0, 1]
    half = 1024
    start = jnp.where(first == half, 0, jnp.where(second == half, first, first + second))
    bound = jnp.where(first == half, half + second, first)
    return start, bound


ANY = pl.BlockSpec(memory_space=pl.ANY)
TN = (((0,), (1,)), ((), ()))


def pair_weights(weights, o, ch=128):
    blank = jnp.zeros((ch, ch), BF16)
    rows = []
    for four in range(4):
        for j in range(3):
            taps = [weights[o, four - r, j] if 0 <= four - r < 3 else blank for r in range(2)]
            rows.append(jnp.concatenate(taps, axis=1))
    return jnp.concatenate(rows, axis=0)


def fold_kernel(patch_any, qkv_any, folded_ref, query_ref, centered_ref, patch_ref, qkv_ref, sems):
    copies = [
        pltpu.make_async_copy(patch_any, patch_ref, sems.at[0]),
        pltpu.make_async_copy(qkv_any.at[:, pl.ds(D, D)], qkv_ref.at[0], sems.at[1]),
        pltpu.make_async_copy(qkv_any.at[:, pl.ds(2 * D, D)], qkv_ref.at[1], sems.at[2]),
        pltpu.make_async_copy(qkv_any.at[:, pl.ds(0, D)], query_ref, sems.at[3]),
    ]
    for copy in copies:
        copy.start()
    copies[0].wait()
    patch = patch_ref[...].astype(F32)
    centered_ref[...] = (patch - jnp.mean(patch, axis=1, keepdims=True)).astype(BF16)
    for part in range(2):
        copies[part + 1].wait()
        product = lax.dot_general(qkv_ref[part], centered_ref[...], TN, preferred_element_type=F32)
        folded_ref[part * D : (part + 1) * D] = product.astype(BF16)
    copies[3].wait()


def fold(patch_weight, qkv_weight):
    inner = patch_weight.shape[0]
    return pl.pallas_call(
        fold_kernel,
        out_shape=(
            jax.ShapeDtypeStruct((2 * D, inner), BF16),
            jax.ShapeDtypeStruct((D, D), BF16),
            jax.ShapeDtypeStruct((inner, D), BF16),
        ),
        in_specs=[ANY, ANY],
        out_specs=(VMEM, VMEM, VMEM),
        scratch_shapes=[
            pltpu.VMEM((inner, D), BF16),
            pltpu.VMEM((2, D, D), BF16),
            pltpu.SemaphoreType.DMA((4,)),
        ],
        compiler_params=params(),
        name="fold",
        cost_estimate=pl.CostEstimate(flops=2 * inner * D * 2 * D, bytes_accessed=12 << 20, transcendentals=0),
    )(patch_weight, qkv_weight)


def frame_taps(counts_ref, frames):
    def clip_of(frame):
        end = 0
        index = 0
        for c in range(counts_ref.shape[0]):
            end = end + counts_ref[c]
            index = index + jnp.where(frame >= end, 1, 0)
        return index

    own = [clip_of(f) for f in range(frames)]
    joined = [jnp.where(own[f] == own[f + 1], 1.0, 0.0) for f in range(frames - 1)]
    return [0.0] + joined, joined + [0.0]


def conv_kernel(
    counts_any, lengths_any, own_any, patch_any, sibling_ref, other_ref, first_ref, second_ref,
    keep_ref, send_ref, grid_one, grid_two, pixels, own_ref, patch_ref, counts_ref, lengths_ref, sems,
):
    copies = [
        pltpu.make_async_copy(own_any, own_ref, sems.at[0]),
        pltpu.make_async_copy(counts_any, counts_ref, sems.at[1]),
        pltpu.make_async_copy(lengths_any, lengths_ref, sems.at[2]),
        pltpu.make_async_copy(patch_any, patch_ref, sems.at[3]),
    ]
    for copy in copies:
        copy.start()
    frames, _, cols, ch = own_ref.shape
    wide = 12 * ch
    position = lax.axis_index("seq")
    column = lax.broadcasted_iota(jnp.int32, (frames, cols, ch), 1)

    def shifted(row):
        left = jnp.where(column == 0, 0.0, pltpu.roll(row, 1, 1))
        right = jnp.where(column == cols - 1, 0.0, pltpu.roll(row, cols - 1, 1))
        return [part.astype(BF16) for part in (left, row, right)]

    blank = jnp.zeros((cols, wide), BF16)
    for g in range(2):
        grid_one[g, 0] = blank
        grid_one[g, frames + 1] = blank
    grid_two[0] = blank
    grid_two[frames + 1] = blank
    on_first = position % 2 == 0

    def source_row(r):
        if r in (2, 3):
            return own_ref[:, r - 2].astype(F32)
        sibling, other = sibling_ref[:, r % 2].astype(F32), other_ref[:, r % 2].astype(F32)
        return jnp.where(on_first, other, sibling) if r < 2 else jnp.where(on_first, sibling, other)

    for r in (0, 1, 4, 5, 2, 3):
        if r == 2:
            copies[0].wait()
        row = silu(source_row(r))
        parts = shifted(row)
        for g in range(2):
            four = r - 2 * g
            if 0 <= four < 4:
                for j in range(3):
                    grid_one[g, 1 : frames + 1, :, (four * 3 + j) * ch : (four * 3 + j + 1) * ch] = parts[j]

    copies[1].wait()
    copies[2].wait()
    before_tap, after_tap = frame_taps(counts_ref, frames)

    def summed(terms):
        rows = []
        for f in range(frames):
            total = terms[1][f]
            if f > 0:
                total = total + before_tap[f] * terms[0][f]
            if f < frames - 1:
                total = total + after_tap[f] * terms[2][f]
            rows.append(total)
        return jnp.stack(rows)

    for g in range(2):
        terms = []
        for o in range(3):
            left = grid_one[g, o : o + frames].reshape(frames * cols, wide)
            terms.append(
                jnp.dot(left, pair_weights(first_ref, o), preferred_element_type=F32).reshape(frames, cols, 2 * ch)
            )
        hidden = summed(terms)
        for out_row in range(2):
            four = 2 * g + out_row
            row = hidden[:, :, out_row * ch : (out_row + 1) * ch]
            if four == 0:
                row = row * jnp.where(position == 0, 0.0, 1.0)
            if four == 3:
                row = row * jnp.where(position == lax.axis_size("seq") - 1, 0.0, 1.0)
            row = silu(row.astype(BF16).astype(F32))
            parts = shifted(row)
            for j in range(3):
                grid_two[1 : frames + 1, :, (four * 3 + j) * ch : (four * 3 + j + 1) * ch] = parts[j]
    terms = []
    for o in range(3):
        left = grid_two[o : o + frames].reshape(frames * cols, wide)
        terms.append(
            jnp.dot(left, pair_weights(second_ref, o), preferred_element_type=F32).reshape(frames, cols, 2 * ch)
        )
    residual = summed(terms)
    for out_row in range(2):
        block = own_ref[:, out_row].astype(F32) + residual[:, :, out_row * ch : (out_row + 1) * ch]
        pixels[out_row] = block.astype(BF16).astype(F32).reshape(frames * cols, ch)
    tokens = frames * cols // 2
    patches = jnp.concatenate(
        [pixels[a, pl.ds(b, tokens, 2), :] for a in range(2) for b in range(2)], axis=1
    )
    copies[3].wait()
    embedded = jnp.dot(patches.astype(BF16), patch_ref[...], preferred_element_type=F32)
    centered = embedded - jnp.mean(embedded, axis=1, keepdims=True)
    variance = jnp.mean(centered * centered, axis=1, keepdims=True)
    scaled = patches * (1.0 / jnp.sqrt(variance + 1e-06))
    half = tokens // 2
    low, high = scaled[:half], scaled[half:]
    start, _ = long_window(lengths_ref)
    q_cols = cols // 2
    slot = lax.broadcasted_iota(jnp.int32, low.shape, 0)
    token = (slot // q_cols) * (lax.axis_size("seq") * q_cols) + position * q_cols + slot % q_cols
    inside = jnp.where(token >= start, 1, 0)
    mine = inside == jnp.where(position % 2 == 0, 1, 0)
    keep = jnp.where(mine, low, high).astype(BF16)
    send = jnp.where(mine, high, low).astype(BF16)
    keep_ref[...] = keep
    send_ref[...] = send


def convolve(counts, lengths, clip, sibling_rows, other_rows, conv_first, conv_second, patch_weight):
    frames, _, cols, ch = clip.shape
    tokens = frames * cols // 2
    out = jax.ShapeDtypeStruct((tokens // 2, 4 * ch), BF16)
    return pl.pallas_call(
        conv_kernel,
        out_shape=(out, out),
        in_specs=[ANY] * 4 + [VMEM] * 4,
        out_specs=(VMEM, VMEM),
        scratch_shapes=[
            pltpu.VMEM((2, frames + 2, cols, 12 * ch), BF16),
            pltpu.VMEM((frames + 2, cols, 12 * ch), BF16),
            pltpu.VMEM((2, frames * cols, ch), F32),
            pltpu.VMEM(clip.shape, BF16),
            pltpu.VMEM(patch_weight.shape, BF16),
            pltpu.SMEM(counts.shape, jnp.int32),
            pltpu.SMEM(lengths.shape, jnp.int32),
            pltpu.SemaphoreType.DMA((4,)),
        ],
        compiler_params=params(),
        name="convolve",
        cost_estimate=pl.CostEstimate(flops=2 << 30, bytes_accessed=4 << 20, transcendentals=1 << 18),
    )(counts, lengths, clip, patch_weight, sibling_rows, other_rows, conv_first, conv_second)


def chip_at(place):
    chips = lax.axis_size("seq") // 2
    place = lax.rem(place + 2 * chips, chips)
    return jnp.where(place < chips // 2, 2 * place, 2 * (chips - 1 - place) + 1)


def ring_place():
    chips = lax.axis_size("seq") // 2
    chip = lax.axis_index("seq") // 2
    return jnp.where(chip % 2 == 0, chip // 2, chips - 1 - chip // 2)


def ring_pairs():
    size = lax.axis_size("seq")
    chips = size // 2
    order = [2 * i for i in range(chips // 2)] + [2 * i + 1 for i in reversed(range(chips // 2))]
    return [
        (2 * order[i] + core, 2 * order[(i + 1) % chips] + core) for i in range(chips) for core in range(2)
    ]


def window_sides(lengths_ref, chip, count):
    size = lax.axis_size("seq")
    core = lax.axis_index("seq") % 2
    start, bound = long_window(lengths_ref)
    lane = lax.broadcasted_iota(jnp.int32, (8, count), 1)
    half = count // 2
    slot = lane % half
    row = 2 * chip + jnp.where(lane < half, core, 1 - core)
    q_cols = 16
    token = (slot // q_cols) * (size * q_cols) + row * q_cols + slot % q_cols
    inside = jnp.where(token >= start, 1, 0)
    upper = inside != jnp.where(core == 0, 1, 0)
    token = jnp.where(upper, token + 4 * size * q_cols, token)
    return jnp.where(token < bound, 1.0, -1.0)


def normed_heads(part, gain):
    count = part.shape[1]
    heads = part.reshape(-1, HD, count)
    factor = lax.rsqrt(jnp.mean(heads * heads, axis=1, keepdims=True) + 1e-06)
    return heads * factor * gain[None]


def as_column(row):
    size = row.shape[1]
    square = (size, size)
    same = lax.broadcasted_iota(jnp.int32, square, 0) == lax.broadcasted_iota(jnp.int32, square, 1)
    return jnp.sum(jnp.where(same, jnp.broadcast_to(row, square), 0.0), axis=1, keepdims=True)


def attend(tokens, sides, folded, key_gain, queries, acc_ref, keys_ref, values_ref, scores_ref, weights_ref):
    count = tokens.shape[0]
    row = lax.broadcasted_iota(jnp.int32, (8, count), 0)
    key_tail = jnp.where(row == 0, sides, jnp.where(row == 1, 1.0, 0.0))
    value_tail = jnp.where(row == 0, 1.0, 0.0)
    heads_at_once = 4
    for first in range(0, HEADS, heads_at_once):
        rows = slice(first * HD, (first + heads_at_once) * HD)
        part = lax.dot_general(folded[rows], tokens, NT, preferred_element_type=F32)
        keys = normed_heads(part, key_gain)
        for h in range(heads_at_once):
            keys_ref[first + h] = jnp.concatenate([keys[h], key_tail], axis=0).astype(BF16)
    for first in range(0, HEADS, heads_at_once):
        rows = slice(D + first * HD, D + (first + heads_at_once) * HD)
        part = lax.dot_general(folded[rows], tokens, NT, preferred_element_type=F32)
        values = part.reshape(heads_at_once, HD, count)
        for h in range(heads_at_once):
            values_ref[first + h] = jnp.concatenate([values[h], value_tail], axis=0).astype(BF16)
    for h in range(HEADS):
        scores_ref[h] = jnp.dot(queries[h], keys_ref[h], preferred_element_type=F32)
    lane = lax.broadcasted_iota(jnp.int32, (128, 128), 1)
    peaks = jnp.zeros((128, 128), F32)
    for h in range(HEADS):
        scores = scores_ref[h]
        peak = jnp.max(scores, axis=1, keepdims=True)
        weights_ref[h] = jnp.exp2(scores - peak).astype(BF16)
        peaks = jnp.where(lane == h, peak, peaks)
    peaks = peaks.T
    tail_row = lax.broadcasted_iota(jnp.int32, (8, 128), 0)
    for h in range(HEADS):
        mixed = lax.dot_general(values_ref[h], weights_ref[h], NT, preferred_element_type=F32)
        acc_ref[h, :HD] = mixed[:HD]
        acc_ref[h, HD:] = jnp.where(tail_row == 1, peaks[h : h + 1], mixed[HD:])


def attend_scratch(count):
    return [
        pltpu.VMEM((HEADS, SLOT, count), BF16),
        pltpu.VMEM((HEADS, SLOT, count), BF16),
        pltpu.VMEM((HEADS, 128, count), F32),
        pltpu.VMEM((HEADS, 128, count), BF16),
    ]


def query_kernel(lengths_ref, block_ref, centered_ref, query_ref, query_gain_ref, queries_ref):
    normed = jnp.dot(block_ref[...], centered_ref[...], preferred_element_type=F32).astype(BF16)
    part = jnp.dot(normed, query_ref[...], preferred_element_type=F32).T
    count = part.shape[1]
    sides = window_sides(lengths_ref, lax.axis_index("seq") // 2, count)
    queries = normed_heads(part, as_column(query_gain_ref[...] * (math.log2(math.e) / math.sqrt(HD))))
    row = lax.broadcasted_iota(jnp.int32, (8, count), 0)
    tail = jnp.where(row == 0, MASK * sides, jnp.where(row == 1, -MASK, 0.0))
    for h in range(HEADS):
        queries_ref[h] = jnp.concatenate([queries[h], tail], axis=0).T.astype(BF16)


def make_queries(lengths, block, centered, query_weight, query_gain):
    return pl.pallas_call(
        query_kernel,
        out_shape=jax.ShapeDtypeStruct((HEADS, 128, SLOT), BF16),
        in_specs=[SMEM] + [VMEM] * 4,
        out_specs=VMEM,
        compiler_params=params(),
        name="queries",
        cost_estimate=pl.CostEstimate(flops=1 << 30, bytes_accessed=4 << 20, transcendentals=0),
    )(lengths, block, centered, query_weight, query_gain)


def step_kernel(offsets, lengths_ref, *refs):
    blocks = refs[: len(offsets)]
    folded_ref, key_gain_ref, queries_ref, acc_ref, *scratch = refs[len(offsets) :]
    place = ring_place()
    tokens = jnp.concatenate([ref[...] for ref in blocks], axis=0)
    sides = jnp.concatenate(
        [window_sides(lengths_ref, chip_at(place + offset), 128) for offset in dict.fromkeys(offsets)], axis=1
    )
    attend(tokens, sides, folded_ref, as_column(key_gain_ref[...]), queries_ref, acc_ref, *scratch)


ACC = jax.ShapeDtypeStruct((HEADS, SLOT, 128), F32)


def step_attention(offsets, lengths, blocks, folded, key_gain, queries):
    count = sum(block.shape[0] for block in blocks)
    flops = 2 * count * 2 * D * 512 + 4 * HEADS * 128 * 128 * count
    return pl.pallas_call(
        functools.partial(step_kernel, offsets),
        out_shape=ACC,
        in_specs=[SMEM] + [VMEM] * (len(blocks) + 3),
        out_specs=VMEM,
        scratch_shapes=attend_scratch(count),
        compiler_params=params(),
        name="step_attention",
        cost_estimate=pl.CostEstimate(flops=2 * flops, bytes_accessed=5 << 20, transcendentals=HEADS * 128 * count),
    )(lengths, *blocks, folded, key_gain, queries)


RING = (0, -1, 1, -2, 2, -3, 3, 4)


def out_kernel(parts, *refs):
    acc_refs = refs[:parts]
    weight_refs = refs[parts:-3]
    keep_ref, send_ref, mixed_ref = refs[-3:]
    for h in range(HEADS):
        peaks = [acc[h, HD + 1 : HD + 2] for acc in acc_refs]
        peak = functools.reduce(jnp.maximum, peaks)
        total = None
        for acc, own in zip(acc_refs, peaks):
            term = acc[h] * jnp.exp2(own - peak)
            total = term if total is None else total + term
        mixed_ref[h] = total[:HD] / total[HD : HD + 1]
    place = ring_place()
    core = lax.axis_index("seq") % 2
    lefts = []
    for side in range(2):
        heads = [2 * chip_at(place + offset) + jnp.where(core == side, 0, 1) for offset in RING]
        lefts.append(jnp.concatenate([mixed_ref[head] for head in heads], axis=0).T.astype(BF16))
    half = keep_ref.shape[0]
    for first in range(0, D, 256):
        columns = slice(first, min(first + 256, D))
        result = jnp.dot(lefts[0], weight_refs[0][:, columns], preferred_element_type=F32)
        result = result + jnp.dot(lefts[1], weight_refs[1][:, columns], preferred_element_type=F32)
        result = result.astype(BF16)
        keep_ref[:, columns] = result[:half]
        send_ref[:, columns] = result[half:]


def project_out(accs, weights):
    out = jax.ShapeDtypeStruct((64, D), BF16)
    return pl.pallas_call(
        functools.partial(out_kernel, len(accs)),
        out_shape=(out, out),
        in_specs=[VMEM] * (len(accs) + len(weights)),
        out_specs=(VMEM, VMEM),
        scratch_shapes=[pltpu.VMEM((HEADS, HD, 128), F32)],
        compiler_params=params(),
        name="project_out",
        cost_estimate=pl.CostEstimate(flops=2 * 128 * 1280 * D, bytes_accessed=4 << 20, transcendentals=0),
    )(*accs, *weights)


def pack_kernel(*refs):
    out_ref = refs[-1]
    for i in range(8):
        out_ref[i] = refs[i][...]


def pack(pieces):
    rows, columns = pieces[0].shape
    out = pl.pallas_call(
        pack_kernel,
        out_shape=jax.ShapeDtypeStruct((8, rows, columns), BF16),
        in_specs=[VMEM] * 8,
        out_specs=VMEM,
        compiler_params=params(),
        name="pack",
    )(*pieces)
    return out.reshape(8 * rows, columns)


def merge_kernel(lengths_ref, keep_ref, got_ref, out_ref):
    position = lax.axis_index("seq")
    keep = keep_ref[...].astype(F32)
    got = got_ref[...].astype(F32)
    start, _ = long_window(lengths_ref)
    q_cols = 16
    slot = lax.broadcasted_iota(jnp.int32, keep.shape, 0)
    token = (slot // q_cols) * (lax.axis_size("seq") * q_cols) + position * q_cols + slot % q_cols
    inside = jnp.where(token >= start, 1, 0)
    mine = inside == jnp.where(position % 2 == 0, 1, 0)
    half = keep.shape[0]
    out_ref[:half] = jnp.where(mine, keep, got).astype(BF16)
    out_ref[half:] = jnp.where(mine, got, keep).astype(BF16)


def merge(lengths, keep, got):
    return pl.pallas_call(
        merge_kernel,
        out_shape=jax.ShapeDtypeStruct((128, D), BF16),
        in_specs=[SMEM, VMEM, VMEM],
        out_specs=VMEM,
        compiler_params=params(),
        name="merge",
    )(lengths, keep, got)


def shards(
    clip, frame_counts, conv_first, conv_second, patch_weight, qkv_weight, query_gain, key_gain,
    out_weight, window_lengths,
):
    size = lax.axis_size("seq")
    facing = [(i, j) for i in range(1, size - 1, 2) for i, j in ((i, i + 1), (i + 1, i))]
    cores = [(i, i ^ 1) for i in range(size)]
    forward = ring_pairs()
    backward = [(j, i) for i, j in forward]

    def send(array, pairs):
        return lax.ppermute(array, "seq", pairs)

    def tied(*arrays):
        return lax.optimization_barrier(arrays)

    def tied(*arrays):
        return lax.optimization_barrier(arrays)

    def both_ways(ahead, behind):
        return send(ahead, forward), send(behind, backward)

    def tied(*arrays):
        return lax.optimization_barrier(arrays)

    def both_ways(ahead, behind):
        return send(ahead, forward), send(behind, backward)

    sibling_rows = send(clip, cores)
    other_rows = send(clip, facing)
    query_row, key_row = query_gain[None], key_gain[None]
    weight_one = both_ways(out_weight, out_weight)
    folded, query_weight, centered = fold(patch_weight, qkv_weight)
    sibling_rows, other_rows, *weight_one, folded = tied(sibling_rows, other_rows, *weight_one, folded)
    weight_two = both_ways(*weight_one)
    keep, other = convolve(
        frame_counts, window_lengths, clip, sibling_rows, other_rows, conv_first, conv_second, patch_weight
    )
    got = send(other, cores)
    got, wu_a, wu_b = tied(got, *weight_two)
    weight_two = (wu_a, wu_b)
    weight_three = both_ways(*weight_two)
    block = jnp.concatenate([keep, got], axis=0)
    one = both_ways(block, block)
    queries = make_queries(window_lengths, block, centered, query_weight, query_row)
    *one, queries = tied(*one, queries)
    two = both_ways(*one)
    acc_one = step_attention((-1, 1), window_lengths, one, folded, key_row, queries)
    wt_a, wt_b, acc_one = tied(*weight_three, acc_one)
    weight_four = send(wt_a, forward)
    *two, acc_one = tied(*two, acc_one)
    three = both_ways(*two)
    acc_two = step_attention((-2, 2), window_lengths, two, folded, key_row, queries)
    *three, acc_two, weight_four = tied(*three, acc_two, weight_four)
    four = both_ways(three[0][:64], three[1][64:])
    weights = pack([out_weight, *weight_one, *weight_two, wt_a, wt_b, weight_four])
    sibling = send(weights, cores)
    acc_three = step_attention((-3, 3), window_lengths, three, folded, key_row, queries)
    *four, acc_three = tied(*four, acc_three)
    acc_four = step_attention((0, 4, 4), window_lengths, [block, *four], folded, key_row, queries)
    keep_rows, send_rows = project_out((acc_one, acc_two, acc_three, acc_four), (weights, sibling))
    return merge(window_lengths, keep_rows, send(send_rows, cores))


def solution(mesh):
    own = mesh.shape["seq"] == HEADS
    return jax.shard_map(
        shards if own else general_shards,
        mesh=mesh,
        in_specs=(
            P("groups", "seq", None, None),
            P("groups"),
            P(),
            P(),
            P(),
            P(),
            P(),
            P(),
            P("seq", None),
            P("groups", None),
        ),
        out_specs=P(("groups", "seq"), None),
        check_vma=False,
    )
```
